32 devices in a mesh: tm: 4 (over z), height: 4 (over y, x), cam: 2 (over core).
Axes of the slice: x: 2, y: 2, z: 4, core: 2. Of those that a mesh axis runs over, the one named last changes fastest.
Arguments:
- video_clip: bfloat16 [2, 16, 16, 64, 256], P('cam', 'tm', 'height'), may hold values from -6 to 6
- valid_from: int32 [2], P('cam'), may hold values from 0 to 8, as said below
- norm_gain: float32 [256], replicated, may hold values from 0.5 to 1.5
- spatial_weight: bfloat16 [3, 3, 256, 256], replicated, may hold values from -0.125 to 0.125
- temporal_weight: bfloat16 [3, 256, 256], replicated, may hold values from -0.21875 to 0.21875
- mix_weight: bfloat16 [3, 256, 256], replicated, may hold values from -0.21875 to 0.21875
- cotangent: bfloat16 [2, 8, 16, 64, 256], P('cam', None, ('height', 'tm')), may hold values from -6 to 6
Outputs:
- encoded: bfloat16 [2, 8, 16, 64, 256], P('cam', None, ('height', 'tm'))
- video_gradient: bfloat16 [2, 16, 16, 64, 256], P('cam', 'tm', 'height')
- spatial_gradient: float32 [3, 3, 256, 256], replicated
- temporal_gradient: float32 [3, 256, 256], replicated
- mix_gradient: float32 [3, 256, 256], replicated
- gain_gradient: float32 [256], replicated
The draws below stay inside these ranges and needn't reach their ends.
Inputs may be any that keep to these rules, and one draw needn't show every extreme that they name: Frames before valid_from of a camera are padding. In every draw some camera starts at 8.
All inputs are finite; a program needn't handle non-finite values.
Results may differ from the reference program's by a relative error of at most 0.0065.
Values may be sent and summed in bfloat16 or wider, within the bound.
No kernel may reach another device: no remote copies, remote signals or barrier semaphores. Data moves between devices by JAX's collectives and lax.ppermute only.
A program may use at most 128 MiB of HBM per device.

```python
import math
import jax
import jax.numpy as jnp
from jax import lax

C = 256
W = 64
CAMS = 2
T_IN = 16
T_OUT = 8
H = 16


def draw_valid_from(key, part):
    starts = jax.random.randint(jax.random.fold_in(key, 11), (CAMS,), 0, T_IN // 2)
    latest = jax.random.randint(jax.random.fold_in(key, 12), (), 0, CAMS)
    starts = starts.at[latest].set(T_IN // 2)
    return starts.astype(jnp.int32)


def block_scale(key, extent, cuts, least, top_value):
    gain = 1.0
    for axis_at, shards_of in cuts:
        heights = jax.random.uniform(jax.random.fold_in(jax.random.fold_in(key, 6), axis_at), (shards_of,), jnp.float32, least / len(cuts), top_value / len(cuts))
        gain = gain * jnp.repeat(jnp.exp(heights), extent[axis_at] // shards_of).reshape((-1,) + (1,) * (len(extent) - 1 - axis_at))
    return gain


def scatter_about(rng, shape, width, limit, pieces=(), held_as=jnp.bfloat16):
    entries = width * jax.random.normal(rng, shape, jnp.float32)
    if pieces:
        entries = entries * block_scale(rng, shape, pieces, -0.22, 0.18)
    return jnp.clip(entries, -limit, limit).astype(held_as)


def setup_inputs(seed: int = 0) -> dict:
    key_of = jax.random.split(jax.random.key(seed), 8)
    video_clip = scatter_about(key_of[0], (CAMS, T_IN, H, W, C), 1.0, 6.0, ((0, 2), (1, 4), (2, 4)))
    valid_from = draw_valid_from(jax.random.fold_in(key_of[7], 71), 0)
    norm_gain = jnp.clip(1.0 + 0.1 * jax.random.normal(key_of[2], (C,), jnp.float32), 0.5, 1.5)
    spatial_weight = scatter_about(key_of[3], (3, 3, C, C), (9 * C) ** -0.5, 0.125)
    temporal_weight = scatter_about(key_of[4], (3, C, C), (3 * C) ** -0.5, 0.21875)
    mix_weight = scatter_about(key_of[5], (3, C, C), (3 * C) ** -0.5, 0.21875)
    cotangent = scatter_about(key_of[6], (CAMS, T_OUT, H, W, C), 1.0, 6.0, ((0, 2), (2, 16)))
    return dict(video_clip=video_clip, valid_from=valid_from, norm_gain=norm_gain, spatial_weight=spatial_weight, temporal_weight=temporal_weight, mix_weight=mix_weight, cotangent=cotangent)


def project(rows_in, weight):
    flat_rows = rows_in.reshape(-1, rows_in.shape[-1])
    product = jnp.dot(flat_rows, weight, preferred_element_type=jnp.float32)
    return product.reshape(rows_in.shape[:-1] + (weight.shape[-1],))

def project_back(rows_in, weight):
    flat_rows = rows_in.reshape(-1, rows_in.shape[-1])
    product = lax.dot_general(flat_rows, weight, (((1,), (1,)), ((), ())), preferred_element_type=jnp.float32)
    return product.reshape(rows_in.shape[:-1] + (weight.shape[0],))

def outer_sum(left_rows, right_rows):
    return lax.dot_general(left_rows.reshape(-1, left_rows.shape[-1]), right_rows.reshape(-1, right_rows.shape[-1]), (((0,), (0,)), ((), ())), preferred_element_type=jnp.float32)

def column_pad(padded):
    return jnp.pad(padded, ((0, 0), (0, 0), (0, 0), (1, 1), (0, 0)))

def spatial(padded, weight):
    columns = column_pad(padded)
    rows_here = padded.shape[2] - 2
    width_here = padded.shape[3]
    accumulated = jnp.zeros(padded.shape[:2] + (rows_here, width_here, weight.shape[-1]), jnp.float32)
    for row_tap in range(3):
        for column_tap in range(3):
            window = columns[:, :, row_tap:row_tap + rows_here, column_tap:column_tap + width_here]
            accumulated = accumulated + project(window, weight[row_tap, column_tap])
    return accumulated

def spatial_grad(padded, gradient):
    columns = column_pad(padded)
    rows_here = padded.shape[2] - 2
    width_here = padded.shape[3]
    outer_rows = []
    for row_tap in range(3):
        inner_rows = []
        for column_tap in range(3):
            window = columns[:, :, row_tap:row_tap + rows_here, column_tap:column_tap + width_here]
            inner_rows.append(outer_sum(window, gradient))
        outer_rows.append(jnp.stack(inner_rows))
    return jnp.stack(outer_rows)

def flipped(weight):
    return jnp.transpose(weight[::-1, ::-1], (0, 1, 3, 2))

def norm_forward(masked, norm_gain):
    values = masked.astype(jnp.float32)
    inverse = lax.rsqrt(lax.optimization_barrier(jnp.mean(values * values, axis=-1, keepdims=True)) + 1e-06)
    unit_rows = values * inverse
    return ((unit_rows * norm_gain).astype(jnp.bfloat16), unit_rows, inverse)

def norm_backward(normed_gradient, unit_rows, inverse, norm_gain, present):
    unit_gradient = normed_gradient * norm_gain
    masked_gradient = inverse * (unit_gradient - unit_rows * lax.optimization_barrier(jnp.mean(unit_gradient * unit_rows, axis=-1, keepdims=True)))
    video_gradient = jnp.where(present, masked_gradient, jnp.zeros_like(masked_gradient)).astype(jnp.bfloat16)
    gain_gradient = lax.optimization_barrier(jnp.sum((normed_gradient * unit_rows).reshape(-1, unit_rows.shape[-1]), axis=0))
    return (video_gradient, gain_gradient)

def split_frames(active, prior_frame):
    dims_in = active.shape
    frame_pairs = active.reshape(dims_in[0], dims_in[1] // 2, 2, dims_in[2], dims_in[3], dims_in[4])
    even_frames = frame_pairs[:, :, 0]
    odd_frames = frame_pairs[:, :, 1]
    prior_odd = jnp.concatenate([prior_frame, odd_frames[:, :-1]], axis=1)
    return (even_frames, odd_frames, prior_odd)

def temporal_forward(even_frames, odd_frames, prior_odd, weight):
    accumulated = project(odd_frames, weight[0]) + project(even_frames, weight[1]) + project(prior_odd, weight[2])
    return accumulated.astype(jnp.bfloat16)

def temporal_backward(even_frames, odd_frames, prior_odd, strided_gradient, following, weight):
    weight_gradient = jnp.stack([outer_sum(odd_frames, strided_gradient), outer_sum(even_frames, strided_gradient), outer_sum(prior_odd, strided_gradient)])
    next_gradient = jnp.concatenate([strided_gradient[:, 1:], following], axis=1)
    odd_gradient = project_back(strided_gradient, weight[0]) + project_back(next_gradient, weight[2])
    even_gradient = project_back(strided_gradient, weight[1])
    dims_in = even_frames.shape
    active_gradient = jnp.stack([even_gradient, odd_gradient], axis=2).reshape(dims_in[0], dims_in[1] * 2, dims_in[2], dims_in[3], dims_in[4])
    return (active_gradient, weight_gradient)

def mix_forward(regrouped, weight):
    frame_count = regrouped.shape[1]
    blank_frames = jnp.zeros(regrouped.shape[:1] + (2,) + regrouped.shape[2:], regrouped.dtype)
    history = jnp.concatenate([blank_frames, regrouped], axis=1)
    accumulated = regrouped.astype(jnp.float32)
    for offset in range(3):
        accumulated = accumulated + project(history[:, 2 - offset:2 - offset + frame_count], weight[offset])
    return (accumulated.astype(jnp.bfloat16), history)

def mix_backward(history, cotangent, weight):
    frame_count = cotangent.shape[1]
    mix_gradient = jnp.stack([outer_sum(history[:, 2 - offset:2 - offset + frame_count], cotangent) for offset in range(3)])
    blank_frames = jnp.zeros(cotangent.shape[:1] + (2,) + cotangent.shape[2:], cotangent.dtype)
    ahead = jnp.concatenate([cotangent, blank_frames], axis=1)
    accumulated = cotangent.astype(jnp.float32)
    for offset in range(3):
        accumulated = accumulated + project_back(ahead[:, offset:offset + frame_count], weight[offset])
    return (mix_gradient, accumulated.astype(jnp.bfloat16))

def activation_backward(active_gradient, pre_activation):
    sigmoid_value = jax.nn.sigmoid(pre_activation)
    return (active_gradient * sigmoid_value * (1.0 + pre_activation * (1.0 - sigmoid_value))).astype(jnp.bfloat16)

def reference(video_clip, valid_from, norm_gain, spatial_weight, temporal_weight, mix_weight, cotangent):
    frames = jnp.arange(T_IN, dtype=jnp.int32)
    present = (frames[None, :] >= valid_from[:, None])[:, :, None, None, None]
    masked = jnp.where(present, video_clip, jnp.zeros_like(video_clip))
    normed, unit_rows, inverse = norm_forward(masked, norm_gain)
    padded = jnp.pad(normed, ((0, 0), (0, 0), (1, 1), (0, 0), (0, 0)))
    pre_activation = spatial(padded, spatial_weight)
    active = jax.nn.silu(pre_activation).astype(jnp.bfloat16)
    prior_frame = jnp.zeros_like(active[:, :1])
    even_frames, odd_frames, prior_odd = split_frames(active, prior_frame)
    strided = temporal_forward(even_frames, odd_frames, prior_odd, temporal_weight)
    encoded, history = mix_forward(strided, mix_weight)
    mix_gradient, strided_gradient = mix_backward(history, cotangent, mix_weight)
    following = jnp.zeros_like(strided_gradient[:, :1])
    active_gradient, temporal_gradient = temporal_backward(even_frames, odd_frames, prior_odd, strided_gradient, following, temporal_weight)
    pre_gradient = activation_backward(active_gradient, pre_activation)
    spatial_gradient = spatial_grad(padded, pre_gradient)
    gradient_padded = jnp.pad(pre_gradient, ((0, 0), (0, 0), (1, 1), (0, 0), (0, 0)))
    normed_gradient = spatial(gradient_padded, flipped(spatial_weight))
    video_gradient, gain_gradient = norm_backward(normed_gradient, unit_rows, inverse, norm_gain, present)
    gradient_scale = 1.0 / math.sqrt(CAMS * T_IN * H * W)
    return (encoded, video_gradient, spatial_gradient * gradient_scale, temporal_gradient * gradient_scale, mix_gradient * gradient_scale, gain_gradient * gradient_scale)
```

```python
import functools
import math

import jax
import jax.numpy as jnp
from jax import lax
from jax.experimental import pallas as pl
from jax.experimental.pallas import tpu as pltpu
from jax.sharding import PartitionSpec as P

F32 = jnp.float32
BF16 = jnp.bfloat16
VMEM_LIMIT = 40 * 1024 * 1024


def dot(left, right):
    return jnp.dot(left, right, preferred_element_type=F32)


def dot_nt(left, right):
    return lax.dot_general(left, right, (((1,), (1,)), ((), ())), preferred_element_type=F32)


def dot_tn(left, right):
    return lax.dot_general(left, right, (((0,), (0,)), ((), ())), preferred_element_type=F32)


def from_left(cells, width):
    column = lax.broadcasted_iota(jnp.int32, cells.shape, 0) % width
    return jnp.where(column == 0, 0.0, pltpu.roll(cells, 1, 0))


def from_right(cells, width):
    column = lax.broadcasted_iota(jnp.int32, cells.shape, 0) % width
    return jnp.where(column == width - 1, 0.0, pltpu.roll(cells, cells.shape[0] - 1, 0))


def present(info, frame):
    return (info[1] + frame >= info[0]).astype(F32)


def normalised(tile, keep):
    values = tile.astype(F32) * keep
    inverse = lax.rsqrt(jnp.mean(values * values, axis=-1, keepdims=True) + 1e-06)
    return (values * inverse, inverse)


def forward_kernel(
    info, video, above, below, gain, weight, wide, slope, even, odd, *, frames, rows, width
):
    block = frames * width
    for row in range(-1, rows + 1):
        for frame in range(frames):
            if row < 0:
                tile = above[frame, 0]
            elif row == rows:
                tile = below[frame, 0]
            else:
                tile = video[frame, row]
            unit, _ = normalised(tile, present(info, frame))
            normed = (unit * gain[...]).astype(BF16)
            for tap in range(3):
                target = row + 1 - tap
                if 0 <= target < rows:
                    at = target * block + frame * width
                    wide[at : at + width, tap * 256 : tap * 256 + 256] = normed
    for row in range(rows):
        cells = wide[row * block : row * block + block]
        taps = [
            dot(cells, jnp.concatenate([weight[0, j], weight[1, j], weight[2, j]], axis=0))
            for j in range(3)
        ]
        pre = from_left(taps[0], width) + taps[1] + from_right(taps[2], width)
        sigmoid = 1.0 / (1.0 + jnp.exp(-pre))
        active = (pre * sigmoid).astype(BF16)
        slope[row * block : row * block + block] = sigmoid * (1.0 + pre * (1.0 - sigmoid))
        for frame in range(frames):
            target = odd if frame % 2 else even
            at = (frame // 2) * rows * width + row * width
            target[at : at + width] = active[frame * width : frame * width + width]


def middle_kernel(
    info, cot_in, slope, even, odd, temporal, mix, pre_gradient, strided, keep, send, cot, sums,
    *, frames, rows, width
):
    outs = frames // 2
    plane = rows * width
    shards = cot_in.shape[0]
    here = rows // shards
    for frame in range(outs + 3):
        for row in range(rows):
            at = frame * plane + row * width
            cot[at : at + width] = cot_in[row // here, frame, row % here]
    span = (outs + 1) * plane
    gradient = cot[0:span].astype(F32)
    for k in range(3):
        gradient = gradient + dot_nt(cot[k * plane : k * plane + span], mix[k])
    gradient = gradient.astype(BF16)
    now = gradient[: outs * plane]
    later = gradient[plane:]
    even_gradient = dot_nt(now, temporal[1])
    odd_gradient = dot_nt(now, temporal[0]) + dot_nt(later, temporal[2])
    for row in range(rows):
        for frame in range(frames):
            source = odd_gradient if frame % 2 else even_gradient
            at = (frame // 2) * plane + row * width
            to = (row * frames + frame) * width
            pre_gradient[row, frame] = (
                source[at : at + width] * slope[to : to + width]
            ).astype(BF16)
    evens = even[...]
    odds = odd[...]
    carried = dot(odds, temporal[2])
    mixed = dot(odds, temporal[0]) + dot(evens, temporal[1])
    parts = [mixed[:plane]]
    for s in range(1, outs):
        parts.append(
            mixed[s * plane : s * plane + plane] + carried[(s - 1) * plane : s * plane]
        )
    parts.append(carried[(outs - 1) * plane :])
    parts = jnp.concatenate(parts, axis=0).astype(BF16)
    for frame in range(outs + 1):
        for row in range(rows):
            at = frame * plane + row * width
            strided[row // here, frame, row % here] = parts[at : at + width]
    for k in range(3):
        sums[k] = dot_tn(parts, cot[k * plane : k * plane + span])
    sums[3] = dot_tn(odds, now)
    sums[4] = dot_tn(evens, now)
    sums[5] = dot_tn(odds, later)
    halves(info, sums, keep, send)


def halves(info, sums, keep, send):
    half = sums.shape[1] // 2
    mine = pl.multiple_of(info[2] * half, half)
    other = pl.multiple_of((1 - info[2]) * half, half)
    keep[...] = sums[:, pl.ds(mine, half)]
    send[...] = sums[:, pl.ds(other, half)].astype(BF16)


def weight_kernel(info, wide, pre_gradient, keep, send, sums, *, width):
    gradient = pre_gradient[...].reshape(-1, 256)
    exact = gradient.astype(F32)
    columns = [
        from_right(exact, width).astype(BF16), gradient, from_left(exact, width).astype(BF16)
    ]
    for i in range(3):
        normed = wide[:, i * 256 : i * 256 + 256]
        product = dot_tn(normed, jnp.concatenate(columns, axis=1))
        for j in range(3):
            sums[i * 3 + j] = product[:, j * 256 : j * 256 + 256]
    halves(info, sums, keep, send)


def input_kernel(
    info, video, pre_gradient, above, below, gain, weight, out, tall, *, frames, rows, width
):
    block = frames * width
    for row in range(-1, rows + 1):
        if row < 0:
            cells = above[...]
        elif row == rows:
            cells = below[...]
        else:
            cells = pre_gradient[row]
        cells = cells.reshape(block, 256)
        for tap in range(3):
            target = row - 1 + tap
            if 0 <= target < rows:
                tall[target * block : target * block + block, tap * 256 : tap * 256 + 256] = cells
    for row in range(rows):
        cells = tall[row * block : row * block + block]
        taps = [
            dot_nt(cells, jnp.concatenate([weight[0, j], weight[1, j], weight[2, j]], axis=1))
            for j in range(3)
        ]
        gradient = from_right(taps[0], width) + taps[1] + from_left(taps[2], width)
        gradient = gradient * gain[...]
        for frame in range(frames):
            keep = present(info, frame)
            unit, inverse = normalised(video[frame, row], keep)
            tile = gradient[frame * width : frame * width + width]
            mean = jnp.mean(tile * unit, axis=-1, keepdims=True)
            out[frame, row] = (inverse * (tile - unit * mean) * keep).astype(BF16)


def encode_kernel(strided, mix, out, line, *, width):
    shards, parts, here = strided.shape[:3]
    outs = parts - 1
    plane = here * width
    total = shards * outs
    for frame in range(total):
        shard, part = (frame // outs, frame % outs)
        cells = strided[shard, part].reshape(plane, 256)
        if part == 0 and shard > 0:
            carried = strided[shard - 1, outs].reshape(plane, 256)
            cells = (cells.astype(F32) + carried.astype(F32)).astype(BF16)
        line[(frame + 2) * plane : (frame + 3) * plane] = cells
    line[0 : 2 * plane] = jnp.zeros((2 * plane, 256), BF16)
    span = total * plane
    result = line[2 * plane : 2 * plane + span].astype(F32)
    for k in range(3):
        result = result + dot(line[(2 - k) * plane : (2 - k) * plane + span], mix[k])
    out[...] = result.astype(BF16).reshape(out.shape)


def finish_kernel(
    info, first, first_other, second, second_other, gain, weight, spatial, temporal, mix, gain_out,
    *, scale
):
    half = 128
    mine = pl.multiple_of(info[2] * half, half)
    other = pl.multiple_of((1 - info[2]) * half, half)
    for at, low, high in ((mine, first, second), (other, first_other, second_other)):
        for k in range(3):
            mix[k, pl.ds(at, half)] = low[k].astype(F32) * scale
            temporal[k, pl.ds(at, half)] = low[3 + k].astype(F32) * scale
        total = jnp.zeros((half, 256), F32)
        for i in range(3):
            for j in range(3):
                piece = high[3 * i + j].astype(F32) * scale
                spatial[i, j, pl.ds(at, half)] = piece
                total = total + piece * weight[i, j, pl.ds(at, half)].astype(F32)
        gain_out[pl.ds(at, half)] = (
            jnp.sum(total, axis=1, keepdims=True) / gain[pl.ds(at, half)]
        )


def call(kernel, outs, scratch=(), flops=0, moved=0):
    smem = pl.BlockSpec(memory_space=pltpu.SMEM)
    vmem = pl.BlockSpec(memory_space=pltpu.VMEM)

    def run(*operands):
        return pl.pallas_call(
            kernel,
            out_shape=[jax.ShapeDtypeStruct(shape, dtype) for shape, dtype in outs],
            in_specs=[smem if a.dtype == jnp.int32 else vmem for a in operands],
            out_specs=[vmem] * len(outs),
            scratch_shapes=[pltpu.VMEM(shape, dtype) for shape, dtype in scratch],
            compiler_params=pltpu.CompilerParams(vmem_limit_bytes=VMEM_LIMIT),
            cost_estimate=pl.CostEstimate(flops=flops, bytes_accessed=moved, transcendentals=0),
        )(*operands)

    return run


def neighbours(last, initial, axis):
    size = lax.axis_size(axis)
    up = [(i, i + 1) for i in range(size - 1)]
    down = [(j, i) for i, j in up]
    return (lax.ppermute(last, axis, up), lax.ppermute(initial, axis, down))


def exchange(array, axis):
    return lax.all_to_all(array, axis, split_axis=0, concat_axis=0, tiled=True)


def swap(array):
    return lax.ppermute(array, "cam", [(0, 1), (1, 0)])


def spread(array, axis):
    size = lax.axis_size(axis)
    return exchange(jnp.broadcast_to(array[None], (size,) + array.shape), axis)


def summed(keep, send):
    total = (keep + swap(send).astype(F32)).astype(BF16).reshape(-1, keep.shape[-1])
    for axis in ("height", "tm"):
        pieces = exchange(total.reshape(lax.axis_size(axis), -1, total.shape[-1]), axis)
        total = jnp.sum(pieces.astype(F32), axis=0).astype(BF16)
    for axis in ("tm", "height"):
        total = spread(total, axis).reshape(-1, total.shape[-1])
    total = total.reshape(keep.shape)
    return (total, swap(total))


def on_device(
    video_clip, valid_from, norm_gain, spatial_weight, temporal_weight, mix_weight, cotangent
):
    video = video_clip[0]
    frames, rows, width, channels = video.shape
    outs = frames // 2
    shards = lax.axis_size("tm")
    here = rows // shards
    cells = frames * rows * width
    sizes = dict(frames=frames, rows=rows, width=width)
    info = jnp.stack(
        [valid_from[0], lax.axis_index("tm") * frames, lax.axis_index("cam")]
    ).astype(jnp.int32)
    gain = norm_gain.reshape(1, channels)

    padded = jnp.pad(cotangent[0], ((0, 3), (0, 0), (0, 0), (0, 0)))
    cot_out = jnp.stack([padded[outs * i : outs * i + outs + 3] for i in range(shards)])
    cot_in = exchange(cot_out, "tm")
    above, below = neighbours(video[:, rows - 1 :], video[:, :1], "height")

    wide, slope, even, odd = call(
        functools.partial(forward_kernel, **sizes),
        [
            ((cells, 3 * channels), BF16),
            ((cells, channels), F32),
            ((cells // 2, channels), BF16),
            ((cells // 2, channels), BF16),
        ],
        flops=18 * cells * channels * channels,
        moved=6 * 1024 * 1024,
    )(info, video, above, below, gain, spatial_weight)

    pre_gradient, strided, keep_low, send_low = call(
        functools.partial(middle_kernel, **sizes),
        [
            ((rows, frames, width, channels), BF16),
            ((shards, outs + 1, here, width, channels), BF16),
            ((6, channels // 2, channels), F32),
            ((6, channels // 2, channels), BF16),
        ],
        [
            (((outs + 3) * rows * width, channels), BF16),
            ((6, channels, channels), F32),
        ],
        flops=18 * cells * channels * channels,
        moved=6 * 1024 * 1024,
    )(info, cot_in, slope, even, odd, temporal_weight, mix_weight)

    keep_high, send_high = call(
        functools.partial(weight_kernel, width=width),
        [((9, channels // 2, channels), F32), ((9, channels // 2, channels), BF16)],
        [((9, channels, channels), F32)],
        flops=18 * cells * channels * channels,
        moved=6 * 1024 * 1024,
    )(info, wide, pre_gradient)

    low = summed(keep_low, send_low)
    high = summed(keep_high, send_high)

    regrouped = exchange(strided, "tm")
    (encoded,) = call(
        functools.partial(encode_kernel, width=width),
        [((shards * outs, here, width, channels), BF16)],
        [(((shards * outs + 2) * here * width, channels), BF16)],
        flops=3 * cells * channels * channels,
        moved=2 * 1024 * 1024,
    )(regrouped, mix_weight)

    above, below = neighbours(pre_gradient[rows - 1], pre_gradient[0], "height")
    (video_gradient,) = call(
        functools.partial(input_kernel, **sizes),
        [((frames, rows, width, channels), BF16)],
        [((cells, 3 * channels), BF16)],
        flops=18 * cells * channels * channels,
        moved=4 * 1024 * 1024,
    )(info, video, pre_gradient, above, below, gain, spatial_weight)

    cell_count = cells * lax.axis_size("cam") * shards * lax.axis_size("height")
    spatial, temporal, mix, gain_gradient = call(
        functools.partial(finish_kernel, scale=1.0 / math.sqrt(cell_count)),
        [
            (spatial_weight.shape, F32),
            (temporal_weight.shape, F32),
            (mix_weight.shape, F32),
            ((channels, 1), F32),
        ],
        moved=8 * 1024 * 1024,
    )(info, *low, *high, norm_gain.reshape(channels, 1), spatial_weight)

    return (
        encoded[None],
        video_gradient[None],
        spatial,
        temporal,
        mix,
        gain_gradient.reshape(channels),
    )


def solution(mesh):
    return jax.shard_map(
        on_device,
        mesh=mesh,
        in_specs=(
            P("cam", "tm", "height", None, None),
            P("cam"),
            P(),
            P(),
            P(),
            P(),
            P("cam", None, ("height", "tm"), None, None),
        ),
        out_specs=(
            P("cam", None, ("height", "tm"), None, None),
            P("cam", "tm", "height", None, None),
            P(),
            P(),
            P(),
            P(),
        ),
        check_vma=False,
    )
```

```python
import functools
import math

import jax
import jax.numpy as jnp
from jax import lax
from jax.experimental import pallas as pl
from jax.experimental.pallas import tpu as pltpu
from jax.sharding import PartitionSpec as P

F32 = jnp.float32
BF16 = jnp.bfloat16
VMEM_LIMIT = 16 * 1024 * 1024


def dot(left, right):
    return jnp.dot(left, right, preferred_element_type=F32)


def dot_nt(left, right):
    return lax.dot_general(left, right, (((1,), (1,)), ((), ())), preferred_element_type=F32)


def dot_tn(left, right):
    return lax.dot_general(left, right, (((0,), (0,)), ((), ())), preferred_element_type=F32)


def from_left(cells, width):
    column = lax.broadcasted_iota(jnp.int32, cells.shape, 0) % width
    return jnp.where(column == 0, 0.0, pltpu.roll(cells, 1, 0))


def from_right(cells, width):
    column = lax.broadcasted_iota(jnp.int32, cells.shape, 0) % width
    return jnp.where(column == width - 1, 0.0, pltpu.roll(cells, cells.shape[0] - 1, 0))


def present(info, frame):
    return (info[1] + frame >= info[0]).astype(F32)


def normalised(tile, keep):
    values = tile.astype(F32) * keep
    inverse = lax.rsqrt(jnp.mean(values * values, axis=-1, keepdims=True) + 1e-06)
    return (values * inverse, inverse)


def prepare_kernel(cotangent, video, cot_out, last, first, *, outs, rows):
    shards, span = cot_out.shape[:2]
    total = cotangent.shape[0]
    for shard in range(shards):
        for part in range(span):
            frame = outs * shard + part
            if frame < total:
                cot_out[shard, part] = cotangent[frame]
            else:
                cot_out[shard, part] = jnp.zeros(cot_out.shape[2:], BF16)
    for frame in range(video.shape[0]):
        last[frame, 0] = video[frame, rows - 1]
        first[frame, 0] = video[frame, 0]


def forward_kernel(
    info, video, above, below, gain, weight, wide, slope, even, odd, *, frames, rows, width
):
    block = frames * width
    for row in range(-1, rows + 1):
        for frame in range(frames):
            if row < 0:
                tile = above[frame, 0]
            elif row == rows:
                tile = below[frame, 0]
            else:
                tile = video[frame, row]
            unit, _ = normalised(tile, present(info, frame))
            normed = (unit * gain[...]).astype(BF16)
            for tap in range(3):
                target = row + 1 - tap
                if 0 <= target < rows:
                    at = target * block + frame * width
                    wide[at : at + width, tap * 256 : tap * 256 + 256] = normed
    for row in range(rows):
        cells = wide[row * block : row * block + block]
        taps = [
            dot(cells, jnp.concatenate([weight[0, j], weight[1, j], weight[2, j]], axis=0))
            for j in range(3)
        ]
        pre = from_left(taps[0], width) + taps[1] + from_right(taps[2], width)
        sigmoid = 1.0 / (1.0 + jnp.exp(-pre))
        active = (pre * sigmoid).astype(BF16)
        slope[row * block : row * block + block] = sigmoid * (1.0 + pre * (1.0 - sigmoid))
        for frame in range(frames):
            target = odd if frame % 2 else even
            at = (frame // 2) * rows * width + row * width
            target[at : at + width] = active[frame * width : frame * width + width]


def middle_kernel(
    info, cot_in, slope, even, odd, wide, temporal, mix,
    pre_gradient, top, bottom, strided, keep, send, cot, sums,
    *, frames, rows, width
):
    outs = frames // 2
    plane = rows * width
    shards = cot_in.shape[0]
    here = rows // shards
    for frame in range(outs + 3):
        for row in range(rows):
            at = frame * plane + row * width
            cot[at : at + width] = cot_in[row // here, frame, row % here]
    span = (outs + 1) * plane
    gradient = cot[0:span].astype(F32)
    for k in range(3):
        gradient = gradient + dot_nt(cot[k * plane : k * plane + span], mix[k])
    gradient = gradient.astype(BF16)
    now = gradient[: outs * plane]
    later = gradient[plane:]
    even_gradient = dot_nt(now, temporal[1])
    odd_gradient = dot_nt(now, temporal[0]) + dot_nt(later, temporal[2])
    for row in range(rows):
        for frame in range(frames):
            source = odd_gradient if frame % 2 else even_gradient
            at = (frame // 2) * plane + row * width
            to = (row * frames + frame) * width
            tile = (source[at : at + width] * slope[to : to + width]).astype(BF16)
            pre_gradient[row, frame] = tile
            if row == 0:
                top[frame] = tile
            if row == rows - 1:
                bottom[frame] = tile
    evens = even[...]
    odds = odd[...]
    carried = dot(odds, temporal[2])
    mixed = dot(odds, temporal[0]) + dot(evens, temporal[1])
    parts = [mixed[:plane]]
    for s in range(1, outs):
        parts.append(
            mixed[s * plane : s * plane + plane] + carried[(s - 1) * plane : s * plane]
        )
    parts.append(carried[(outs - 1) * plane :])
    parts = jnp.concatenate(parts, axis=0).astype(BF16)
    for frame in range(outs + 1):
        for row in range(rows):
            at = frame * plane + row * width
            strided[row // here, frame, row % here] = parts[at : at + width]
    for k in range(3):
        sums[k] = dot_tn(parts, cot[k * plane : k * plane + span])
    sums[3] = dot_tn(odds, now)
    sums[4] = dot_tn(evens, now)
    sums[5] = dot_tn(odds, later)
    gradient = pre_gradient[...].reshape(-1, 256)
    exact = gradient.astype(F32)
    columns = [
        from_right(exact, width).astype(BF16), gradient, from_left(exact, width).astype(BF16)
    ]
    for i in range(3):
        normed = wide[:, i * 256 : i * 256 + 256]
        product = dot_tn(normed, jnp.concatenate(columns, axis=1))
        for j in range(3):
            sums[6 + i * 3 + j] = product[:, j * 256 : j * 256 + 256]
    mine, other = core_columns(info)
    keep[...] = sums[:, :, mine]
    send[...] = sums[:, :, other].astype(BF16)


def core_columns(info):
    mine = pl.ds(pl.multiple_of(info[2] * 128, 128), 128)
    other = pl.ds(pl.multiple_of((1 - info[2]) * 128, 128), 128)
    return (mine, other)


def deal(info, place, total, kept, sends):
    kept[...] = total(info[place])
    for step, send in enumerate(sends):
        send[...] = total(info[place] ^ (step + 1)).astype(BF16)


def first_sum_kernel(info, keep, got, kept, *sends):
    deal(info, 3, lambda at: keep[at] + got[at].astype(F32), kept, sends)


def second_sum_kernel(info, kept_in, *refs):
    count = kept_in.shape[0]
    received = refs[: len(refs) - count]
    kept, *sends = refs[len(refs) - count :]

    def total(at):
        value = kept_in[at]
        for piece in received:
            value = value + piece[at].astype(F32)
        return value

    deal(info, 4, total, kept, sends)


def last_sum_kernel(kept, *refs):
    value = kept[...]
    for piece in refs[:-1]:
        value = value + piece[...].astype(F32)
    refs[-1][...] = value.astype(BF16)


def assemble_kernel(info, *refs):
    for step, piece in enumerate(refs[:-1]):
        refs[-1][info[4] ^ step] = piece[...]


def input_kernel(
    info, video, pre_gradient, above, below, gain, weight, out, tall, *, frames, rows, width
):
    block = frames * width
    for row in range(-1, rows + 1):
        if row < 0:
            cells = above[...]
        elif row == rows:
            cells = below[...]
        else:
            cells = pre_gradient[row]
        cells = cells.reshape(block, 256)
        for tap in range(3):
            target = row - 1 + tap
            if 0 <= target < rows:
                tall[target * block : target * block + block, tap * 256 : tap * 256 + 256] = cells
    for row in range(rows):
        cells = tall[row * block : row * block + block]
        taps = [
            dot_nt(cells, jnp.concatenate([weight[0, j], weight[1, j], weight[2, j]], axis=1))
            for j in range(3)
        ]
        gradient = from_right(taps[0], width) + taps[1] + from_left(taps[2], width)
        gradient = gradient * gain[...]
        for frame in range(frames):
            keep = present(info, frame)
            unit, inverse = normalised(video[frame, row], keep)
            tile = gradient[frame * width : frame * width + width]
            mean = jnp.mean(tile * unit, axis=-1, keepdims=True)
            out[frame, row] = (inverse * (tile - unit * mean) * keep).astype(BF16)


def encode_kernel(strided, mix, out, line, *, width):
    shards, parts, here = strided.shape[:3]
    outs = parts - 1
    plane = here * width
    total = shards * outs
    for frame in range(total):
        shard, part = (frame // outs, frame % outs)
        cells = strided[shard, part].reshape(plane, 256)
        if part == 0 and shard > 0:
            carried = strided[shard - 1, outs].reshape(plane, 256)
            cells = (cells.astype(F32) + carried.astype(F32)).astype(BF16)
        line[(frame + 2) * plane : (frame + 3) * plane] = cells
    line[0 : 2 * plane] = jnp.zeros((2 * plane, 256), BF16)
    span = total * plane
    result = line[2 * plane : 2 * plane + span].astype(F32)
    for k in range(3):
        result = result + dot(line[(2 - k) * plane : (2 - k) * plane + span], mix[k])
    out[...] = result.astype(BF16).reshape(out.shape)


def finish_kernel(info, *refs, scale, parts):
    pieces = refs[: 2 * parts]
    gain, weight, spatial, temporal, mix, gain_out, whole, total = refs[2 * parts :]
    step = pl.program_id(0)
    size = whole.shape[1] // parts

    @pl.when(step == 0)
    def _():
        for core in range(2):
            for part in range(parts):
                at = pl.multiple_of((info[3] ^ part) * size, size)
                whole[core, pl.ds(at, size)] = pieces[core * parts + part][...]
        total[...] = jnp.zeros_like(total)

    for core, columns in enumerate(core_columns(info)):

        def matrix(index):
            at = pl.multiple_of(index * 256, 256)
            return whole[core, pl.ds(at, 256)].astype(F32) * scale

        mix[0, :, columns] = matrix(step)
        temporal[0, :, columns] = matrix(step + 3)
        for j in range(3):
            piece = matrix(step * 3 + (6 + j))
            spatial[0, j, :, columns] = piece
            total[...] += piece * weight[step, j, :, columns].astype(F32)

    @pl.when(step == 2)
    def _():
        gain_out[...] = jnp.sum(total[...].T, axis=0, keepdims=True) / gain[...]


def call(kernel, outs, scratch=(), flops=0, moved=0):
    smem = pl.BlockSpec(memory_space=pltpu.SMEM)
    vmem = pl.BlockSpec(memory_space=pltpu.VMEM)

    def run(*operands):
        return pl.pallas_call(
            kernel,
            out_shape=[jax.ShapeDtypeStruct(shape, dtype) for shape, dtype in outs],
            in_specs=[smem if a.dtype == jnp.int32 else vmem for a in operands],
            out_specs=[vmem] * len(outs),
            scratch_shapes=[pltpu.VMEM(shape, dtype) for shape, dtype in scratch],
            compiler_params=pltpu.CompilerParams(vmem_limit_bytes=VMEM_LIMIT),
            cost_estimate=pl.CostEstimate(flops=flops, bytes_accessed=moved, transcendentals=0),
        )(*operands)

    return run


def neighbours(last, initial, axis):
    size = lax.axis_size(axis)
    up = [(i, i + 1) for i in range(size - 1)]
    down = [(j, i) for i, j in up]
    return (lax.ppermute(last, axis, up), lax.ppermute(initial, axis, down))


def exchange(array, axis):
    return lax.all_to_all(array, axis, split_axis=0, concat_axis=0, tiled=True)


def pair(array, axis, step):
    return lax.ppermute(array, axis, [(i, i ^ step) for i in range(lax.axis_size(axis))])


def pairs(arrays, axis):
    return [pair(array, axis, step + 1) for step, array in enumerate(arrays)]


def together(*values):
    return lax.optimization_barrier(values)


def on_device(
    video_clip, valid_from, norm_gain, spatial_weight, temporal_weight, mix_weight, cotangent
):
    video = video_clip[0]
    frames, rows, width, channels = video.shape
    outs = frames // 2
    shards = lax.axis_size("tm")
    here = rows // shards
    cells = frames * rows * width
    sizes = dict(frames=frames, rows=rows, width=width)
    info = jnp.stack(
        [
            valid_from[0],
            lax.axis_index("tm") * frames,
            lax.axis_index("cam"),
            lax.axis_index("height"),
            lax.axis_index("tm"),
        ]
    ).astype(jnp.int32)
    gain = norm_gain.reshape(1, channels)
    edge = ((frames, 1, width, channels), BF16)

    cot_out, last, first = call(
        functools.partial(prepare_kernel, outs=outs, rows=rows),
        [((shards, outs + 3, here, width, channels), BF16), edge, edge],
        moved=2 * 1024 * 1024,
    )(cotangent[0], video)
    cot_in = exchange(cot_out, "tm")
    above, below = neighbours(last, first, "height")

    wide, slope, even, odd = call(
        functools.partial(forward_kernel, **sizes),
        [
            ((cells, 3 * channels), BF16),
            ((cells, channels), F32),
            ((cells // 2, channels), BF16),
            ((cells // 2, channels), BF16),
        ],
        flops=18 * cells * channels * channels,
        moved=6 * 1024 * 1024,
    )(info, video, above, below, gain, spatial_weight)

    pre_gradient, top, bottom, strided, keep, send = call(
        functools.partial(middle_kernel, **sizes),
        [
            ((rows, frames, width, channels), BF16),
            ((frames, width, channels), BF16),
            ((frames, width, channels), BF16),
            ((shards, outs + 1, here, width, channels), BF16),
            ((15, channels, channels // 2), F32),
            ((15, channels, channels // 2), BF16),
        ],
        [
            (((outs + 3) * rows * width, channels), BF16),
            ((15, channels, channels), F32),
        ],
        flops=40 * cells * channels * channels,
        moved=12 * 1024 * 1024,
    )(info, cot_in, slope, even, odd, wide, temporal_weight, mix_weight)

    lines = lax.axis_size("height")
    large = 15 * channels // lines
    small = large // shards
    half = channels // 2
    got = pair(send, "cam", 1)
    kept, *sends = call(
        first_sum_kernel,
        [((large, half), F32)] + [((large, half), BF16)] * (lines - 1),
        moved=8 * 1024 * 1024,
    )(info, keep.reshape(lines, large, half), got.reshape(lines, large, half))
    kept, strided, top, bottom = together(kept, strided, top, bottom)
    received = pairs(sends, "height")
    regrouped = exchange(strided, "tm")
    above, below = neighbours(bottom, top, "height")
    kept, above, below = together(kept, above, below)
    kept, *sends = call(
        second_sum_kernel,
        [((small, half), F32)] + [((small, half), BF16)] * (shards - 1),
        moved=2 * 1024 * 1024,
    )(info, *[a.reshape(shards, small, half) for a in [kept] + received])
    received = pairs(sends, "tm")

    (video_gradient,) = call(
        functools.partial(input_kernel, **sizes),
        [((frames, rows, width, channels), BF16)],
        [((cells, 3 * channels), BF16)],
        flops=18 * cells * channels * channels,
        moved=4 * 1024 * 1024,
    )(info, video, pre_gradient, above, below, gain, spatial_weight)

    kept, video_gradient = together(kept, video_gradient)
    (total,) = call(last_sum_kernel, [((small, half), BF16)], moved=1024 * 1024)(
        kept, *received
    )
    received = pairs([total] * (shards - 1), "tm")
    (encoded,) = call(
        functools.partial(encode_kernel, width=width),
        [((shards * outs, here, width, channels), BF16)],
        [(((shards * outs + 2) * here * width, channels), BF16)],
        flops=3 * cells * channels * channels,
        moved=2 * 1024 * 1024,
    )(regrouped, mix_weight)
    total, encoded = together(total, encoded)
    (total,) = call(assemble_kernel, [((shards, small, half), BF16)], moved=1024 * 1024)(
        info, total, *received
    )
    total = total.reshape(large, half)
    pieces = [total] + pairs([total] * (lines - 1), "height")
    pieces = pieces + [pair(piece, "cam", 1) for piece in pieces]

    cell_count = cells * lax.axis_size("cam") * shards * lax.axis_size("height")
    smem = pl.BlockSpec(memory_space=pltpu.SMEM)
    vmem = pl.BlockSpec(memory_space=pltpu.VMEM)
    spatial, temporal, mix, gain_gradient = pl.pallas_call(
        functools.partial(finish_kernel, scale=1.0 / math.sqrt(cell_count), parts=lines),
        grid=(3,),
        out_shape=[
            jax.ShapeDtypeStruct(spatial_weight.shape, F32),
            jax.ShapeDtypeStruct(temporal_weight.shape, F32),
            jax.ShapeDtypeStruct(mix_weight.shape, F32),
            jax.ShapeDtypeStruct((1, channels), F32),
        ],
        in_specs=[smem] + [vmem] * (2 * lines + 2),
        out_specs=[
            pl.BlockSpec((1, 3, channels, channels), lambda i: (i, 0, 0, 0)),
            pl.BlockSpec((1, channels, channels), lambda i: (i, 0, 0)),
            pl.BlockSpec((1, channels, channels), lambda i: (i, 0, 0)),
            pl.BlockSpec((1, channels), lambda i: (0, 0)),
        ],
        scratch_shapes=[
            pltpu.VMEM((2, 15 * channels, half), BF16),
            pltpu.VMEM((channels, half), F32),
        ],
        compiler_params=pltpu.CompilerParams(vmem_limit_bytes=VMEM_LIMIT),
        cost_estimate=pl.CostEstimate(
            flops=0, bytes_accessed=8 * 1024 * 1024, transcendentals=0
        ),
    )(info, *pieces, gain, spatial_weight)

    return (
        encoded[None],
        video_gradient[None],
        spatial,
        temporal,
        mix,
        gain_gradient.reshape(channels),
    )


def solution(mesh):
    return jax.shard_map(
        on_device,
        mesh=mesh,
        in_specs=(
            P("cam", "tm", "height", None, None),
            P("cam"),
            P(),
            P(),
            P(),
            P(),
            P("cam", None, ("height", "tm"), None, None),
        ),
        out_specs=(
            P("cam", None, ("height", "tm"), None, None),
            P("cam", "tm", "height", None, None),
            P(),
            P(),
            P(),
            P(),
        ),
        check_vma=False,
    )
```

```python
import functools
import math

import jax
import jax.numpy as jnp
from jax import lax
from jax.experimental import pallas as pl
from jax.experimental.pallas import tpu as pltpu
from jax.sharding import PartitionSpec as P

F32 = jnp.float32
BF16 = jnp.bfloat16
VMEM_LIMIT = 16 * 1024 * 1024


def dot(left, right):
    return jnp.dot(left, right, preferred_element_type=F32)


def dot_nt(left, right):
    return lax.dot_general(left, right, (((1,), (1,)), ((), ())), preferred_element_type=F32)


def dot_tn(left, right):
    return lax.dot_general(left, right, (((0,), (0,)), ((), ())), preferred_element_type=F32)


def from_left(cells, width):
    column = lax.broadcasted_iota(jnp.int32, cells.shape, 0) % width
    return jnp.where(column == 0, 0.0, pltpu.roll(cells, 1, 0))


def from_right(cells, width):
    column = lax.broadcasted_iota(jnp.int32, cells.shape, 0) % width
    return jnp.where(column == width - 1, 0.0, pltpu.roll(cells, cells.shape[0] - 1, 0))


def present(start, frame, frames):
    return (lax.axis_index("tm") * frames + frame >= start[0]).astype(F32)


def normalised(tile, keep):
    values = tile.astype(F32) * keep
    inverse = lax.rsqrt(jnp.mean(values * values, axis=-1, keepdims=True) + 1e-06)
    return (values * inverse, inverse)


def first_frame(shard, outs, span, total):
    return jnp.minimum(shard * outs, total - span)


def prepare_kernel(cotangent, video, inner, outer, *refs, outs, rows):
    pieces, done = (refs[:-1], refs[-1])
    span = outs + 3
    odd = lax.axis_index("height") % 2
    copies = []
    for step, piece in enumerate(pieces):
        begin = first_frame(lax.axis_index("tm") ^ step, outs, span, cotangent.shape[0])
        copies.append((cotangent.at[pl.ds(begin, span)], piece))
    copies.append((video.at[:, (1 - odd) * (rows - 1)], inner))
    copies.append((video.at[:, odd * (rows - 1)], outer))
    copies = [
        pltpu.make_async_copy(source, target, done.at[at])
        for at, (source, target) in enumerate(copies)
    ]
    for copy in copies:
        copy.start()
    for copy in copies:
        copy.wait()


def place_halos(halo, inner, outer):
    odd = lax.axis_index("height") % 2
    halo[1 - odd] = inner[...]
    halo[odd] = outer[...]


def forward_kernel(
    start, video, inner, outer, gain, weight, wide, slope, even, odd, halo, *, frames, rows, width
):
    place_halos(halo, inner, outer)
    block = frames * width
    for row in range(-1, rows + 1):
        for frame in range(frames):
            if row < 0:
                tile = halo[0, frame]
            elif row == rows:
                tile = halo[1, frame]
            else:
                tile = video[frame, row]
            unit, _ = normalised(tile, present(start, frame, frames))
            normed = (unit * gain[...]).astype(BF16)
            for tap in range(3):
                target = row + 1 - tap
                if 0 <= target < rows:
                    at = target * block + frame * width
                    wide[at : at + width, tap * 256 : tap * 256 + 256] = normed
    for row in range(rows):
        cells = wide[row * block : row * block + block]
        taps = [
            dot(cells, jnp.concatenate([weight[0, j], weight[1, j], weight[2, j]], axis=0))
            for j in range(3)
        ]
        pre = from_left(taps[0], width) + taps[1] + from_right(taps[2], width)
        sigmoid = 1.0 / (1.0 + jnp.exp(-pre))
        active = (pre * sigmoid).astype(BF16)
        slope[row * block : row * block + block] = sigmoid * (1.0 + pre * (1.0 - sigmoid))
        for frame in range(frames):
            target = odd if frame % 2 else even
            at = (frame // 2) * rows * width + row * width
            target[at : at + width] = active[frame * width : frame * width + width]


def middle_kernel(
    slope, even, odd, wide, temporal, mix, *refs, frames, rows, width, shards
):
    outs = frames // 2
    plane = rows * width
    here = rows // shards
    pieces, refs = (refs[:shards], refs[shards:])
    pre_gradient, inner, outer, keep, send, *refs = refs
    strided, (cot, sums, lines) = (refs[:shards], refs[shards:])
    me = lax.axis_index("tm")
    total = shards * outs
    cut = outs + 3
    skip = me * outs - first_frame(me, outs, cut, total)
    for frame in range(cut):
        here_is = (me * outs + frame < total).astype(F32)
        for step, piece in enumerate(pieces):
            cells = piece[jnp.minimum(frame + skip, cut - 1)].astype(F32) * here_is
            cot[frame, me ^ step] = cells.astype(BF16).reshape(here * width, 256)

    def ahead(k, count=outs + 1):
        return cot[k : k + count].reshape(count * plane, 256)

    gradient = ahead(0).astype(F32)
    for k in range(3):
        gradient = gradient + dot_nt(ahead(k), mix[k])
    gradient = gradient.astype(BF16)
    now = gradient[: outs * plane]
    later = gradient[plane:]
    even_gradient = dot_nt(now, temporal[1])
    odd_gradient = dot_nt(now, temporal[0]) + dot_nt(later, temporal[2])
    for row in range(rows):
        for frame in range(frames):
            source = odd_gradient if frame % 2 else even_gradient
            at = (frame // 2) * plane + row * width
            to = (row * frames + frame) * width
            tile = (source[at : at + width] * slope[to : to + width]).astype(BF16)
            pre_gradient[row, frame] = tile
    side = (lax.axis_index("height") % 2) * (rows - 1)
    inner[...] = pre_gradient[rows - 1 - side]
    outer[...] = pre_gradient[side]
    evens = even[...]
    odds = odd[...]
    carried = dot(odds, temporal[2])
    mixed = dot(odds, temporal[0]) + dot(evens, temporal[1])
    parts = [mixed[:plane]]
    for s in range(1, outs):
        parts.append(
            mixed[s * plane : s * plane + plane] + carried[(s - 1) * plane : s * plane]
        )
    parts.append(carried[(outs - 1) * plane :])
    parts = jnp.concatenate(parts, axis=0).astype(BF16)
    for frame in range(outs + 1):
        cells = parts[frame * plane : frame * plane + plane]
        lines[:, frame * here * width : (frame + 1) * here * width] = cells.reshape(
            shards, here * width, 256
        )
    for step, piece in enumerate(strided):
        piece[...] = lines[me ^ step].reshape(piece.shape)
    for k in range(3):
        sums[k] = dot_tn(parts, ahead(k))
    sums[3] = dot_tn(odds, now)
    sums[4] = dot_tn(evens, now)
    sums[5] = dot_tn(odds, later)
    gradient = pre_gradient[...].reshape(-1, 256)
    exact = gradient.astype(F32)
    columns = [
        from_right(exact, width).astype(BF16), gradient, from_left(exact, width).astype(BF16)
    ]
    for i in range(3):
        normed = wide[:, i * 256 : i * 256 + 256]
        product = dot_tn(normed, jnp.concatenate(columns, axis=1))
        for j in range(3):
            sums[6 + i * 3 + j] = product[:, j * 256 : j * 256 + 256]
    mine, other = core_columns()
    keep[...] = sums[:, :, mine]
    send[...] = sums[:, :, other].astype(BF16)


def core_columns():
    mine = pl.ds(pl.multiple_of(lax.axis_index("cam") * 128, 128), 128)
    other = pl.ds(pl.multiple_of((1 - lax.axis_index("cam")) * 128, 128), 128)
    return (mine, other)


def deal(axis, total, kept, sends):
    me = lax.axis_index(axis)
    kept[...] = total(me)
    for step, send in enumerate(sends):
        send[...] = total(me ^ (step + 1)).astype(BF16)


def first_sum_kernel(keep, got, kept, *sends):
    deal("height", lambda at: keep[at] + got[at].astype(F32), kept, sends)


def second_sum_kernel(kept_in, *refs):
    count = kept_in.shape[0]
    received = refs[: len(refs) - count]
    kept, *sends = refs[len(refs) - count :]

    def total(at):
        value = kept_in[at]
        for piece in received:
            value = value + piece[at].astype(F32)
        return value

    deal("tm", total, kept, sends)


def last_sum_kernel(kept, *refs):
    value = kept[...]
    for piece in refs[:-1]:
        value = value + piece[...].astype(F32)
    refs[-1][...] = value.astype(BF16)


def assemble_kernel(*refs):
    for step, piece in enumerate(refs[:-1]):
        refs[-1][lax.axis_index("tm") ^ step] = piece[...]


def input_kernel(
    start, video, pre_gradient, inner, outer, gain, weight, out, tall, halo, *, frames, rows, width
):
    place_halos(halo, inner, outer)
    block = frames * width
    for row in range(-1, rows + 1):
        if row < 0:
            cells = halo[0]
        elif row == rows:
            cells = halo[1]
        else:
            cells = pre_gradient[row]
        cells = cells.reshape(block, 256)
        for tap in range(3):
            target = row - 1 + tap
            if 0 <= target < rows:
                tall[target * block : target * block + block, tap * 256 : tap * 256 + 256] = cells
    for row in range(rows):
        cells = tall[row * block : row * block + block]
        taps = [
            dot_nt(cells, jnp.concatenate([weight[0, j], weight[1, j], weight[2, j]], axis=1))
            for j in range(3)
        ]
        gradient = from_right(taps[0], width) + taps[1] + from_left(taps[2], width)
        gradient = gradient * gain[...]
        for frame in range(frames):
            keep = present(start, frame, frames)
            unit, inverse = normalised(video[frame, row], keep)
            tile = gradient[frame * width : frame * width + width]
            mean = jnp.mean(tile * unit, axis=-1, keepdims=True)
            out[frame, row] = (inverse * (tile - unit * mean) * keep).astype(BF16)


def encode_kernel(mix, *refs, width, shards):
    pieces, (out, line, strided) = (refs[:shards], refs[shards:])
    for step, piece in enumerate(pieces):
        strided[lax.axis_index("tm") ^ step] = piece[...]
    parts, here = strided.shape[1:3]
    outs = parts - 1
    plane = here * width
    total = shards * outs
    for frame in range(total):
        shard, part = (frame // outs, frame % outs)
        cells = strided[shard, part].reshape(plane, 256)
        if part == 0 and shard > 0:
            carried = strided[shard - 1, outs].reshape(plane, 256)
            cells = (cells.astype(F32) + carried.astype(F32)).astype(BF16)
        line[(frame + 2) * plane : (frame + 3) * plane] = cells
    line[0 : 2 * plane] = jnp.zeros((2 * plane, 256), BF16)
    span = total * plane
    result = line[2 * plane : 2 * plane + span].astype(F32)
    for k in range(3):
        result = result + dot(line[(2 - k) * plane : (2 - k) * plane + span], mix[k])
    out[...] = result.astype(BF16).reshape(out.shape)


def finish_kernel(*refs, scale, parts):
    pieces = refs[: 2 * parts]
    gain, weight, spatial, temporal, mix, gain_out, whole, total = refs[2 * parts :]
    step = pl.program_id(0)
    size = whole.shape[1] // parts

    @pl.when(step == 0)
    def _():
        for core in range(2):
            for part in range(parts):
                at = pl.multiple_of((lax.axis_index("height") ^ part) * size, size)
                whole[core, pl.ds(at, size)] = pieces[core * parts + part][...]
        total[...] = jnp.zeros_like(total)

    for core, columns in enumerate(core_columns()):

        def matrix(index):
            at = pl.multiple_of(index * 256, 256)
            return whole[core, pl.ds(at, 256)].astype(F32) * scale

        mix[0, :, columns] = matrix(step)
        temporal[0, :, columns] = matrix(step + 3)
        for j in range(3):
            piece = matrix(step * 3 + (6 + j))
            spatial[0, j, :, columns] = piece
            total[...] += piece * weight[step, j, :, columns].astype(F32)

    @pl.when(step == 2)
    def _():
        gain_out[...] = jnp.sum(total[...].T, axis=0, keepdims=True) / gain[...]


def call(kernel, outs, scratch=(), flops=0, moved=0, space=pltpu.VMEM):
    smem = pl.BlockSpec(memory_space=pltpu.SMEM)
    vmem = pl.BlockSpec(memory_space=pltpu.VMEM)

    def run(*operands):
        return pl.pallas_call(
            kernel,
            out_shape=[jax.ShapeDtypeStruct(shape, dtype) for shape, dtype in outs],
            in_specs=[
                smem if a.dtype == jnp.int32 else pl.BlockSpec(memory_space=space)
                for a in operands
            ],
            out_specs=[vmem] * len(outs),
            scratch_shapes=list(scratch),
            compiler_params=pltpu.CompilerParams(vmem_limit_bytes=VMEM_LIMIT),
            cost_estimate=pl.CostEstimate(flops=flops, bytes_accessed=moved, transcendentals=0),
        )(*operands)

    return run


def neighbours(inner, outer, axis):
    size = lax.axis_size(axis)
    links = [(i, i + 1) for i in range(1, size - 1, 2)]
    links = links + [(j, i) for i, j in links]
    return (pair(inner, axis, 1), lax.ppermute(outer, axis, links))


def pair(array, axis, step):
    return lax.ppermute(array, axis, [(i, i ^ step) for i in range(lax.axis_size(axis))])


def pairs(arrays, axis):
    return [pair(array, axis, step + 1) for step, array in enumerate(arrays)]


def together(*values):
    return lax.optimization_barrier(values)


def on_device(
    video_clip, valid_from, norm_gain, spatial_weight, temporal_weight, mix_weight, cotangent
):
    video = video_clip[0]
    frames, rows, width, channels = video.shape
    outs = frames // 2
    shards = lax.axis_size("tm")
    lines = lax.axis_size("height")
    here = rows // shards
    cells = frames * rows * width
    sizes = dict(frames=frames, rows=rows, width=width)
    gain = norm_gain.reshape(1, channels)
    edge = ((frames, width, channels), BF16)
    halo = pltpu.VMEM((2, frames, width, channels), BF16)

    inner, outer, *pieces = call(
        functools.partial(prepare_kernel, outs=outs, rows=rows),
        [edge, edge] + [((outs + 3, here, width, channels), BF16)] * shards,
        [pltpu.SemaphoreType.DMA((shards + 2,))],
        moved=2 * 1024 * 1024,
        space=pltpu.HBM,
    )(cotangent[0], video)
    pieces = [pieces[0]] + pairs(pieces[1:], "tm")
    inner, outer = neighbours(inner, outer, "height")

    wide, slope, even, odd = call(
        functools.partial(forward_kernel, **sizes),
        [
            ((cells, 3 * channels), BF16),
            ((cells, channels), F32),
            ((cells // 2, channels), BF16),
            ((cells // 2, channels), BF16),
        ],
        [halo],
        flops=18 * cells * channels * channels,
        moved=6 * 1024 * 1024,
    )(valid_from, video, inner, outer, gain, spatial_weight)

    pre_gradient, inner, outer, keep, send, *strided = call(
        functools.partial(middle_kernel, **sizes, shards=shards),
        [
            ((rows, frames, width, channels), BF16),
            edge,
            edge,
            ((15, channels, channels // 2), F32),
            ((15, channels, channels // 2), BF16),
        ]
        + [((outs + 1, here, width, channels), BF16)] * shards,
        [
            pltpu.VMEM((outs + 3, shards, here * width, channels), BF16),
            pltpu.VMEM((15, channels, channels), F32),
            pltpu.VMEM((shards, (outs + 1) * here * width, channels), BF16),
        ],
        flops=40 * cells * channels * channels,
        moved=12 * 1024 * 1024,
    )(slope, even, odd, wide, temporal_weight, mix_weight, *pieces)

    large = 15 * channels // lines
    small = large // shards
    half = channels // 2
    got = pair(send, "cam", 1)
    strided = [strided[0]] + pairs(strided[1:], "tm")
    kept, *sends = call(
        first_sum_kernel,
        [((large, half), F32)] + [((large, half), BF16)] * (lines - 1),
        moved=8 * 1024 * 1024,
    )(keep.reshape(lines, large, half), got.reshape(lines, large, half))
    received = pairs(sends, "height")
    kept, *sends = call(
        second_sum_kernel,
        [((small, half), F32)] + [((small, half), BF16)] * (shards - 1),
        moved=2 * 1024 * 1024,
    )(*[a.reshape(shards, small, half) for a in [kept] + received])
    received = pairs(sends, "tm")
    kept, inner, outer = together(kept, inner, outer)
    inner, outer = neighbours(inner, outer, "height")
    kept, inner, outer = together(kept, inner, outer)
    (total,) = call(last_sum_kernel, [((small, half), BF16)], moved=1024 * 1024)(
        kept, *received
    )
    received = pairs([total] * (shards - 1), "tm")
    (video_gradient,) = call(
        functools.partial(input_kernel, **sizes),
        [((frames, rows, width, channels), BF16)],
        [pltpu.VMEM((cells, 3 * channels), BF16), halo],
        flops=18 * cells * channels * channels,
        moved=4 * 1024 * 1024,
    )(valid_from, video, pre_gradient, inner, outer, gain, spatial_weight)
    total, video_gradient = together(total, video_gradient)
    (total,) = call(assemble_kernel, [((shards, small, half), BF16)], moved=1024 * 1024)(
        total, *received
    )
    total = total.reshape(large, half)
    pieces = [total] + pairs([total] * (lines - 1), "height")
    (encoded,) = call(
        functools.partial(encode_kernel, width=width, shards=shards),
        [((shards * outs, here, width, channels), BF16)],
        [
            pltpu.VMEM(((shards * outs + 2) * here * width, channels), BF16),
            pltpu.VMEM((shards, outs + 1, here, width, channels), BF16),
        ],
        flops=3 * cells * channels * channels,
        moved=2 * 1024 * 1024,
    )(mix_weight, *strided)
    pieces[-1], encoded = together(pieces[-1], encoded)
    pieces = pieces + [pair(piece, "cam", 1) for piece in pieces]

    cell_count = cells * lax.axis_size("cam") * shards * lines
    vmem = pl.BlockSpec(memory_space=pltpu.VMEM)
    spatial, temporal, mix, gain_gradient = pl.pallas_call(
        functools.partial(finish_kernel, scale=1.0 / math.sqrt(cell_count), parts=lines),
        grid=(3,),
        out_shape=[
            jax.ShapeDtypeStruct(spatial_weight.shape, F32),
            jax.ShapeDtypeStruct(temporal_weight.shape, F32),
            jax.ShapeDtypeStruct(mix_weight.shape, F32),
            jax.ShapeDtypeStruct((1, channels), F32),
        ],
        in_specs=[vmem] * (2 * lines + 2),
        out_specs=[
            pl.BlockSpec((1, 3, channels, channels), lambda i: (i, 0, 0, 0)),
            pl.BlockSpec((1, channels, channels), lambda i: (i, 0, 0)),
            pl.BlockSpec((1, channels, channels), lambda i: (i, 0, 0)),
            pl.BlockSpec((1, channels), lambda i: (0, 0)),
        ],
        scratch_shapes=[
            pltpu.VMEM((2, 15 * channels, half), BF16),
            pltpu.VMEM((channels, half), F32),
        ],
        compiler_params=pltpu.CompilerParams(vmem_limit_bytes=VMEM_LIMIT),
        cost_estimate=pl.CostEstimate(
            flops=0, bytes_accessed=8 * 1024 * 1024, transcendentals=0
        ),
    )(*pieces, gain, spatial_weight)

    return (
        encoded[None],
        video_gradient[None],
        spatial,
        temporal,
        mix,
        gain_gradient.reshape(channels),
    )


def solution(mesh):
    return jax.shard_map(
        on_device,
        mesh=mesh,
        in_specs=(
            P("cam", "tm", "height", None, None),
            P("cam"),
            P(),
            P(),
            P(),
            P(),
            P("cam", None, ("height", "tm"), None, None),
        ),
        out_specs=(
            P("cam", None, ("height", "tm"), None, None),
            P("cam", "tm", "height", None, None),
            P(),
            P(),
            P(),
            P(),
        ),
        check_vma=False,
    )
```

```python
import functools
import math

import jax
import jax.numpy as jnp
from jax import lax
from jax.experimental import pallas as pl
from jax.experimental.pallas import tpu as pltpu
from jax.sharding import PartitionSpec as P

F32 = jnp.float32
BF16 = jnp.bfloat16
VMEM_LIMIT = 16 * 1024 * 1024
FIRST_LIMIT = 56 * 1024 * 1024


def dot(left, right):
    return jnp.dot(left, right, preferred_element_type=F32)


def dot_nt(left, right):
    return lax.dot_general(left, right, (((1,), (1,)), ((), ())), preferred_element_type=F32)


def dot_tn(left, right):
    return lax.dot_general(left, right, (((0,), (0,)), ((), ())), preferred_element_type=F32)


def from_left(cells, width):
    column = lax.broadcasted_iota(jnp.int32, cells.shape, 0) % width
    return jnp.where(column == 0, 0.0, pltpu.roll(cells, 1, 0))


def from_right(cells, width):
    column = lax.broadcasted_iota(jnp.int32, cells.shape, 0) % width
    return jnp.where(column == width - 1, 0.0, pltpu.roll(cells, cells.shape[0] - 1, 0))


def present(start, frame, frames):
    return (lax.axis_index("tm") * frames + frame >= start[0]).astype(F32)


def normalised(tile, keep):
    values = tile.astype(F32) * keep
    inverse = lax.rsqrt(jnp.mean(values * values, axis=-1, keepdims=True) + 1e-06)
    return (values * inverse, inverse)


def first_frame(shard, outs, span, total):
    return jnp.minimum(shard * outs, total - span)


def run_copies(pairs_of_refs, done):
    copies = [
        pltpu.make_async_copy(source, target, done.at[at])
        for at, (source, target) in enumerate(pairs_of_refs)
    ]
    for copy in copies:
        copy.start()
    for copy in copies:
        copy.wait()


def pieces_kernel(cotangent, *refs, outs):
    pieces, done = (refs[:-1], refs[-1])
    span = outs + 3
    me = lax.axis_index("tm")
    copies = []
    for step, piece in enumerate(pieces):
        begin = first_frame(me ^ step, outs, span, cotangent.shape[0])
        copies.append((cotangent.at[pl.ds(begin, span)], piece))
    run_copies(copies, done)


def edges_kernel(video, inner, outer, done, *, rows):
    odd = lax.axis_index("height") % 2
    run_copies(
        [
            (video.at[:, (1 - odd) * (rows - 1)], inner),
            (video.at[:, odd * (rows - 1)], outer),
        ],
        done,
    )


def first_frame(shard, outs, span, total):
    return jnp.minimum(shard * outs, total - span)


def place_halos(halo, inner, outer):
    odd = lax.axis_index("height") % 2
    halo[1 - odd] = inner[...]
    halo[odd] = outer[...]


def column_sum(cells, weight, taps, width):
    products = [
        dot(cells, jnp.concatenate([weight[i, j] for i in taps], axis=0)) for j in range(3)
    ]
    return from_left(products[0], width) + products[1] + from_right(products[2], width)


def own_kernel(
    valid_from, video, gain, weight, normed, partial, start, done, *, frames, rows, width
):
    run_copies([(valid_from, start)], done)
    block = frames * width
    for row in range(rows):
        for frame in range(frames):
            unit, _ = normalised(video[frame, row], present(start, frame, frames))
            at = row * block + frame * width
            normed[at : at + width] = (unit * gain[...]).astype(BF16)
    for row in range(rows):
        taps = [i for i in range(3) if 0 <= row + i - 1 < rows]
        cells = [normed[(row + i - 1) * block : (row + i) * block] for i in taps]
        partial[row * block : row * block + block] = column_sum(
            jnp.concatenate(cells, axis=1), weight, taps, width
        )


def middle_kernel(
    valid_from, normed, partial, inner, outer, gain, weight, temporal, mix, *refs,
    frames, rows, width, shards
):
    pieces, refs = (refs[:shards], refs[shards:])
    pre_gradient, inner_out, outer_out, keep, send, *refs = refs
    strided, refs = (refs[:shards], refs[shards:])
    tall, slope, active, halo, start, done, cot, sums, lines = refs
    outs = frames // 2
    plane = rows * width
    here = rows // shards
    block = frames * width

    run_copies([(valid_from, start)], done)
    place_halos(halo, inner, outer)
    tall[block : block + rows * block] = normed[...]
    for side, at in ((0, 0), (1, (rows + 1) * block)):
        for frame in range(frames):
            unit, _ = normalised(halo[side, frame], present(start, frame, frames))
            to = at + frame * width
            tall[to : to + width] = (unit * gain[...]).astype(BF16)
    for row in range(rows):
        pre = partial[row * block : row * block + block]
        if row == 0:
            pre = pre + column_sum(tall[:block], weight, [0], width)
        if row == rows - 1:
            pre = pre + column_sum(tall[(rows + 1) * block :], weight, [2], width)
        sigmoid = 1.0 / (1.0 + jnp.exp(-pre))
        slope[row * block : row * block + block] = sigmoid * (1.0 + pre * (1.0 - sigmoid))
        cells = (pre * sigmoid).astype(BF16)
        for frame in range(frames):
            at = (frame // 2) * plane + row * width
            active[frame % 2, at : at + width] = cells[frame * width : frame * width + width]
    evens = active[0]
    odds = active[1]
    carried = dot(odds, temporal[2])
    mixed = dot(odds, temporal[0]) + dot(evens, temporal[1])
    parts = [mixed[:plane]]
    for s in range(1, outs):
        parts.append(
            mixed[s * plane : s * plane + plane] + carried[(s - 1) * plane : s * plane]
        )
    parts.append(carried[(outs - 1) * plane :])
    parts = jnp.concatenate(parts, axis=0).astype(BF16)
    for frame in range(outs + 1):
        cells = parts[frame * plane : frame * plane + plane]
        lines[:, frame] = cells.reshape(shards, here, width, 256)
    for step, piece in enumerate(strided):
        piece[...] = lines[lax.axis_index("tm") ^ step]
    me = lax.axis_index("tm")
    total = shards * outs
    cut = outs + 3
    skip = me * outs - first_frame(me, outs, cut, total)
    for frame in range(cut):
        here_is = (me * outs + frame < total).astype(F32)
        for step, piece in enumerate(reversed(pieces)):
            cells = piece[jnp.minimum(frame + skip, cut - 1)].astype(F32) * here_is
            cot[frame, me ^ step] = cells.astype(BF16).reshape(here * width, 256)

    def ahead(k, count=outs + 1):
        return cot[k : k + count].reshape(count * plane, 256)

    gradient = ahead(0).astype(F32)
    for k in range(3):
        gradient = gradient + dot_nt(ahead(k), mix[k])
    gradient = gradient.astype(BF16)
    now = gradient[: outs * plane]
    later = gradient[plane:]
    even_gradient = dot_nt(now, temporal[1])
    odd_gradient = dot_nt(now, temporal[0]) + dot_nt(later, temporal[2])
    for row in range(rows):
        for frame in range(frames):
            source = odd_gradient if frame % 2 else even_gradient
            at = (frame // 2) * plane + row * width
            to = (row * frames + frame) * width
            tile = (source[at : at + width] * slope[to : to + width]).astype(BF16)
            pre_gradient[row, frame] = tile
    side = (lax.axis_index("height") % 2) * (rows - 1)
    inner_out[...] = pre_gradient[rows - 1 - side]
    outer_out[...] = pre_gradient[side]
    for k in range(3):
        sums[k] = dot_tn(parts, ahead(k))
    sums[3] = dot_tn(odds, now)
    sums[4] = dot_tn(evens, now)
    sums[5] = dot_tn(odds, later)
    gradient = pre_gradient[...].reshape(-1, 256)
    exact = gradient.astype(F32)
    columns = [
        from_right(exact, width).astype(BF16), gradient, from_left(exact, width).astype(BF16)
    ]
    for i in range(3):
        cells = tall[i * block : (i + rows) * block]
        product = dot_tn(cells, jnp.concatenate(columns, axis=1))
        for j in range(3):
            sums[6 + i * 3 + j] = product[:, j * 256 : j * 256 + 256]
    mine, other = core_columns()
    keep[...] = sums[:, :, mine]
    send[...] = sums[:, :, other].astype(BF16)


def core_columns():
    mine = pl.ds(pl.multiple_of(lax.axis_index("cam") * 128, 128), 128)
    other = pl.ds(pl.multiple_of((1 - lax.axis_index("cam")) * 128, 128), 128)
    return (mine, other)


def deal(axis, total, kept, sends):
    me = lax.axis_index(axis)
    kept[...] = total(me)
    for step, send in enumerate(sends):
        send[...] = total(me ^ (step + 1)).astype(BF16)


def first_sum_kernel(keep, got, kept, *sends):
    deal("height", lambda at: keep[at] + got[at].astype(F32), kept, sends)


def second_sum_kernel(kept_in, *refs):
    count = kept_in.shape[0]
    received = refs[: len(refs) - count]
    kept, *sends = refs[len(refs) - count :]

    def total(at):
        value = kept_in[at]
        for piece in received:
            value = value + piece[at].astype(F32)
        return value

    deal("tm", total, kept, sends)


def last_sum_kernel(kept, *refs):
    value = kept[...]
    for piece in refs[:-1]:
        value = value + piece[...].astype(F32)
    refs[-1][...] = value.astype(BF16)


def assemble_kernel(*refs):
    for step, piece in enumerate(reversed(refs[:-1])):
        refs[-1][lax.axis_index("tm") ^ step] = piece[...]


def input_kernel(
    valid_from, video, pre_gradient, inner, outer, gain, weight, out, tall, halo, start, done,
    *, frames, rows, width
):
    run_copies([(valid_from, start)], done)
    place_halos(halo, inner, outer)
    block = frames * width
    for row in range(-1, rows + 1):
        if row < 0:
            cells = halo[0]
        elif row == rows:
            cells = halo[1]
        else:
            cells = pre_gradient[row]
        cells = cells.reshape(block, 256)
        for tap in range(3):
            target = row - 1 + tap
            if 0 <= target < rows:
                tall[target * block : target * block + block, tap * 256 : tap * 256 + 256] = cells
    for row in range(rows):
        cells = tall[row * block : row * block + block]
        taps = [
            dot_nt(cells, jnp.concatenate([weight[0, j], weight[1, j], weight[2, j]], axis=1))
            for j in range(3)
        ]
        gradient = from_right(taps[0], width) + taps[1] + from_left(taps[2], width)
        gradient = gradient * gain[...]
        for frame in range(frames):
            keep = present(start, frame, frames)
            unit, inverse = normalised(video[frame, row], keep)
            tile = gradient[frame * width : frame * width + width]
            mean = jnp.mean(tile * unit, axis=-1, keepdims=True)
            out[frame, row] = (inverse * (tile - unit * mean) * keep).astype(BF16)


def encode_kernel(mix, *refs, width, shards):
    pieces, (out, line, strided) = (refs[:shards], refs[shards:])
    for step, piece in enumerate(pieces):
        strided[lax.axis_index("tm") ^ step] = piece[...]
    parts, here = strided.shape[1:3]
    outs = parts - 1
    plane = here * width
    total = shards * outs
    for frame in range(total):
        shard, part = (frame // outs, frame % outs)
        cells = strided[shard, part].reshape(plane, 256)
        if part == 0 and shard > 0:
            carried = strided[shard - 1, outs].reshape(plane, 256)
            cells = (cells.astype(F32) + carried.astype(F32)).astype(BF16)
        line[(frame + 2) * plane : (frame + 3) * plane] = cells
    line[0 : 2 * plane] = jnp.zeros((2 * plane, 256), BF16)
    span = total * plane
    result = line[2 * plane : 2 * plane + span].astype(F32)
    for k in range(3):
        result = result + dot(line[(2 - k) * plane : (2 - k) * plane + span], mix[k])
    out[...] = result.astype(BF16).reshape(out.shape)


def finish_kernel(*refs, scale, parts):
    pieces = refs[: 2 * parts]
    gain, weight, spatial, temporal, mix, gain_out, whole, total = refs[2 * parts :]
    step = pl.program_id(0)
    size = whole.shape[1] // parts

    @pl.when(step == 0)
    def _():
        for core in range(2):
            for part in range(parts):
                at = pl.multiple_of((lax.axis_index("height") ^ part) * size, size)
                whole[core, pl.ds(at, size)] = pieces[core * parts + part][...]
        total[...] = jnp.zeros_like(total)

    for core, columns in enumerate(core_columns()):

        def matrix(index):
            at = pl.multiple_of(index * 256, 256)
            return whole[core, pl.ds(at, 256)].astype(F32) * scale

        mix[0, :, columns] = matrix(step)
        temporal[0, :, columns] = matrix(step + 3)
        for j in range(3):
            piece = matrix(step * 3 + (6 + j))
            spatial[0, j, :, columns] = piece
            total[...] += piece * weight[step, j, :, columns].astype(F32)

    @pl.when(step == 2)
    def _():
        gain_out[...] = jnp.sum(total[...].T, axis=0, keepdims=True) / gain[...]


def call(kernel, outs, scratch=(), flops=0, moved=0, space=pltpu.VMEM, limit=VMEM_LIMIT):
    vmem = pl.BlockSpec(memory_space=pltpu.VMEM)

    def run(*operands):
        results = pl.pallas_call(
            kernel,
            out_shape=[jax.ShapeDtypeStruct(shape, dtype) for shape, dtype in outs],
            in_specs=[
                pl.BlockSpec(memory_space=pltpu.HBM if a.dtype == jnp.int32 else space)
                for a in operands
            ],
            out_specs=[vmem] * len(outs),
            scratch_shapes=list(scratch),
            compiler_params=pltpu.CompilerParams(vmem_limit_bytes=limit),
            cost_estimate=pl.CostEstimate(flops=flops, bytes_accessed=moved, transcendentals=0),
        )(*operands)
        return list(results)

    return run


def neighbours(inner, outer, axis):
    size = lax.axis_size(axis)
    links = [(i, i + 1) for i in range(1, size - 1, 2)]
    links = links + [(j, i) for i, j in links]
    return (pair(inner, axis, 1), lax.ppermute(outer, axis, links))


def pair(array, axis, step):
    return lax.ppermute(array, axis, [(i, i ^ step) for i in range(lax.axis_size(axis))])


def pairs(arrays, axis):
    return [pair(array, axis, step + 1) for step, array in enumerate(arrays)]


def together(*values):
    return lax.optimization_barrier(values)


def on_device(
    video_clip, valid_from, norm_gain, spatial_weight, temporal_weight, mix_weight, cotangent
):
    video = video_clip[0]
    frames, rows, width, channels = video.shape
    outs = frames // 2
    shards = lax.axis_size("tm")
    lines = lax.axis_size("height")
    here = rows // shards
    cells = frames * rows * width
    sizes = dict(frames=frames, rows=rows, width=width)
    gain = norm_gain.reshape(1, channels)
    edge = ((frames, width, channels), BF16)
    halo = pltpu.VMEM((2, frames, width, channels), BF16)

    scalar = [pltpu.SMEM((1,), jnp.int32), pltpu.SemaphoreType.DMA((1,))]
    pieces = call(
        functools.partial(pieces_kernel, outs=outs),
        [((outs + 3, here, width, channels), BF16)] * shards,
        [pltpu.SemaphoreType.DMA((shards,))],
        moved=1024 * 1024,
        space=pltpu.HBM,
        limit=FIRST_LIMIT,
    )(cotangent[0])
    *pieces, edges = together(*pieces, video)
    pieces = [pieces[0]] + pairs(pieces[1:], "tm")
    inner, outer = call(
        functools.partial(edges_kernel, rows=rows),
        [edge, edge],
        [pltpu.SemaphoreType.DMA((2,))],
        moved=512 * 1024,
        space=pltpu.HBM,
        limit=FIRST_LIMIT,
    )(edges)
    inner, outer = neighbours(inner, outer, "height")

    normed, partial = call(
        functools.partial(own_kernel, **sizes),
        [((cells, channels), BF16), ((cells, channels), F32)],
        scalar,
        flops=18 * cells * channels * channels,
        moved=4 * 1024 * 1024,
    )(valid_from, video, gain, spatial_weight)

    pre_gradient, inner, outer, keep, send, *strided = call(
        functools.partial(middle_kernel, **sizes, shards=shards),
        [
            ((rows, frames, width, channels), BF16),
            edge,
            edge,
            ((15, channels, channels // 2), F32),
            ((15, channels, channels // 2), BF16),
        ]
        + [((outs + 1, here, width, channels), BF16)] * shards,
        [
            pltpu.VMEM((cells + 2 * frames * width, channels), BF16),
            pltpu.VMEM((cells, channels), F32),
            pltpu.VMEM((2, cells // 2, channels), BF16),
            halo,
            *scalar,
            pltpu.VMEM((outs + 3, shards, here * width, channels), BF16),
            pltpu.VMEM((15, channels, channels), F32),
            pltpu.VMEM((shards, outs + 1, here, width, channels), BF16),
        ],
        flops=46 * cells * channels * channels,
        moved=12 * 1024 * 1024,
    )(
        valid_from, normed, partial, inner, outer, gain, spatial_weight, temporal_weight,
        mix_weight, *reversed(pieces),
    )

    large = 15 * channels // lines
    small = large // shards
    half = channels // 2
    got = pair(send, "cam", 1)
    kept, *sends = call(
        first_sum_kernel,
        [((large, half), F32)] + [((large, half), BF16)] * (lines - 1),
        moved=8 * 1024 * 1024,
    )(keep.reshape(lines, large, half), got.reshape(lines, large, half))
    received = pairs(sends, "height")
    strided = [strided[0]] + pairs(strided[1:], "tm")
    kept, *strided = together(kept, *strided)
    kept, *sends = call(
        second_sum_kernel,
        [((small, half), F32)] + [((small, half), BF16)] * (shards - 1),
        moved=2 * 1024 * 1024,
    )(*[a.reshape(shards, small, half) for a in [kept] + received[::-1]])
    received = pairs(sends, "tm")
    (encoded,) = call(
        functools.partial(encode_kernel, width=width, shards=shards),
        [((shards * outs, here, width, channels), BF16)],
        [
            pltpu.VMEM(((shards * outs + 2) * here * width, channels), BF16),
            pltpu.VMEM((shards, outs + 1, here, width, channels), BF16),
        ],
        flops=3 * cells * channels * channels,
        moved=2 * 1024 * 1024,
    )(mix_weight, *strided)
    kept, encoded = together(kept, encoded)
    (total,) = call(last_sum_kernel, [((small, half), BF16)], moved=1024 * 1024)(
        kept, *received[::-1]
    )
    total, inner, outer = together(total, inner, outer)
    received = pairs([total] * (shards - 1), "tm")
    inner, outer = neighbours(inner, outer, "height")
    *received, total, inner, outer = together(*received[::-1], total, inner, outer)
    (total,) = call(assemble_kernel, [((shards, small, half), BF16)], moved=1024 * 1024)(
        *received, total
    )
    total = total.reshape(large, half)
    pieces = [total] + pairs([total] * (lines - 1), "height")
    (video_gradient,) = call(
        functools.partial(input_kernel, **sizes),
        [((frames, rows, width, channels), BF16)],
        [pltpu.VMEM((cells, 3 * channels), BF16), halo] + scalar,
        flops=18 * cells * channels * channels,
        moved=4 * 1024 * 1024,
    )(valid_from, video, pre_gradient, inner, outer, gain, spatial_weight)
    pieces[-1], video_gradient = together(pieces[-1], video_gradient)
    pieces = pieces + [pair(piece, "cam", 1) for piece in pieces]

    cell_count = cells * lax.axis_size("cam") * shards * lines
    vmem = pl.BlockSpec(memory_space=pltpu.VMEM)
    spatial, temporal, mix, gain_gradient = pl.pallas_call(
        functools.partial(finish_kernel, scale=1.0 / math.sqrt(cell_count), parts=lines),
        grid=(3,),
        out_shape=[
            jax.ShapeDtypeStruct(spatial_weight.shape, F32),
            jax.ShapeDtypeStruct(temporal_weight.shape, F32),
            jax.ShapeDtypeStruct(mix_weight.shape, F32),
            jax.ShapeDtypeStruct((1, channels), F32),
        ],
        in_specs=[vmem] * (2 * lines + 2),
        out_specs=[
            pl.BlockSpec((1, 3, channels, channels), lambda i: (i, 0, 0, 0)),
            pl.BlockSpec((1, channels, channels), lambda i: (i, 0, 0)),
            pl.BlockSpec((1, channels, channels), lambda i: (i, 0, 0)),
            pl.BlockSpec((1, channels), lambda i: (0, 0)),
        ],
        scratch_shapes=[
            pltpu.VMEM((2, 15 * channels, half), BF16),
            pltpu.VMEM((channels, half), F32),
        ],
        compiler_params=pltpu.CompilerParams(vmem_limit_bytes=VMEM_LIMIT),
        cost_estimate=pl.CostEstimate(
            flops=0, bytes_accessed=8 * 1024 * 1024, transcendentals=0
        ),
    )(*pieces, gain, spatial_weight)

    return (
        encoded[None],
        video_gradient[None],
        spatial,
        temporal,
        mix,
        gain_gradient.reshape(channels),
    )


def solution(mesh):
    return jax.shard_map(
        on_device,
        mesh=mesh,
        in_specs=(
            P("cam", "tm", "height", None, None),
            P("cam"),
            P(),
            P(),
            P(),
            P(),
            P("cam", None, ("height", "tm"), None, None),
        ),
        out_specs=(
            P("cam", None, ("height", "tm"), None, None),
            P("cam", "tm", "height", None, None),
            P(),
            P(),
            P(),
            P(),
        ),
        check_vma=False,
    )
```

```python
import functools
import math

import jax
import jax.numpy as jnp
from jax import lax
from jax.experimental import pallas as pl
from jax.experimental.pallas import tpu as pltpu
from jax.sharding import PartitionSpec as P

F32 = jnp.float32
BF16 = jnp.bfloat16
VMEM_LIMIT = 16 * 1024 * 1024
FIRST_LIMIT = 56 * 1024 * 1024


def dot(left, right):
    return jnp.dot(left, right, preferred_element_type=F32)


def dot_nt(left, right):
    return lax.dot_general(left, right, (((1,), (1,)), ((), ())), preferred_element_type=F32)


def dot_tn(left, right):
    return lax.dot_general(left, right, (((0,), (0,)), ((), ())), preferred_element_type=F32)


def from_left(cells, width):
    column = lax.broadcasted_iota(jnp.int32, cells.shape, 0) % width
    return jnp.where(column == 0, 0.0, pltpu.roll(cells, 1, 0))


def from_right(cells, width):
    column = lax.broadcasted_iota(jnp.int32, cells.shape, 0) % width
    return jnp.where(column == width - 1, 0.0, pltpu.roll(cells, cells.shape[0] - 1, 0))


def present(start, frame, frames):
    return (lax.axis_index("tm") * frames + frame >= start[0]).astype(F32)


def normalised(tile, keep):
    values = tile.astype(F32) * keep
    inverse = lax.rsqrt(jnp.mean(values * values, axis=-1, keepdims=True) + 1e-06)
    return (values * inverse, inverse)


def first_frame(shard, outs, span, total):
    return jnp.minimum(shard * outs, total - span)


def run_copies(pairs_of_refs, done):
    copies = [
        pltpu.make_async_copy(source, target, done.at[at])
        for at, (source, target) in enumerate(pairs_of_refs)
    ]
    for copy in copies:
        copy.start()
    for copy in copies:
        copy.wait()


def pieces_kernel(cotangent, *refs, outs):
    pieces, done = (refs[:-1], refs[-1])
    span = outs + 3
    me = lax.axis_index("tm")
    copies = []
    for step, piece in enumerate(pieces):
        begin = first_frame(me ^ (step + 1), outs, span, cotangent.shape[0])
        copies.append((cotangent.at[pl.ds(begin, span)], piece))
    run_copies(copies, done)


def edges_kernel(video, inner, outer, done, *, rows):
    odd = lax.axis_index("height") % 2
    run_copies(
        [
            (video.at[:, (1 - odd) * (rows - 1)], inner),
            (video.at[:, odd * (rows - 1)], outer),
        ],
        done,
    )


def first_frame(shard, outs, span, total):
    return jnp.minimum(shard * outs, total - span)


def place_halos(halo, inner, outer):
    odd = lax.axis_index("height") % 2
    halo[1 - odd] = inner[...]
    halo[odd] = outer[...]


def column_sum(cells, weight, taps, width):
    products = [
        dot(cells, jnp.concatenate([weight[i, j] for i in taps], axis=0)) for j in range(3)
    ]
    return from_left(products[0], width) + products[1] + from_right(products[2], width)


def own_kernel(
    valid_from, video, gain, weight, normed, partial, start, done, *, frames, rows, width
):
    run_copies([(valid_from, start)], done)
    block = frames * width
    for row in range(rows):
        for frame in range(frames):
            unit, _ = normalised(video[frame, row], present(start, frame, frames))
            at = row * block + frame * width
            normed[at : at + width] = (unit * gain[...]).astype(BF16)
    for row in range(rows):
        taps = [i for i in range(3) if 0 <= row + i - 1 < rows]
        cells = [normed[(row + i - 1) * block : (row + i) * block] for i in taps]
        partial[row * block : row * block + block] = column_sum(
            jnp.concatenate(cells, axis=1), weight, taps, width
        )


def front_kernel(
    valid_from, normed, partial, inner, outer, gain, weight, temporal, *refs,
    frames, rows, width, shards
):
    tall, slope, active, parts, *refs = refs
    strided, (halo, start, done, lines) = (refs[:shards], refs[shards:])
    outs = frames // 2
    plane = rows * width
    here = rows // shards
    block = frames * width

    run_copies([(valid_from, start)], done)
    place_halos(halo, inner, outer)
    tall[block : block + rows * block] = normed[...]
    for side, at in ((0, 0), (1, (rows + 1) * block)):
        for frame in range(frames):
            unit, _ = normalised(halo[side, frame], present(start, frame, frames))
            to = at + frame * width
            tall[to : to + width] = (unit * gain[...]).astype(BF16)
    for row in range(rows):
        pre = partial[row * block : row * block + block]
        if row == 0:
            pre = pre + column_sum(tall[:block], weight, [0], width)
        if row == rows - 1:
            pre = pre + column_sum(tall[(rows + 1) * block :], weight, [2], width)
        sigmoid = 1.0 / (1.0 + jnp.exp(-pre))
        slope[row * block : row * block + block] = sigmoid * (1.0 + pre * (1.0 - sigmoid))
        cells = (pre * sigmoid).astype(BF16)
        for frame in range(frames):
            at = (frame // 2) * plane + row * width
            active[frame % 2, at : at + width] = cells[frame * width : frame * width + width]
    evens = active[0]
    odds = active[1]
    carried = dot(odds, temporal[2])
    mixed = dot(odds, temporal[0]) + dot(evens, temporal[1])
    pieces = [mixed[:plane]]
    for s in range(1, outs):
        pieces.append(
            mixed[s * plane : s * plane + plane] + carried[(s - 1) * plane : s * plane]
        )
    pieces.append(carried[(outs - 1) * plane :])
    pieces = jnp.concatenate(pieces, axis=0).astype(BF16)
    parts[...] = pieces
    for frame in range(outs + 1):
        cells = pieces[frame * plane : frame * plane + plane]
        lines[:, frame] = cells.reshape(shards, here, width, 256)
    for step, piece in enumerate(strided):
        piece[...] = lines[lax.axis_index("tm") ^ step]


def middle_kernel(
    tall, slope, active, parts, temporal, mix, cotangent, *refs, frames, rows, width, shards
):
    pieces, refs = (refs[: shards - 1], refs[shards - 1 :])
    pre_gradient, inner_out, outer_out, keep, send, cot = refs
    outs = frames // 2
    plane = rows * width
    here = rows // shards
    me = lax.axis_index("tm")
    total = shards * outs
    cut = outs + 3
    skip = me * outs - first_frame(me, outs, cut, total)
    for frame in range(cut):
        here_is = (me * outs + frame < total).astype(F32)
        own = cotangent[jnp.minimum(me * outs + frame, total - 1)]
        others = [piece[jnp.minimum(frame + skip, cut - 1)] for piece in pieces]
        for step, cells in enumerate([own] + others[::-1]):
            cells = (cells.astype(F32) * here_is).astype(BF16)
            cot[frame, me ^ step] = cells.reshape(here * width, 256)

    def ahead(k, count=outs + 1):
        return cot[k : k + count].reshape(count * plane, 256)

    gradient = ahead(0).astype(F32)
    for k in range(3):
        gradient = gradient + dot_nt(ahead(k), mix[k])
    gradient = gradient.astype(BF16)
    now = gradient[: outs * plane]
    later = gradient[plane:]
    even_gradient = dot_nt(now, temporal[1])
    odd_gradient = dot_nt(now, temporal[0]) + dot_nt(later, temporal[2])
    for row in range(rows):
        for frame in range(frames):
            source = odd_gradient if frame % 2 else even_gradient
            at = (frame // 2) * plane + row * width
            to = (row * frames + frame) * width
            tile = (source[at : at + width] * slope[to : to + width]).astype(BF16)
            pre_gradient[row, frame] = tile
    side = (lax.axis_index("height") % 2) * (rows - 1)
    inner_out[...] = pre_gradient[rows - 1 - side]
    outer_out[...] = pre_gradient[side]
    first = jnp.full((256, 128), lax.axis_index("cam")) == 0

    def deliver(index, product):
        low, high = (product[:, :128], product[:, 128:])
        keep[index] = jnp.where(first, low, high)
        send[index] = jnp.where(first, high, low).astype(BF16)

    evens = active[0]
    odds = active[1]
    for k in range(3):
        deliver(k, dot_tn(parts[...], ahead(k)))
    deliver(3, dot_tn(odds, now))
    deliver(4, dot_tn(evens, now))
    deliver(5, dot_tn(odds, later))
    gradient = pre_gradient[...].reshape(-1, 256)
    exact = gradient.astype(F32)
    columns = [
        from_right(exact, width).astype(BF16), gradient, from_left(exact, width).astype(BF16)
    ]
    block = frames * width
    for i in range(3):
        cells = tall[i * block : (i + rows) * block]
        product = dot_tn(cells, jnp.concatenate(columns, axis=1))
        for j in range(3):
            deliver(6 + i * 3 + j, product[:, j * 256 : j * 256 + 256])


def core_columns():
    mine = pl.ds(pl.multiple_of(lax.axis_index("cam") * 128, 128), 128)
    other = pl.ds(pl.multiple_of((1 - lax.axis_index("cam")) * 128, 128), 128)
    return (mine, other)


def deal(axis, total, kept, sends):
    me = lax.axis_index(axis)
    kept[...] = total(me)
    for step, send in enumerate(sends):
        send[...] = total(me ^ (step + 1)).astype(BF16)


def first_sum_kernel(keep, got, kept, *sends):
    deal("height", lambda at: keep[at] + got[at].astype(F32), kept, sends)


def second_sum_kernel(kept_in, *refs):
    count = kept_in.shape[0]
    received = refs[: len(refs) - count]
    kept, *sends = refs[len(refs) - count :]

    def total(at):
        value = kept_in[at]
        for piece in received:
            value = value + piece[at].astype(F32)
        return value

    deal("tm", total, kept, sends)


def last_sum_kernel(inner, outer, kept, *refs):
    del inner, outer
    value = kept[...]
    for piece in refs[:-1]:
        value = value + piece[...].astype(F32)
    refs[-1][...] = value.astype(BF16)


def assemble_kernel(*refs):
    for step, piece in enumerate(reversed(refs[:-1])):
        refs[-1][lax.axis_index("tm") ^ step] = piece[...]


def input_kernel(
    valid_from, video, pre_gradient, inner, outer, gain, weight, out, tall, halo, start, done,
    *, frames, rows, width
):
    run_copies([(valid_from, start)], done)
    place_halos(halo, inner, outer)
    block = frames * width
    for row in range(-1, rows + 1):
        if row < 0:
            cells = halo[0]
        elif row == rows:
            cells = halo[1]
        else:
            cells = pre_gradient[row]
        cells = cells.reshape(block, 256)
        for tap in range(3):
            target = row - 1 + tap
            if 0 <= target < rows:
                tall[target * block : target * block + block, tap * 256 : tap * 256 + 256] = cells
    for row in range(rows):
        cells = tall[row * block : row * block + block]
        taps = [
            dot_nt(cells, jnp.concatenate([weight[0, j], weight[1, j], weight[2, j]], axis=1))
            for j in range(3)
        ]
        gradient = from_right(taps[0], width) + taps[1] + from_left(taps[2], width)
        gradient = gradient * gain[...]
        for frame in range(frames):
            keep = present(start, frame, frames)
            unit, inverse = normalised(video[frame, row], keep)
            tile = gradient[frame * width : frame * width + width]
            mean = jnp.mean(tile * unit, axis=-1, keepdims=True)
            out[frame, row] = (inverse * (tile - unit * mean) * keep).astype(BF16)


def encode_kernel(mix, *refs, width, shards):
    pieces, (out, line, strided) = (refs[:shards], refs[shards:])
    for step, piece in enumerate(pieces):
        strided[lax.axis_index("tm") ^ step] = piece[...]
    parts, here = strided.shape[1:3]
    outs = parts - 1
    plane = here * width
    total = shards * outs
    for frame in range(total):
        shard, part = (frame // outs, frame % outs)
        cells = strided[shard, part].reshape(plane, 256)
        if part == 0 and shard > 0:
            carried = strided[shard - 1, outs].reshape(plane, 256)
            cells = (cells.astype(F32) + carried.astype(F32)).astype(BF16)
        line[(frame + 2) * plane : (frame + 3) * plane] = cells
    line[0 : 2 * plane] = jnp.zeros((2 * plane, 256), BF16)
    span = total * plane
    result = line[2 * plane : 2 * plane + span].astype(F32)
    for k in range(3):
        result = result + dot(line[(2 - k) * plane : (2 - k) * plane + span], mix[k])
    out[...] = result.astype(BF16).reshape(out.shape)


def finish_kernel(*refs, scale, parts):
    pieces = refs[: 2 * parts]
    gain, weight, spatial, temporal, mix, gain_out, whole, total = refs[2 * parts :]
    step = pl.program_id(0)
    size = whole.shape[1] // parts

    @pl.when(step == 0)
    def _():
        for core in range(2):
            for part in range(parts):
                at = pl.multiple_of((lax.axis_index("height") ^ part) * size, size)
                whole[core, pl.ds(at, size)] = pieces[core * parts + part][...]
        total[...] = jnp.zeros_like(total)

    for core, columns in enumerate(core_columns()):

        def matrix(index):
            at = pl.multiple_of(index * 256, 256)
            return whole[core, pl.ds(at, 256)].astype(F32) * scale

        mix[0, :, columns] = matrix(step)
        temporal[0, :, columns] = matrix(step + 3)
        for j in range(3):
            piece = matrix(step * 3 + (6 + j))
            spatial[0, j, :, columns] = piece
            total[...] += piece * weight[step, j, :, columns].astype(F32)

    @pl.when(step == 2)
    def _():
        gain_out[...] = jnp.sum(total[...].T, axis=0, keepdims=True) / gain[...]


def call(kernel, outs, scratch=(), flops=0, moved=0, space=pltpu.VMEM, limit=VMEM_LIMIT):
    where = pl.BlockSpec(memory_space=space)

    def run(*operands):
        results = pl.pallas_call(
            kernel,
            out_shape=[jax.ShapeDtypeStruct(shape, dtype) for shape, dtype in outs],
            in_specs=[
                pl.BlockSpec(memory_space=pltpu.HBM) if a.dtype == jnp.int32 else where
                for a in operands
            ],
            out_specs=[where] * len(outs),
            scratch_shapes=list(scratch),
            compiler_params=pltpu.CompilerParams(vmem_limit_bytes=limit),
            cost_estimate=pl.CostEstimate(flops=flops, bytes_accessed=moved, transcendentals=0),
        )(*operands)
        return list(results)

    return run


def neighbours(inner, outer, axis):
    size = lax.axis_size(axis)
    links = [(i, i + 1) for i in range(1, size - 1, 2)]
    links = links + [(j, i) for i, j in links]
    return (pair(inner, axis, 1), lax.ppermute(outer, axis, links))


def pair(array, axis, step):
    return lax.ppermute(array, axis, [(i, i ^ step) for i in range(lax.axis_size(axis))])


def pairs(arrays, axis):
    return [pair(array, axis, step + 1) for step, array in enumerate(arrays)]


def together(*values):
    return lax.optimization_barrier(values)


def on_device(
    video_clip, valid_from, norm_gain, spatial_weight, temporal_weight, mix_weight, cotangent
):
    video = video_clip[0]
    frames, rows, width, channels = video.shape
    outs = frames // 2
    shards = lax.axis_size("tm")
    lines = lax.axis_size("height")
    here = rows // shards
    cells = frames * rows * width
    sizes = dict(frames=frames, rows=rows, width=width)
    gain = norm_gain.reshape(1, channels)
    edge = ((frames, width, channels), BF16)
    halo = pltpu.VMEM((2, frames, width, channels), BF16)

    scalar = [pltpu.SMEM((1,), jnp.int32), pltpu.SemaphoreType.DMA((1,))]
    pieces = call(
        functools.partial(pieces_kernel, outs=outs),
        [((outs + 3, here, width, channels), BF16)] * (shards - 1),
        [pltpu.SemaphoreType.DMA((shards - 1,))],
        moved=1024 * 1024,
        space=pltpu.HBM,
        limit=FIRST_LIMIT,
    )(cotangent[0])
    *pieces, edges = together(*pieces, video)
    pieces = pairs(pieces, "tm")
    inner, outer = call(
        functools.partial(edges_kernel, rows=rows),
        [edge, edge],
        [pltpu.SemaphoreType.DMA((2,))],
        moved=512 * 1024,
        space=pltpu.HBM,
    )(edges)
    inner, outer = neighbours(inner, outer, "height")

    normed, partial = call(
        functools.partial(own_kernel, **sizes),
        [((cells, channels), BF16), ((cells, channels), F32)],
        scalar,
        flops=18 * cells * channels * channels,
        moved=4 * 1024 * 1024,
    )(valid_from, video, gain, spatial_weight)

    tall, slope, active, parts, *strided = call(
        functools.partial(front_kernel, **sizes, shards=shards),
        [
            ((cells + 2 * frames * width, channels), BF16),
            ((cells, channels), F32),
            ((2, cells // 2, channels), BF16),
            (((outs + 1) * rows * width, channels), BF16),
        ]
        + [((outs + 1, here, width, channels), BF16)] * shards,
        [halo, *scalar, pltpu.VMEM((shards, outs + 1, here, width, channels), BF16)],
    )(valid_from, normed, partial, inner, outer, gain, spatial_weight, temporal_weight)

    pre_gradient, inner, outer, keep, send = call(
        functools.partial(middle_kernel, **sizes, shards=shards),
        [
            ((rows, frames, width, channels), BF16),
            edge,
            edge,
            ((15, channels, channels // 2), F32),
            ((15, channels, channels // 2), BF16),
        ],
        [pltpu.VMEM((outs + 3, shards, here * width, channels), BF16)],
        flops=36 * cells * channels * channels,
        moved=12 * 1024 * 1024,
    )(
        tall, slope, active, parts, temporal_weight, mix_weight, cotangent[0],
        *reversed(pieces),
    )

    large = 15 * channels // lines
    small = large // shards
    half = channels // 2
    got = pair(send, "cam", 1)
    kept, *sends = call(
        first_sum_kernel,
        [((large, half), F32)] + [((large, half), BF16)] * (lines - 1),
        moved=8 * 1024 * 1024,
    )(keep.reshape(lines, large, half), got.reshape(lines, large, half))
    received = pairs(sends, "height")
    middle = shards // 2
    strided = [strided[0]] + pairs(strided[1:], "tm")
    kept, strided[middle] = together(kept, strided[middle])
    kept, *sends = call(
        second_sum_kernel,
        [((small, half), F32)] + [((small, half), BF16)] * (shards - 1),
        moved=2 * 1024 * 1024,
    )(*[a.reshape(shards, small, half) for a in [kept] + received[::-1]])
    kept, inner, outer = together(kept, inner, outer)
    received = pairs(sends, "tm")
    inner, outer = neighbours(inner, outer, "height")
    (total,) = call(last_sum_kernel, [((small, half), BF16)], moved=1024 * 1024)(
        inner, outer, kept, *received[::-1]
    )
    received = pairs([total] * (shards - 1), "tm")
    (total,) = call(assemble_kernel, [((shards, small, half), BF16)], moved=1024 * 1024)(
        *received[::-1], total
    )
    total = total.reshape(large, half)
    pieces = [total] + pairs([total] * (lines - 1), "height")
    (video_gradient,) = call(
        functools.partial(input_kernel, **sizes),
        [((frames, rows, width, channels), BF16)],
        [pltpu.VMEM((cells, 3 * channels), BF16), halo] + scalar,
        flops=18 * cells * channels * channels,
        moved=4 * 1024 * 1024,
    )(valid_from, video, pre_gradient, inner, outer, gain, spatial_weight)
    (encoded,) = call(
        functools.partial(encode_kernel, width=width, shards=shards),
        [((shards * outs, here, width, channels), BF16)],
        [
            pltpu.VMEM(((shards * outs + 2) * here * width, channels), BF16),
            pltpu.VMEM((shards, outs + 1, here, width, channels), BF16),
        ],
        flops=3 * cells * channels * channels,
        moved=2 * 1024 * 1024,
    )(mix_weight, *strided)
    pieces[-1], video_gradient, encoded = together(pieces[-1], video_gradient, encoded)
    pieces = pieces + [pair(piece, "cam", 1) for piece in pieces]

    cell_count = cells * lax.axis_size("cam") * shards * lines
    vmem = pl.BlockSpec(memory_space=pltpu.VMEM)
    spatial, temporal, mix, gain_gradient = pl.pallas_call(
        functools.partial(finish_kernel, scale=1.0 / math.sqrt(cell_count), parts=lines),
        grid=(3,),
        out_shape=[
            jax.ShapeDtypeStruct(spatial_weight.shape, F32),
            jax.ShapeDtypeStruct(temporal_weight.shape, F32),
            jax.ShapeDtypeStruct(mix_weight.shape, F32),
            jax.ShapeDtypeStruct((1, channels), F32),
        ],
        in_specs=[vmem] * (2 * lines + 2),
        out_specs=[
            pl.BlockSpec((1, 3, channels, channels), lambda i: (i, 0, 0, 0)),
            pl.BlockSpec((1, channels, channels), lambda i: (i, 0, 0)),
            pl.BlockSpec((1, channels, channels), lambda i: (i, 0, 0)),
            pl.BlockSpec((1, channels), lambda i: (0, 0)),
        ],
        scratch_shapes=[
            pltpu.VMEM((2, 15 * channels, half), BF16),
            pltpu.VMEM((channels, half), F32),
        ],
        compiler_params=pltpu.CompilerParams(vmem_limit_bytes=VMEM_LIMIT),
        cost_estimate=pl.CostEstimate(
            flops=0, bytes_accessed=8 * 1024 * 1024, transcendentals=0
        ),
    )(*pieces, gain, spatial_weight)

    return (
        encoded[None],
        video_gradient[None],
        spatial,
        temporal,
        mix,
        gain_gradient.reshape(channels),
    )


def solution(mesh):
    return jax.shard_map(
        on_device,
        mesh=mesh,
        in_specs=(
            P("cam", "tm", "height", None, None),
            P("cam"),
            P(),
            P(),
            P(),
            P(),
            P("cam", None, ("height", "tm"), None, None),
        ),
        out_specs=(
            P("cam", None, ("height", "tm"), None, None),
            P("cam", "tm", "height", None, None),
            P(),
            P(),
            P(),
            P(),
        ),
        check_vma=False,
    )
```

```python
import functools
import math

import jax
import jax.numpy as jnp
from jax import lax
from jax.experimental import pallas as pl
from jax.experimental.pallas import tpu as pltpu
from jax.sharding import PartitionSpec as P

F32 = jnp.float32
BF16 = jnp.bfloat16
VMEM_LIMIT = 16 * 1024 * 1024


def dot(left, right):
    return jnp.dot(left, right, preferred_element_type=F32)


def dot_nt(left, right):
    return lax.dot_general(left, right, (((1,), (1,)), ((), ())), preferred_element_type=F32)


def dot_tn(left, right):
    return lax.dot_general(left, right, (((0,), (0,)), ((), ())), preferred_element_type=F32)


def from_left(cells, width):
    column = lax.broadcasted_iota(jnp.int32, cells.shape, 0) % width
    return jnp.where(column == 0, 0.0, pltpu.roll(cells, 1, 0))


def from_right(cells, width):
    column = lax.broadcasted_iota(jnp.int32, cells.shape, 0) % width
    return jnp.where(column == width - 1, 0.0, pltpu.roll(cells, cells.shape[0] - 1, 0))


def present(start, frame, frames):
    return (lax.axis_index("tm") * frames + frame >= start[0]).astype(F32)


def normalised(tile, keep):
    values = tile.astype(F32) * keep
    inverse = lax.rsqrt(jnp.mean(values * values, axis=-1, keepdims=True) + 1e-06)
    return (values * inverse, inverse)


def first_frame(shard, outs, span, total):
    return jnp.minimum(shard * outs, total - span)


def run_copies(pairs_of_refs, done):
    copies = [
        pltpu.make_async_copy(source, target, done.at[at])
        for at, (source, target) in enumerate(pairs_of_refs)
    ]
    for copy in copies:
        copy.start()
    for copy in copies:
        copy.wait()


def pieces_kernel(cotangent, *refs, outs):
    pieces, done = (refs[:-1], refs[-1])
    span = outs + 3
    me = lax.axis_index("tm")
    copies = []
    for step, piece in enumerate(pieces):
        begin = first_frame(me ^ (step + 1), outs, span, cotangent.shape[0])
        copies.append((cotangent.at[pl.ds(begin, span)], piece))
    run_copies(copies, done)


def edges_kernel(source, inner, outer, done, *, rows, frames_first):
    odd = lax.axis_index("height") % 2

    def row(at):
        return source.at[:, at] if frames_first else source.at[at]

    run_copies(
        [(row((1 - odd) * (rows - 1)), inner), (row(odd * (rows - 1)), outer)], done
    )


def first_frame(shard, outs, span, total):
    return jnp.minimum(shard * outs, total - span)


def place_halos(halo, inner, outer):
    odd = lax.axis_index("height") % 2
    halo[1 - odd] = inner[...]
    halo[odd] = outer[...]


def column_sum(cells, weight, taps, width):
    products = [
        dot(cells, jnp.concatenate([weight[i, j] for i in taps], axis=0)) for j in range(3)
    ]
    return from_left(products[0], width) + products[1] + from_right(products[2], width)


def halo_kernel(inner, outer, halo):
    place_halos(halo, inner, outer)


def own_kernel(
    valid_from, video, gain, weight, normed, partial, start, done, *, frames, rows, width
):
    run_copies([(valid_from, start)], done)
    block = frames * width
    for row in range(rows):
        for frame in range(frames):
            unit, _ = normalised(video[frame, row], present(start, frame, frames))
            at = row * block + frame * width
            normed[at : at + width] = (unit * gain[...]).astype(BF16)
    for row in range(rows):
        taps = [i for i in range(3) if 0 <= row + i - 1 < rows]
        cells = [normed[(row + i - 1) * block : (row + i) * block] for i in taps]
        partial[row * block : row * block + block] = column_sum(
            jnp.concatenate(cells, axis=1), weight, taps, width
        )


def front_kernel(
    valid_from, normed, partial, inner, outer, gain, weight, temporal, *refs,
    frames, rows, width, shards
):
    tall, slope, active, parts, *refs = refs
    strided, (halo, start, done, lines) = (refs[:shards], refs[shards:])
    outs = frames // 2
    plane = rows * width
    here = rows // shards
    block = frames * width

    run_copies([(valid_from, start)], done)
    place_halos(halo, inner, outer)
    tall[block : block + rows * block] = normed[...]
    for side, at in ((0, 0), (1, (rows + 1) * block)):
        for frame in range(frames):
            unit, _ = normalised(halo[side, frame], present(start, frame, frames))
            to = at + frame * width
            tall[to : to + width] = (unit * gain[...]).astype(BF16)
    for row in range(rows):
        pre = partial[row * block : row * block + block]
        if row == 0:
            pre = pre + column_sum(tall[:block], weight, [0], width)
        if row == rows - 1:
            pre = pre + column_sum(tall[(rows + 1) * block :], weight, [2], width)
        sigmoid = 1.0 / (1.0 + jnp.exp(-pre))
        slope[row * block : row * block + block] = sigmoid * (1.0 + pre * (1.0 - sigmoid))
        cells = (pre * sigmoid).astype(BF16)
        for frame in range(frames):
            at = (frame // 2) * plane + row * width
            active[frame % 2, at : at + width] = cells[frame * width : frame * width + width]
    evens = active[0]
    odds = active[1]
    carried = dot(odds, temporal[2])
    mixed = dot(odds, temporal[0]) + dot(evens, temporal[1])
    pieces = [mixed[:plane]]
    for s in range(1, outs):
        pieces.append(
            mixed[s * plane : s * plane + plane] + carried[(s - 1) * plane : s * plane]
        )
    pieces.append(carried[(outs - 1) * plane :])
    pieces = jnp.concatenate(pieces, axis=0).astype(BF16)
    parts[...] = pieces
    for frame in range(outs + 1):
        cells = pieces[frame * plane : frame * plane + plane]
        lines[:, frame] = cells.reshape(shards, here, width, 256)
    for step, piece in enumerate(strided):
        piece[...] = lines[lax.axis_index("tm") ^ step]


def middle_kernel(
    tall, slope, active, parts, temporal, mix, cotangent, *refs, frames, rows, width, shards
):
    pieces, refs = (refs[: shards - 1], refs[shards - 1 :])
    pre_gradient, keep, send, cot = refs
    outs = frames // 2
    plane = rows * width
    here = rows // shards
    me = lax.axis_index("tm")
    total = shards * outs
    cut = outs + 3
    skip = me * outs - first_frame(me, outs, cut, total)
    for frame in range(cut):
        here_is = (me * outs + frame < total).astype(F32)
        own = cotangent[jnp.minimum(me * outs + frame, total - 1)]
        others = [piece[jnp.minimum(frame + skip, cut - 1)] for piece in pieces]
        for step, cells in enumerate([own] + others[::-1]):
            cells = (cells.astype(F32) * here_is).astype(BF16)
            cot[frame, me ^ step] = cells.reshape(here * width, 256)

    def ahead(k, count=outs + 1):
        return cot[k : k + count].reshape(count * plane, 256)

    gradient = ahead(0).astype(F32)
    for k in range(3):
        gradient = gradient + dot_nt(ahead(k), mix[k])
    gradient = gradient.astype(BF16)
    now = gradient[: outs * plane]
    later = gradient[plane:]
    even_gradient = dot_nt(now, temporal[1])
    odd_gradient = dot_nt(now, temporal[0]) + dot_nt(later, temporal[2])
    for row in range(rows):
        for frame in range(frames):
            source = odd_gradient if frame % 2 else even_gradient
            at = (frame // 2) * plane + row * width
            to = (row * frames + frame) * width
            tile = (source[at : at + width] * slope[to : to + width]).astype(BF16)
            pre_gradient[row, frame] = tile
    first = jnp.full((256, 128), lax.axis_index("cam")) == 0

    def deliver(index, product):
        low, high = (product[:, :128], product[:, 128:])
        keep[index] = jnp.where(first, low, high)
        send[index] = jnp.where(first, high, low).astype(BF16)

    evens = active[0]
    odds = active[1]
    for k in range(3):
        deliver(k, dot_tn(parts[...], ahead(k)))
    deliver(3, dot_tn(odds, now))
    deliver(4, dot_tn(evens, now))
    deliver(5, dot_tn(odds, later))
    gradient = pre_gradient[...].reshape(-1, 256)
    exact = gradient.astype(F32)
    columns = [
        from_right(exact, width).astype(BF16), gradient, from_left(exact, width).astype(BF16)
    ]
    block = frames * width
    for i in range(3):
        cells = tall[i * block : (i + rows) * block]
        product = dot_tn(cells, jnp.concatenate(columns, axis=1))
        for j in range(3):
            deliver(6 + i * 3 + j, product[:, j * 256 : j * 256 + 256])


def core_columns():
    mine = pl.ds(pl.multiple_of(lax.axis_index("cam") * 128, 128), 128)
    other = pl.ds(pl.multiple_of((1 - lax.axis_index("cam")) * 128, 128), 128)
    return (mine, other)


def deal(axis, total, kept, sends):
    me = lax.axis_index(axis)
    kept[...] = total(me)
    for step, send in enumerate(sends):
        send[...] = total(me ^ (step + 1)).astype(BF16)


def first_sum_kernel(keep, got, kept, *sends):
    deal("height", lambda at: keep[at] + got[at].astype(F32), kept, sends)


def second_sum_kernel(kept_in, *refs):
    count = kept_in.shape[0]
    received = refs[: len(refs) - count]
    kept, *sends = refs[len(refs) - count :]

    def total(at):
        value = kept_in[at]
        for piece in received:
            value = value + piece[at].astype(F32)
        return value

    deal("tm", total, kept, sends)


def last_sum_kernel(halo, kept, *refs):
    del halo
    value = kept[...]
    for piece in refs[:-1]:
        value = value + piece[...].astype(F32)
    refs[-1][...] = value.astype(BF16)


def assemble_kernel(*refs):
    for step, piece in enumerate(reversed(refs[:-1])):
        refs[-1][lax.axis_index("tm") ^ step] = piece[...]


def input_kernel(
    valid_from, video, pre_gradient, halo, gain, weight, out, tall, start, done,
    *, frames, rows, width
):
    run_copies([(valid_from, start)], done)
    block = frames * width
    for row in range(-1, rows + 1):
        if row < 0:
            cells = halo[0]
        elif row == rows:
            cells = halo[1]
        else:
            cells = pre_gradient[row]
        cells = cells.reshape(block, 256)
        for tap in range(3):
            target = row - 1 + tap
            if 0 <= target < rows:
                tall[target * block : target * block + block, tap * 256 : tap * 256 + 256] = cells
    for row in range(rows):
        cells = tall[row * block : row * block + block]
        taps = [
            dot_nt(cells, jnp.concatenate([weight[0, j], weight[1, j], weight[2, j]], axis=1))
            for j in range(3)
        ]
        gradient = from_right(taps[0], width) + taps[1] + from_left(taps[2], width)
        gradient = gradient * gain[...]
        for frame in range(frames):
            keep = present(start, frame, frames)
            unit, inverse = normalised(video[frame, row], keep)
            tile = gradient[frame * width : frame * width + width]
            mean = jnp.mean(tile * unit, axis=-1, keepdims=True)
            out[frame, row] = (inverse * (tile - unit * mean) * keep).astype(BF16)


def encode_kernel(mix, *refs, width, shards):
    pieces, (out, line, strided) = (refs[:shards], refs[shards:])
    for step, piece in enumerate(pieces):
        strided[lax.axis_index("tm") ^ step] = piece[...]
    parts, here = strided.shape[1:3]
    outs = parts - 1
    plane = here * width
    total = shards * outs
    for frame in range(total):
        shard, part = (frame // outs, frame % outs)
        cells = strided[shard, part].reshape(plane, 256)
        if part == 0 and shard > 0:
            carried = strided[shard - 1, outs].reshape(plane, 256)
            cells = (cells.astype(F32) + carried.astype(F32)).astype(BF16)
        line[(frame + 2) * plane : (frame + 3) * plane] = cells
    line[0 : 2 * plane] = jnp.zeros((2 * plane, 256), BF16)
    span = total * plane
    result = line[2 * plane : 2 * plane + span].astype(F32)
    for k in range(3):
        result = result + dot(line[(2 - k) * plane : (2 - k) * plane + span], mix[k])
    out[...] = result.astype(BF16).reshape(out.shape)


def finish_kernel(*refs, scale, parts):
    pieces = refs[: 2 * parts]
    gain, weight, spatial, temporal, mix, gain_out, whole, total = refs[2 * parts :]
    step = pl.program_id(0)
    size = whole.shape[1] // parts

    @pl.when(step == 0)
    def _():
        for core in range(2):
            for part in range(parts):
                at = pl.multiple_of((lax.axis_index("height") ^ part) * size, size)
                whole[core, pl.ds(at, size)] = pieces[core * parts + part][...]
        total[...] = jnp.zeros_like(total)

    for core, columns in enumerate(core_columns()):

        def matrix(index):
            at = pl.multiple_of(index * 256, 256)
            return whole[core, pl.ds(at, 256)].astype(F32) * scale

        mix[0, :, columns] = matrix(step)
        temporal[0, :, columns] = matrix(step + 3)
        for j in range(3):
            piece = matrix(step * 3 + (6 + j))
            spatial[0, j, :, columns] = piece
            total[...] += piece * weight[step, j, :, columns].astype(F32)

    @pl.when(step == 2)
    def _():
        gain_out[...] = jnp.sum(total[...].T, axis=0, keepdims=True) / gain[...]


def call(kernel, outs, scratch=(), flops=0, moved=0):
    where = pl.BlockSpec(memory_space=pltpu.VMEM)

    def run(*operands):
        results = pl.pallas_call(
            kernel,
            out_shape=[jax.ShapeDtypeStruct(shape, dtype) for shape, dtype in outs],
            in_specs=[
                pl.BlockSpec(memory_space=pltpu.HBM) if a.dtype == jnp.int32 else where
                for a in operands
            ],
            out_specs=[where] * len(outs),
            scratch_shapes=list(scratch),
            compiler_params=pltpu.CompilerParams(vmem_limit_bytes=VMEM_LIMIT),
            cost_estimate=pl.CostEstimate(flops=flops, bytes_accessed=moved, transcendentals=0),
        )(*operands)
        return list(results)

    return run


def neighbours(inner, outer, axis):
    size = lax.axis_size(axis)
    links = [(i, i + 1) for i in range(1, size - 1, 2)]
    links = links + [(j, i) for i, j in links]
    return (pair(inner, axis, 1), lax.ppermute(outer, axis, links))


def pair(array, axis, step):
    return lax.ppermute(array, axis, [(i, i ^ step) for i in range(lax.axis_size(axis))])


def pairs(arrays, axis):
    return [pair(array, axis, step + 1) for step, array in enumerate(arrays)]


def together(*values):
    return lax.optimization_barrier(values)


def on_device(
    video_clip, valid_from, norm_gain, spatial_weight, temporal_weight, mix_weight, cotangent
):
    video = video_clip[0]
    frames, rows, width, channels = video.shape
    outs = frames // 2
    shards = lax.axis_size("tm")
    lines = lax.axis_size("height")
    here = rows // shards
    cells = frames * rows * width
    sizes = dict(frames=frames, rows=rows, width=width)
    gain = norm_gain.reshape(1, channels)
    edge = ((frames, width, channels), BF16)
    halo = pltpu.VMEM((2, frames, width, channels), BF16)

    scalar = [pltpu.SMEM((1,), jnp.int32), pltpu.SemaphoreType.DMA((1,))]
    pieces = call(
        functools.partial(pieces_kernel, outs=outs),
        [((outs + 3, here, width, channels), BF16)] * (shards - 1),
        [pltpu.SemaphoreType.DMA((shards - 1,))],
        moved=1024 * 1024,
    )(cotangent[0])
    *pieces, edges = together(*pieces, video)
    pieces = pairs(pieces, "tm")
    def edges_of(source, frames_first):
        return call(
            functools.partial(edges_kernel, rows=rows, frames_first=frames_first),
            [edge, edge],
            [pltpu.SemaphoreType.DMA((2,))],
            moved=512 * 1024,
        )(source)

    inner, outer = edges_of(edges, True)
    inner, outer = neighbours(inner, outer, "height")

    normed, partial = call(
        functools.partial(own_kernel, **sizes),
        [((cells, channels), BF16), ((cells, channels), F32)],
        scalar,
        flops=18 * cells * channels * channels,
        moved=4 * 1024 * 1024,
    )(valid_from, video, gain, spatial_weight)

    tall, slope, active, parts, *strided = call(
        functools.partial(front_kernel, **sizes, shards=shards),
        [
            ((cells + 2 * frames * width, channels), BF16),
            ((cells, channels), F32),
            ((2, cells // 2, channels), BF16),
            (((outs + 1) * rows * width, channels), BF16),
        ]
        + [((outs + 1, here, width, channels), BF16)] * shards,
        [halo, *scalar, pltpu.VMEM((shards, outs + 1, here, width, channels), BF16)],
    )(valid_from, normed, partial, inner, outer, gain, spatial_weight, temporal_weight)

    pre_gradient, keep, send = call(
        functools.partial(middle_kernel, **sizes, shards=shards),
        [
            ((rows, frames, width, channels), BF16),
            ((15, channels, channels // 2), F32),
            ((15, channels, channels // 2), BF16),
        ],
        [pltpu.VMEM((outs + 3, shards, here * width, channels), BF16)],
        flops=36 * cells * channels * channels,
        moved=12 * 1024 * 1024,
    )(
        tall, slope, active, parts, temporal_weight, mix_weight, cotangent[0],
        *reversed(pieces),
    )

    large = 15 * channels // lines
    small = large // shards
    half = channels // 2
    got = pair(send, "cam", 1)
    kept, *sends = call(
        first_sum_kernel,
        [((large, half), F32)] + [((large, half), BF16)] * (lines - 1),
        moved=8 * 1024 * 1024,
    )(keep.reshape(lines, large, half), got.reshape(lines, large, half))
    received = pairs(sends, "height")
    middle = shards // 2
    strided = [strided[0]] + pairs(strided[1:], "tm")
    kept, strided[middle] = together(kept, strided[middle])
    kept, *sends = call(
        second_sum_kernel,
        [((small, half), F32)] + [((small, half), BF16)] * (shards - 1),
        moved=2 * 1024 * 1024,
    )(*[a.reshape(shards, small, half) for a in [kept] + received[::-1]])
    kept, pre_gradient = together(kept, pre_gradient)
    received = pairs(sends, "tm")
    inner, outer = edges_of(pre_gradient, False)
    inner, outer = neighbours(inner, outer, "height")
    (halo_rows,) = call(halo_kernel, [((2, frames, width, channels), BF16)])(inner, outer)
    (total,) = call(last_sum_kernel, [((small, half), BF16)], moved=1024 * 1024)(
        halo_rows, kept, *received[::-1]
    )
    received = pairs([total] * (shards - 1), "tm")
    (video_gradient,) = call(
        functools.partial(input_kernel, **sizes),
        [((frames, rows, width, channels), BF16)],
        [pltpu.VMEM((cells, 3 * channels), BF16)] + scalar,
        flops=18 * cells * channels * channels,
        moved=4 * 1024 * 1024,
    )(valid_from, video, pre_gradient, halo_rows, gain, spatial_weight)
    total, video_gradient = together(total, video_gradient)
    (total,) = call(assemble_kernel, [((shards, small, half), BF16)], moved=1024 * 1024)(
        *received[::-1], total
    )
    total = total.reshape(large, half)
    pieces = [total] + pairs([total] * (lines - 1), "height")
    (encoded,) = call(
        functools.partial(encode_kernel, width=width, shards=shards),
        [((shards * outs, here, width, channels), BF16)],
        [
            pltpu.VMEM(((shards * outs + 2) * here * width, channels), BF16),
            pltpu.VMEM((shards, outs + 1, here, width, channels), BF16),
        ],
        flops=3 * cells * channels * channels,
        moved=2 * 1024 * 1024,
    )(mix_weight, *strided)
    pieces[-1], encoded = together(pieces[-1], encoded)
    pieces = pieces + [pair(piece, "cam", 1) for piece in pieces]

    cell_count = cells * lax.axis_size("cam") * shards * lines
    vmem = pl.BlockSpec(memory_space=pltpu.VMEM)
    spatial, temporal, mix, gain_gradient = pl.pallas_call(
        functools.partial(finish_kernel, scale=1.0 / math.sqrt(cell_count), parts=lines),
        grid=(3,),
        out_shape=[
            jax.ShapeDtypeStruct(spatial_weight.shape, F32),
            jax.ShapeDtypeStruct(temporal_weight.shape, F32),
            jax.ShapeDtypeStruct(mix_weight.shape, F32),
            jax.ShapeDtypeStruct((1, channels), F32),
        ],
        in_specs=[vmem] * (2 * lines + 2),
        out_specs=[
            pl.BlockSpec((1, 3, channels, channels), lambda i: (i, 0, 0, 0)),
            pl.BlockSpec((1, channels, channels), lambda i: (i, 0, 0)),
            pl.BlockSpec((1, channels, channels), lambda i: (i, 0, 0)),
            pl.BlockSpec((1, channels), lambda i: (0, 0)),
        ],
        scratch_shapes=[
            pltpu.VMEM((2, 15 * channels, half), BF16),
            pltpu.VMEM((channels, half), F32),
        ],
        compiler_params=pltpu.CompilerParams(vmem_limit_bytes=VMEM_LIMIT),
        cost_estimate=pl.CostEstimate(
            flops=0, bytes_accessed=8 * 1024 * 1024, transcendentals=0
        ),
    )(*pieces, gain, spatial_weight)

    return (
        encoded[None],
        video_gradient[None],
        spatial,
        temporal,
        mix,
        gain_gradient.reshape(channels),
    )


def solution(mesh):
    return jax.shard_map(
        on_device,
        mesh=mesh,
        in_specs=(
            P("cam", "tm", "height", None, None),
            P("cam"),
            P(),
            P(),
            P(),
            P(),
            P("cam", None, ("height", "tm"), None, None),
        ),
        out_specs=(
            P("cam", None, ("height", "tm"), None, None),
            P("cam", "tm", "height", None, None),
            P(),
            P(),
            P(),
            P(),
        ),
        check_vma=False,
    )
```

```python
import functools
import math

import jax
import jax.numpy as jnp
from jax import lax
from jax.experimental import pallas as pl
from jax.experimental.pallas import tpu as pltpu
from jax.sharding import PartitionSpec as P

F32 = jnp.float32
BF16 = jnp.bfloat16
VMEM_LIMIT = 16 * 1024 * 1024


def dot(left, right):
    return jnp.dot(left, right, preferred_element_type=F32)


def dot_nt(left, right):
    return lax.dot_general(left, right, (((1,), (1,)), ((), ())), preferred_element_type=F32)


def dot_tn(left, right):
    return lax.dot_general(left, right, (((0,), (0,)), ((), ())), preferred_element_type=F32)


def from_left(cells, width):
    column = lax.broadcasted_iota(jnp.int32, cells.shape, 0) % width
    return jnp.where(column == 0, 0.0, pltpu.roll(cells, 1, 0))


def from_right(cells, width):
    column = lax.broadcasted_iota(jnp.int32, cells.shape, 0) % width
    return jnp.where(column == width - 1, 0.0, pltpu.roll(cells, cells.shape[0] - 1, 0))


def present(start, frame, frames):
    return (lax.axis_index("tm") * frames + frame >= start[0]).astype(F32)


def normalised(tile, keep):
    values = tile.astype(F32) * keep
    inverse = lax.rsqrt(jnp.mean(values * values, axis=-1, keepdims=True) + 1e-06)
    return (values * inverse, inverse)


def first_frame(shard, outs, span, total):
    return jnp.minimum(shard * outs, total - span)


def run_copies(pairs_of_refs, done):
    copies = [
        pltpu.make_async_copy(source, target, done.at[at])
        for at, (source, target) in enumerate(pairs_of_refs)
    ]
    for copy in copies:
        copy.start()
    for copy in copies:
        copy.wait()


def pieces_kernel(cotangent, *refs, outs):
    pieces, done = (refs[:-1], refs[-1])
    span = outs + 3
    me = lax.axis_index("tm")
    copies = []
    for step, piece in enumerate(pieces):
        begin = first_frame(me ^ (step + 1), outs, span, cotangent.shape[0])
        copies.append((cotangent.at[pl.ds(begin, span)], piece))
    run_copies(copies, done)


def edges_kernel(video, inner, outer, done, *, rows):
    odd = lax.axis_index("height") % 2
    run_copies(
        [
            (video.at[:, (1 - odd) * (rows - 1)], inner),
            (video.at[:, odd * (rows - 1)], outer),
        ],
        done,
    )


def first_frame(shard, outs, span, total):
    return jnp.minimum(shard * outs, total - span)


def place_halos(halo, inner, outer):
    odd = lax.axis_index("height") % 2
    halo[1 - odd] = inner[...]
    halo[odd] = outer[...]


def column_sum(cells, weight, taps, width):
    products = [
        dot(cells, jnp.concatenate([weight[i, j] for i in taps], axis=0)) for j in range(3)
    ]
    return from_left(products[0], width) + products[1] + from_right(products[2], width)


def halo_kernel(inner, outer, halo):
    place_halos(halo, inner, outer)


def own_kernel(
    valid_from, video, gain, weight, normed, partial, start, done, *, frames, rows, width
):
    run_copies([(valid_from, start)], done)
    block = frames * width
    for row in range(rows):
        for frame in range(frames):
            unit, _ = normalised(video[frame, row], present(start, frame, frames))
            at = row * block + frame * width
            normed[at : at + width] = (unit * gain[...]).astype(BF16)
    for row in range(rows):
        taps = [i for i in range(3) if 0 <= row + i - 1 < rows]
        cells = [normed[(row + i - 1) * block : (row + i) * block] for i in taps]
        partial[row * block : row * block + block] = column_sum(
            jnp.concatenate(cells, axis=1), weight, taps, width
        )


def front_kernel(
    valid_from, normed, partial, inner, outer, gain, weight, temporal, *refs,
    frames, rows, width, shards
):
    tall, slope, active, parts, *refs = refs
    strided, (halo, start, done, lines) = (refs[:shards], refs[shards:])
    outs = frames // 2
    plane = rows * width
    here = rows // shards
    block = frames * width

    run_copies([(valid_from, start)], done)
    place_halos(halo, inner, outer)
    tall[block : block + rows * block] = normed[...]
    for side, at in ((0, 0), (1, (rows + 1) * block)):
        for frame in range(frames):
            unit, _ = normalised(halo[side, frame], present(start, frame, frames))
            to = at + frame * width
            tall[to : to + width] = (unit * gain[...]).astype(BF16)
    for row in range(rows):
        pre = partial[row * block : row * block + block]
        if row == 0:
            pre = pre + column_sum(tall[:block], weight, [0], width)
        if row == rows - 1:
            pre = pre + column_sum(tall[(rows + 1) * block :], weight, [2], width)
        sigmoid = 1.0 / (1.0 + jnp.exp(-pre))
        slope[row * block : row * block + block] = sigmoid * (1.0 + pre * (1.0 - sigmoid))
        cells = (pre * sigmoid).astype(BF16)
        for frame in range(frames):
            at = (frame // 2) * plane + row * width
            active[frame % 2, at : at + width] = cells[frame * width : frame * width + width]
    evens = active[0]
    odds = active[1]
    carried = dot(odds, temporal[2])
    mixed = dot(odds, temporal[0]) + dot(evens, temporal[1])
    pieces = [mixed[:plane]]
    for s in range(1, outs):
        pieces.append(
            mixed[s * plane : s * plane + plane] + carried[(s - 1) * plane : s * plane]
        )
    pieces.append(carried[(outs - 1) * plane :])
    pieces = jnp.concatenate(pieces, axis=0).astype(BF16)
    parts[...] = pieces
    for frame in range(outs + 1):
        cells = pieces[frame * plane : frame * plane + plane]
        lines[:, frame] = cells.reshape(shards, here, width, 256)
    for step, piece in enumerate(strided):
        piece[...] = lines[lax.axis_index("tm") ^ step]


def middle_kernel(
    tall, slope, active, parts, temporal, mix, cotangent, *refs, frames, rows, width, shards
):
    pieces, refs = (refs[: shards - 1], refs[shards - 1 :])
    pre_gradient, inner_out, outer_out, keep, send, cot = refs
    outs = frames // 2
    plane = rows * width
    here = rows // shards
    me = lax.axis_index("tm")
    total = shards * outs
    cut = outs + 3
    skip = me * outs - first_frame(me, outs, cut, total)
    for frame in range(cut):
        here_is = (me * outs + frame < total).astype(F32)
        own = cotangent[jnp.minimum(me * outs + frame, total - 1)]
        others = [piece[jnp.minimum(frame + skip, cut - 1)] for piece in pieces]
        for step, cells in enumerate([own] + others[::-1]):
            cells = (cells.astype(F32) * here_is).astype(BF16)
            cot[frame, me ^ step] = cells.reshape(here * width, 256)

    def ahead(k, count=outs + 1):
        return cot[k : k + count].reshape(count * plane, 256)

    gradient = ahead(0).astype(F32)
    for k in range(3):
        gradient = gradient + dot_nt(ahead(k), mix[k])
    gradient = gradient.astype(BF16)
    now = gradient[: outs * plane]
    later = gradient[plane:]
    even_gradient = dot_nt(now, temporal[1])
    odd_gradient = dot_nt(now, temporal[0]) + dot_nt(later, temporal[2])
    for row in range(rows):
        for frame in range(frames):
            source = odd_gradient if frame % 2 else even_gradient
            at = (frame // 2) * plane + row * width
            to = (row * frames + frame) * width
            tile = (source[at : at + width] * slope[to : to + width]).astype(BF16)
            pre_gradient[row, frame] = tile
    side = (lax.axis_index("height") % 2) * (rows - 1)
    inner_out[...] = pre_gradient[rows - 1 - side]
    outer_out[...] = pre_gradient[side]
    first = jnp.full((256, 128), lax.axis_index("cam")) == 0

    def deliver(index, product):
        low, high = (product[:, :128], product[:, 128:])
        keep[index] = jnp.where(first, low, high)
        send[index] = jnp.where(first, high, low).astype(BF16)

    evens = active[0]
    odds = active[1]
    for k in range(3):
        deliver(k, dot_tn(parts[...], ahead(k)))
    deliver(3, dot_tn(odds, now))
    deliver(4, dot_tn(evens, now))
    deliver(5, dot_tn(odds, later))
    gradient = pre_gradient[...].reshape(-1, 256)
    exact = gradient.astype(F32)
    columns = [
        from_right(exact, width).astype(BF16), gradient, from_left(exact, width).astype(BF16)
    ]
    block = frames * width
    for i in range(3):
        cells = tall[i * block : (i + rows) * block]
        product = dot_tn(cells, jnp.concatenate(columns, axis=1))
        for j in range(3):
            deliver(6 + i * 3 + j, product[:, j * 256 : j * 256 + 256])


def core_columns():
    mine = pl.ds(pl.multiple_of(lax.axis_index("cam") * 128, 128), 128)
    other = pl.ds(pl.multiple_of((1 - lax.axis_index("cam")) * 128, 128), 128)
    return (mine, other)


def deal(axis, total, kept, sends):
    me = lax.axis_index(axis)
    kept[...] = total(me)
    for step, send in enumerate(sends):
        send[...] = total(me ^ (step + 1)).astype(BF16)


def first_sum_kernel(keep, got, kept, *sends):
    deal("height", lambda at: keep[at] + got[at].astype(F32), kept, sends)


def second_sum_kernel(kept_in, *refs):
    count = kept_in.shape[0]
    received = refs[: len(refs) - count]
    kept, *sends = refs[len(refs) - count :]

    def total(at):
        value = kept_in[at]
        for piece in received:
            value = value + piece[at].astype(F32)
        return value

    deal("tm", total, kept, sends)


def last_sum_kernel(halo, kept, *refs):
    del halo
    value = kept[...]
    for piece in refs[:-1]:
        value = value + piece[...].astype(F32)
    refs[-1][...] = value.astype(BF16)


def assemble_kernel(*refs):
    for step, piece in enumerate(reversed(refs[:-1])):
        refs[-1][lax.axis_index("tm") ^ step] = piece[...]


def input_kernel(
    valid_from, video, pre_gradient, halo, gain, weight, out, tall, start, done,
    *, frames, rows, width
):
    run_copies([(valid_from, start)], done)
    block = frames * width
    for row in range(-1, rows + 1):
        if row < 0:
            cells = halo[0]
        elif row == rows:
            cells = halo[1]
        else:
            cells = pre_gradient[row]
        cells = cells.reshape(block, 256)
        for tap in range(3):
            target = row - 1 + tap
            if 0 <= target < rows:
                tall[target * block : target * block + block, tap * 256 : tap * 256 + 256] = cells
    for row in range(rows):
        cells = tall[row * block : row * block + block]
        taps = [
            dot_nt(cells, jnp.concatenate([weight[0, j], weight[1, j], weight[2, j]], axis=1))
            for j in range(3)
        ]
        gradient = from_right(taps[0], width) + taps[1] + from_left(taps[2], width)
        gradient = gradient * gain[...]
        for frame in range(frames):
            keep = present(start, frame, frames)
            unit, inverse = normalised(video[frame, row], keep)
            tile = gradient[frame * width : frame * width + width]
            mean = jnp.mean(tile * unit, axis=-1, keepdims=True)
            out[frame, row] = (inverse * (tile - unit * mean) * keep).astype(BF16)


def encode_kernel(mix, *refs, width, shards):
    pieces, (out, line, strided) = (refs[:shards], refs[shards:])
    for step, piece in enumerate(pieces):
        strided[lax.axis_index("tm") ^ step] = piece[...]
    parts, here = strided.shape[1:3]
    outs = parts - 1
    plane = here * width
    total = shards * outs
    for frame in range(total):
        shard, part = (frame // outs, frame % outs)
        cells = strided[shard, part].reshape(plane, 256)
        if part == 0 and shard > 0:
            carried = strided[shard - 1, outs].reshape(plane, 256)
            cells = (cells.astype(F32) + carried.astype(F32)).astype(BF16)
        line[(frame + 2) * plane : (frame + 3) * plane] = cells
    line[0 : 2 * plane] = jnp.zeros((2 * plane, 256), BF16)
    span = total * plane
    result = line[2 * plane : 2 * plane + span].astype(F32)
    for k in range(3):
        result = result + dot(line[(2 - k) * plane : (2 - k) * plane + span], mix[k])
    out[...] = result.astype(BF16).reshape(out.shape)


def finish_kernel(*refs, scale, parts, last):
    pieces, refs = (refs[:parts], refs[parts:])
    weight, *refs = refs
    if last:
        gain, before, _, _, _, spatial, temporal, mix, gain_out, staged, done = refs
        columns = core_columns()[1]
        total = before[...]
    else:
        spatial, temporal, mix, after, staged, done = refs
        columns = core_columns()[0]
        total = jnp.zeros((256, 128), F32)
    size = staged.shape[0] // parts
    for step, piece in enumerate(pieces):
        at = pl.multiple_of((lax.axis_index("height") ^ step) * size, size)
        staged[pl.ds(at, size)] = piece[...].astype(F32) * scale
    results = [(mix, k) for k in range(3)] + [(temporal, k) for k in range(3)]
    results = results + [(spatial, k) for k in range(9)]
    copies = []
    for index, (result, k) in enumerate(results):
        copies.append(
            pltpu.make_async_copy(
                staged.at[pl.ds(index * 256, 256)], result.at[k, :, columns], done.at[index]
            )
        )
    for copy in copies:
        copy.start()
    for k in range(9):
        cells = staged[1536 + k * 256 : 1792 + k * 256]
        total = total + cells * weight[k // 3, k % 3, :, columns].astype(F32)
    if last:
        gain_out[...] = jnp.sum(total.T, axis=0, keepdims=True) / gain[...]
    else:
        after[...] = total
    for copy in copies:
        copy.wait()


def call(kernel, outs, scratch=(), flops=0, moved=0, aliases=None, far=0):
    where = pl.BlockSpec(memory_space=pltpu.VMEM)

    def run(*operands):
        results = pl.pallas_call(
            kernel,
            out_shape=[jax.ShapeDtypeStruct(shape, dtype) for shape, dtype in outs],
            in_specs=[
                pl.BlockSpec(memory_space=pltpu.HBM)
                if a.dtype == jnp.int32 or at in (aliases or ())
                else where
                for at, a in enumerate(operands)
            ],
            out_specs=[pl.BlockSpec(memory_space=pltpu.HBM)] * far + [where] * (len(outs) - far),
            input_output_aliases=aliases or {},
            scratch_shapes=list(scratch),
            compiler_params=pltpu.CompilerParams(vmem_limit_bytes=VMEM_LIMIT),
            cost_estimate=pl.CostEstimate(flops=flops, bytes_accessed=moved, transcendentals=0),
        )(*operands)
        return list(results)

    return run


def neighbours(inner, outer, axis):
    size = lax.axis_size(axis)
    links = [(i, i + 1) for i in range(1, size - 1, 2)]
    links = links + [(j, i) for i, j in links]
    return (pair(inner, axis, 1), lax.ppermute(outer, axis, links))


def pair(array, axis, step):
    return lax.ppermute(array, axis, [(i, i ^ step) for i in range(lax.axis_size(axis))])


def pairs(arrays, axis):
    return [pair(array, axis, step + 1) for step, array in enumerate(arrays)]


def together(*values):
    return lax.optimization_barrier(values)


def on_device(
    video_clip, valid_from, norm_gain, spatial_weight, temporal_weight, mix_weight, cotangent
):
    video = video_clip[0]
    frames, rows, width, channels = video.shape
    outs = frames // 2
    shards = lax.axis_size("tm")
    lines = lax.axis_size("height")
    here = rows // shards
    cells = frames * rows * width
    sizes = dict(frames=frames, rows=rows, width=width)
    gain = norm_gain.reshape(1, channels)
    edge = ((frames, width, channels), BF16)
    halo = pltpu.VMEM((2, frames, width, channels), BF16)

    scalar = [pltpu.SMEM((1,), jnp.int32), pltpu.SemaphoreType.DMA((1,))]
    pieces = call(
        functools.partial(pieces_kernel, outs=outs),
        [((outs + 3, here, width, channels), BF16)] * (shards - 1),
        [pltpu.SemaphoreType.DMA((shards - 1,))],
        moved=1024 * 1024,
    )(cotangent[0])
    *pieces, edges = together(*pieces, video)
    pieces = pairs(pieces, "tm")
    inner, outer = call(
        functools.partial(edges_kernel, rows=rows),
        [edge, edge],
        [pltpu.SemaphoreType.DMA((2,))],
        moved=512 * 1024,
    )(edges)
    inner, outer = neighbours(inner, outer, "height")

    normed, partial = call(
        functools.partial(own_kernel, **sizes),
        [((cells, channels), BF16), ((cells, channels), F32)],
        scalar,
        flops=18 * cells * channels * channels,
        moved=4 * 1024 * 1024,
    )(valid_from, video, gain, spatial_weight)

    tall, slope, active, parts, *strided = call(
        functools.partial(front_kernel, **sizes, shards=shards),
        [
            ((cells + 2 * frames * width, channels), BF16),
            ((cells, channels), F32),
            ((2, cells // 2, channels), BF16),
            (((outs + 1) * rows * width, channels), BF16),
        ]
        + [((outs + 1, here, width, channels), BF16)] * shards,
        [halo, *scalar, pltpu.VMEM((shards, outs + 1, here, width, channels), BF16)],
    )(valid_from, normed, partial, inner, outer, gain, spatial_weight, temporal_weight)

    pre_gradient, inner, outer, keep, send = call(
        functools.partial(middle_kernel, **sizes, shards=shards),
        [
            ((rows, frames, width, channels), BF16),
            edge,
            edge,
            ((15, channels, channels // 2), F32),
            ((15, channels, channels // 2), BF16),
        ],
        [pltpu.VMEM((outs + 3, shards, here * width, channels), BF16)],
        flops=36 * cells * channels * channels,
        moved=12 * 1024 * 1024,
    )(
        tall, slope, active, parts, temporal_weight, mix_weight, cotangent[0],
        *reversed(pieces),
    )

    large = 15 * channels // lines
    small = large // shards
    half = channels // 2
    got = pair(send, "cam", 1)
    kept, *sends = call(
        first_sum_kernel,
        [((large, half), F32)] + [((large, half), BF16)] * (lines - 1),
        moved=8 * 1024 * 1024,
    )(keep.reshape(lines, large, half), got.reshape(lines, large, half))
    received = pairs(sends, "height")
    middle = shards // 2
    strided = [strided[0]] + pairs(strided[1:], "tm")
    kept, strided[middle] = together(kept, strided[middle])
    kept, *sends = call(
        second_sum_kernel,
        [((small, half), F32)] + [((small, half), BF16)] * (shards - 1),
        moved=2 * 1024 * 1024,
    )(*[a.reshape(shards, small, half) for a in [kept] + received[::-1]])
    kept, inner, outer = together(kept, inner, outer)
    received = pairs(sends, "tm")
    inner, outer = neighbours(inner, outer, "height")
    (halo_rows,) = call(halo_kernel, [((2, frames, width, channels), BF16)])(inner, outer)
    (total,) = call(last_sum_kernel, [((small, half), BF16)], moved=1024 * 1024)(
        halo_rows, kept, *received[::-1]
    )
    received = pairs([total] * (shards - 1), "tm")
    (video_gradient,) = call(
        functools.partial(input_kernel, **sizes),
        [((frames, rows, width, channels), BF16)],
        [pltpu.VMEM((cells, 3 * channels), BF16)] + scalar,
        flops=18 * cells * channels * channels,
        moved=4 * 1024 * 1024,
    )(valid_from, video, pre_gradient, halo_rows, gain, spatial_weight)
    total, video_gradient = together(total, video_gradient)
    (total,) = call(assemble_kernel, [((shards, small, half), BF16)], moved=1024 * 1024)(
        *received[::-1], total
    )
    total = total.reshape(large, half)
    pieces = [total] + pairs([total] * (lines - 1), "height")
    (encoded,) = call(
        functools.partial(encode_kernel, width=width, shards=shards),
        [((shards * outs, here, width, channels), BF16)],
        [
            pltpu.VMEM(((shards * outs + 2) * here * width, channels), BF16),
            pltpu.VMEM((shards, outs + 1, here, width, channels), BF16),
        ],
        flops=3 * cells * channels * channels,
        moved=2 * 1024 * 1024,
    )(mix_weight, *strided)
    pieces[-1], encoded = together(pieces[-1], encoded)
    pieces = pieces + [pair(piece, "cam", 1) for piece in pieces]

    cell_count = cells * lax.axis_size("cam") * shards * lines
    scale = 1.0 / math.sqrt(cell_count)
    results = [((9, channels, channels), F32)] + [((3, channels, channels), F32)] * 2
    scratch = [pltpu.VMEM((15 * channels, half), F32), pltpu.SemaphoreType.DMA((15,))]
    *results_own, total = call(
        functools.partial(finish_kernel, scale=scale, parts=lines, last=False),
        results + [((channels, half), F32)],
        scratch,
        moved=4 * 1024 * 1024,
        far=3,
    )(*pieces[:lines], spatial_weight)
    spatial, temporal, mix, gain_gradient = call(
        functools.partial(finish_kernel, scale=scale, parts=lines, last=True),
        results + [((1, channels), F32)],
        scratch,
        moved=4 * 1024 * 1024,
        aliases={lines + 3 + at: at for at in range(3)},
        far=3,
    )(*pieces[lines:], spatial_weight, gain, total, *results_own)

    return (
        encoded[None],
        video_gradient[None],
        spatial.reshape(spatial_weight.shape),
        temporal,
        mix,
        gain_gradient.reshape(channels),
    )


def solution(mesh):
    return jax.shard_map(
        on_device,
        mesh=mesh,
        in_specs=(
            P("cam", "tm", "height", None, None),
            P("cam"),
            P(),
            P(),
            P(),
            P(),
            P("cam", None, ("height", "tm"), None, None),
        ),
        out_specs=(
            P("cam", None, ("height", "tm"), None, None),
            P("cam", "tm", "height", None, None),
            P(),
            P(),
            P(),
            P(),
        ),
        check_vma=False,
    )
```

```python
import functools
import math

import jax
import jax.numpy as jnp
from jax import lax
from jax.experimental import pallas as pl
from jax.experimental.pallas import tpu as pltpu
from jax.sharding import PartitionSpec as P

F32 = jnp.float32
BF16 = jnp.bfloat16
VMEM_LIMIT = 16 * 1024 * 1024


def dot(left, right):
    return jnp.dot(left, right, preferred_element_type=F32)


def dot_nt(left, right):
    return lax.dot_general(left, right, (((1,), (1,)), ((), ())), preferred_element_type=F32)


def dot_tn(left, right):
    return lax.dot_general(left, right, (((0,), (0,)), ((), ())), preferred_element_type=F32)


def from_left(cells, width):
    column = lax.broadcasted_iota(jnp.int32, cells.shape, 0) % width
    return jnp.where(column == 0, 0.0, pltpu.roll(cells, 1, 0))


def from_right(cells, width):
    column = lax.broadcasted_iota(jnp.int32, cells.shape, 0) % width
    return jnp.where(column == width - 1, 0.0, pltpu.roll(cells, cells.shape[0] - 1, 0))


def present(start, frame, frames):
    return (lax.axis_index("tm") * frames + frame >= start[0]).astype(F32)


def normalised(tile, keep):
    values = tile.astype(F32) * keep
    inverse = lax.rsqrt(jnp.mean(values * values, axis=-1, keepdims=True) + 1e-06)
    return (values * inverse, inverse)


def first_frame(shard, outs, span, total):
    return jnp.minimum(shard * outs, total - span)


def run_copies(pairs_of_refs, done):
    copies = [
        pltpu.make_async_copy(source, target, done.at[at])
        for at, (source, target) in enumerate(pairs_of_refs)
    ]
    for copy in copies:
        copy.start()
    for copy in copies:
        copy.wait()


def pieces_kernel(cotangent, *refs, outs):
    pieces, done = (refs[:-1], refs[-1])
    span = outs + 3
    me = lax.axis_index("tm")
    copies = []
    for step, piece in enumerate(pieces):
        begin = first_frame(me ^ (step + 1), outs, span, cotangent.shape[0])
        copies.append((cotangent.at[pl.ds(begin, span)], piece))
    run_copies(copies, done)


def edges_kernel(video, inner, outer, done, *, rows):
    odd = lax.axis_index("height") % 2
    run_copies(
        [
            (video.at[:, (1 - odd) * (rows - 1)], inner),
            (video.at[:, odd * (rows - 1)], outer),
        ],
        done,
    )


def first_frame(shard, outs, span, total):
    return jnp.minimum(shard * outs, total - span)


def place_halos(halo, inner, outer):
    odd = lax.axis_index("height") % 2
    halo[1 - odd] = inner[...]
    halo[odd] = outer[...]


def column_sum(cells, weight, taps, width):
    products = [
        dot(cells, jnp.concatenate([weight[i, j] for i in taps], axis=0)) for j in range(3)
    ]
    return from_left(products[0], width) + products[1] + from_right(products[2], width)


def halo_kernel(inner, outer, halo):
    place_halos(halo, inner, outer)


def own_kernel(
    valid_from, video, gain, weight, normed, partial, start, done, *, frames, rows, width
):
    run_copies([(valid_from, start)], done)
    block = frames * width
    for row in range(rows):
        for frame in range(frames):
            unit, _ = normalised(video[frame, row], present(start, frame, frames))
            at = row * block + frame * width
            normed[at : at + width] = (unit * gain[...]).astype(BF16)
    for row in range(rows):
        taps = [i for i in range(3) if 0 <= row + i - 1 < rows]
        cells = [normed[(row + i - 1) * block : (row + i) * block] for i in taps]
        partial[row * block : row * block + block] = column_sum(
            jnp.concatenate(cells, axis=1), weight, taps, width
        )


def front_kernel(
    valid_from, normed, partial, inner, outer, gain, weight, temporal, *refs,
    frames, rows, width, shards
):
    tall, slope, active, parts, *refs = refs
    strided, (halo, start, done, lines) = (refs[:shards], refs[shards:])
    outs = frames // 2
    plane = rows * width
    here = rows // shards
    block = frames * width

    run_copies([(valid_from, start)], done)
    place_halos(halo, inner, outer)
    tall[block : block + rows * block] = normed[...]
    for side, at in ((0, 0), (1, (rows + 1) * block)):
        for frame in range(frames):
            unit, _ = normalised(halo[side, frame], present(start, frame, frames))
            to = at + frame * width
            tall[to : to + width] = (unit * gain[...]).astype(BF16)
    for row in range(rows):
        pre = partial[row * block : row * block + block]
        if row == 0:
            pre = pre + column_sum(tall[:block], weight, [0], width)
        if row == rows - 1:
            pre = pre + column_sum(tall[(rows + 1) * block :], weight, [2], width)
        sigmoid = 1.0 / (1.0 + jnp.exp(-pre))
        slope[row * block : row * block + block] = sigmoid * (1.0 + pre * (1.0 - sigmoid))
        cells = (pre * sigmoid).astype(BF16)
        for frame in range(frames):
            at = (frame // 2) * plane + row * width
            active[frame % 2, at : at + width] = cells[frame * width : frame * width + width]
    evens = active[0]
    odds = active[1]
    carried = dot(odds, temporal[2])
    mixed = dot(odds, temporal[0]) + dot(evens, temporal[1])
    pieces = [mixed[:plane]]
    for s in range(1, outs):
        pieces.append(
            mixed[s * plane : s * plane + plane] + carried[(s - 1) * plane : s * plane]
        )
    pieces.append(carried[(outs - 1) * plane :])
    pieces = jnp.concatenate(pieces, axis=0).astype(BF16)
    parts[...] = pieces
    for frame in range(outs + 1):
        cells = pieces[frame * plane : frame * plane + plane]
        lines[:, frame] = cells.reshape(shards, here, width, 256)
    for step, piece in enumerate(strided):
        piece[...] = lines[lax.axis_index("tm") ^ step]


def middle_kernel(
    tall, slope, active, parts, temporal, mix, cotangent, *refs, frames, rows, width, shards
):
    pieces, refs = (refs[: shards - 1], refs[shards - 1 :])
    pre_gradient, inner_out, outer_out, keep, send, cot = refs
    outs = frames // 2
    plane = rows * width
    here = rows // shards
    me = lax.axis_index("tm")
    total = shards * outs
    cut = outs + 3
    skip = me * outs - first_frame(me, outs, cut, total)
    for frame in range(cut):
        here_is = (me * outs + frame < total).astype(F32)
        own = cotangent[jnp.minimum(me * outs + frame, total - 1)]
        others = [piece[jnp.minimum(frame + skip, cut - 1)] for piece in pieces]
        for step, cells in enumerate([own] + others[::-1]):
            cells = (cells.astype(F32) * here_is).astype(BF16)
            cot[frame, me ^ step] = cells.reshape(here * width, 256)

    def ahead(k, count=outs + 1):
        return cot[k : k + count].reshape(count * plane, 256)

    gradient = ahead(0).astype(F32)
    for k in range(3):
        gradient = gradient + dot_nt(ahead(k), mix[k])
    gradient = gradient.astype(BF16)
    now = gradient[: outs * plane]
    later = gradient[plane:]
    even_gradient = dot_nt(now, temporal[1])
    odd_gradient = dot_nt(now, temporal[0]) + dot_nt(later, temporal[2])
    for row in range(rows):
        for frame in range(frames):
            source = odd_gradient if frame % 2 else even_gradient
            at = (frame // 2) * plane + row * width
            to = (row * frames + frame) * width
            tile = (source[at : at + width] * slope[to : to + width]).astype(BF16)
            pre_gradient[row, frame] = tile
    side = (lax.axis_index("height") % 2) * (rows - 1)
    inner_out[...] = pre_gradient[rows - 1 - side]
    outer_out[...] = pre_gradient[side]
    evens = active[0]
    odds = active[1]
    for k in range(3):
        deliver(keep, send, k, dot_tn(parts[...], ahead(k)))
    deliver(keep, send, 3, dot_tn(odds, now))
    deliver(keep, send, 4, dot_tn(evens, now))
    deliver(keep, send, 5, dot_tn(odds, later))
    columns = column_shifts(pre_gradient, width)
    block = frames * width
    deliver(keep, send, 6, dot_tn(tall[: rows * block], columns[0]))


def spatial_kernel(tall, pre_gradient, keep, send, *, frames, rows, width):
    columns = column_shifts(pre_gradient, width)
    block = frames * width
    for i in range(3):
        cells = tall[i * block : (i + rows) * block]
        skipped = 1 if i == 0 else 0
        product = dot_tn(cells, jnp.concatenate(columns[skipped:], axis=1))
        for j in range(skipped, 3):
            at = (j - skipped) * 256
            deliver(keep, send, i * 3 + j - 1, product[:, at : at + 256])


def column_shifts(pre_gradient, width):
    gradient = pre_gradient[...].reshape(-1, 256)
    exact = gradient.astype(F32)
    left = from_right(exact, width).astype(BF16)
    right = from_left(exact, width).astype(BF16)
    return [left, gradient, right]


def deliver(keep, send, index, product):
    first = jnp.full((256, 128), lax.axis_index("cam")) == 0
    low, high = (product[:, :128], product[:, 128:])
    at = index * 256
    keep[at : at + 256] = jnp.where(first, low, high)
    send[at : at + 256] = jnp.where(first, high, low).astype(BF16)


def core_columns():
    mine = pl.ds(pl.multiple_of(lax.axis_index("cam") * 128, 128), 128)
    other = pl.ds(pl.multiple_of((1 - lax.axis_index("cam")) * 128, 128), 128)
    return (mine, other)


def deal_kernel(keep, got, kept, *sends):
    me = lax.axis_index("height")
    kept[...] = keep[me] + got[me].astype(F32)
    for step, send in enumerate(sends):
        at = me ^ (step + 1)
        send[...] = (keep[at] + got[at].astype(F32)).astype(BF16)


def halve_kernel(*refs):
    (kept_in, *received), (kept, send) = (refs[:-2], refs[-2:])
    mine = lax.axis_index("tm") % 2

    def total(at):
        value = kept_in[at]
        for piece in received:
            value = value + piece[at].astype(F32)
        return value

    kept[...] = total(mine)
    send[...] = total(1 - mine).astype(BF16)


def add_kernel(left, right, out):
    out[...] = (left[...].astype(F32) + right[...].astype(F32)).astype(BF16)


def whole_kernel(mine, other, out):
    at = lax.axis_index("tm") % 2
    out[at] = mine[...]
    out[1 - at] = other[...]


def join_kernel(*refs):
    for step, piece in enumerate(refs[:-1]):
        refs[-1][lax.axis_index("height") ^ step] = piece[...]


def input_kernel(
    valid_from, video, pre_gradient, halo, gain, weight, out, tall, start, done,
    *, frames, rows, width
):
    run_copies([(valid_from, start)], done)
    block = frames * width
    for row in range(-1, rows + 1):
        if row < 0:
            cells = halo[0]
        elif row == rows:
            cells = halo[1]
        else:
            cells = pre_gradient[row]
        cells = cells.reshape(block, 256)
        for tap in range(3):
            target = row - 1 + tap
            if 0 <= target < rows:
                tall[target * block : target * block + block, tap * 256 : tap * 256 + 256] = cells
    for row in range(rows):
        cells = tall[row * block : row * block + block]
        taps = [
            dot_nt(cells, jnp.concatenate([weight[0, j], weight[1, j], weight[2, j]], axis=1))
            for j in range(3)
        ]
        gradient = from_right(taps[0], width) + taps[1] + from_left(taps[2], width)
        gradient = gradient * gain[...]
        for frame in range(frames):
            keep = present(start, frame, frames)
            unit, inverse = normalised(video[frame, row], keep)
            tile = gradient[frame * width : frame * width + width]
            mean = jnp.mean(tile * unit, axis=-1, keepdims=True)
            out[frame, row] = (inverse * (tile - unit * mean) * keep).astype(BF16)


def encode_kernel(mix, *refs, width, shards):
    pieces, (out, line, strided) = (refs[:shards], refs[shards:])
    for step, piece in enumerate(pieces):
        strided[lax.axis_index("tm") ^ step] = piece[...]
    parts, here = strided.shape[1:3]
    outs = parts - 1
    plane = here * width
    total = shards * outs
    for frame in range(total):
        shard, part = (frame // outs, frame % outs)
        cells = strided[shard, part].reshape(plane, 256)
        if part == 0 and shard > 0:
            carried = strided[shard - 1, outs].reshape(plane, 256)
            cells = (cells.astype(F32) + carried.astype(F32)).astype(BF16)
        line[(frame + 2) * plane : (frame + 3) * plane] = cells
    line[0 : 2 * plane] = jnp.zeros((2 * plane, 256), BF16)
    span = total * plane
    result = line[2 * plane : 2 * plane + span].astype(F32)
    for k in range(3):
        result = result + dot(line[(2 - k) * plane : (2 - k) * plane + span], mix[k])
    out[...] = result.astype(BF16).reshape(out.shape)


def finish_kernel(*refs, scale, first, sides, last):
    blocks, refs = (refs[: len(sides)], refs[len(sides) :])
    weight, *refs = refs
    staged, done = refs[-2:]
    if first == 0:
        spatial, temporal, mix, after = refs[:-2]
        results = [(mix, k) for k in range(3)] + [(temporal, k) for k in range(3)]
        results.append((spatial, 0))
        total = jnp.zeros((256, 128), F32)
    else:
        before, *refs = refs
        if last:
            gain, *refs = refs
        _, spatial, after = refs[:-2]
        results = [(spatial, k) for k in range(1, 9)]
        total = before[...]
    copies = []
    for place, side in enumerate(sides):
        columns = core_columns()[side]
        staged[place] = blocks[place][...].astype(F32) * scale
        for index, (result, k) in enumerate(results):
            copies.append(
                pltpu.make_async_copy(
                    staged.at[place, pl.ds(index * 256, 256)],
                    result.at[k, :, columns],
                    done.at[place, index],
                )
            )
            copies[-1].start()
    for place, side in enumerate(sides):
        columns = core_columns()[side]
        for index, (result, k) in enumerate(results):
            if result is spatial:
                cells = staged[place, index * 256 : index * 256 + 256]
                total = total + cells * weight[k // 3, k % 3, :, columns].astype(F32)
    if last:
        high = total.astype(BF16)
        low = (total - high.astype(F32)).astype(BF16)
        ones = jnp.ones((16, 128), BF16)
        after[...] = (dot_nt(ones, high) + dot_nt(ones, low))[:1] / gain[...]
    else:
        after[...] = total
    for copy in copies:
        copy.wait()


def call(kernel, outs, scratch=(), flops=0, moved=0, aliases=None, far=0):
    where = pl.BlockSpec(memory_space=pltpu.VMEM)

    def run(*operands):
        results = pl.pallas_call(
            kernel,
            out_shape=[jax.ShapeDtypeStruct(shape, dtype) for shape, dtype in outs],
            in_specs=[
                pl.BlockSpec(memory_space=pltpu.HBM)
                if a.dtype == jnp.int32 or at in (aliases or ())
                else where
                for at, a in enumerate(operands)
            ],
            out_specs=[pl.BlockSpec(memory_space=pltpu.HBM)] * far + [where] * (len(outs) - far),
            input_output_aliases=aliases or {},
            scratch_shapes=list(scratch),
            compiler_params=pltpu.CompilerParams(vmem_limit_bytes=VMEM_LIMIT),
            cost_estimate=pl.CostEstimate(flops=flops, bytes_accessed=moved, transcendentals=0),
        )(*operands)
        return list(results)

    return run


def neighbours(inner, outer, axis):
    size = lax.axis_size(axis)
    links = [(i, i + 1) for i in range(1, size - 1, 2)]
    links = links + [(j, i) for i, j in links]
    return (pair(inner, axis, 1), lax.ppermute(outer, axis, links))


def pair(array, axis, step):
    return lax.ppermute(array, axis, [(i, i ^ step) for i in range(lax.axis_size(axis))])


def pairs(arrays, axis):
    return [pair(array, axis, step + 1) for step, array in enumerate(arrays)]


def together(*values):
    return lax.optimization_barrier(values)


def on_device(
    video_clip, valid_from, norm_gain, spatial_weight, temporal_weight, mix_weight, cotangent
):
    video = video_clip[0]
    frames, rows, width, channels = video.shape
    outs = frames // 2
    shards = lax.axis_size("tm")
    lines = lax.axis_size("height")
    here = rows // shards
    cells = frames * rows * width
    sizes = dict(frames=frames, rows=rows, width=width)
    gain = norm_gain.reshape(1, channels)
    edge = ((frames, width, channels), BF16)
    halo = pltpu.VMEM((2, frames, width, channels), BF16)

    scalar = [pltpu.SMEM((1,), jnp.int32), pltpu.SemaphoreType.DMA((1,))]
    pieces = call(
        functools.partial(pieces_kernel, outs=outs),
        [((outs + 3, here, width, channels), BF16)] * (shards - 1),
        [pltpu.SemaphoreType.DMA((shards - 1,))],
        moved=1024 * 1024,
    )(cotangent[0])
    *pieces, edges = together(*pieces, video)
    pieces = pairs(pieces, "tm")
    inner, outer = call(
        functools.partial(edges_kernel, rows=rows),
        [edge, edge],
        [pltpu.SemaphoreType.DMA((2,))],
        moved=512 * 1024,
    )(edges)
    inner, outer = neighbours(inner, outer, "height")

    normed, partial = call(
        functools.partial(own_kernel, **sizes),
        [((cells, channels), BF16), ((cells, channels), F32)],
        scalar,
        flops=18 * cells * channels * channels,
        moved=4 * 1024 * 1024,
    )(valid_from, video, gain, spatial_weight)

    tall, slope, active, parts, *strided = call(
        functools.partial(front_kernel, **sizes, shards=shards),
        [
            ((cells + 2 * frames * width, channels), BF16),
            ((cells, channels), F32),
            ((2, cells // 2, channels), BF16),
            (((outs + 1) * rows * width, channels), BF16),
        ]
        + [((outs + 1, here, width, channels), BF16)] * shards,
        [halo, *scalar, pltpu.VMEM((shards, outs + 1, here, width, channels), BF16)],
    )(valid_from, normed, partial, inner, outer, gain, spatial_weight, temporal_weight)

    half = channels // 2
    pre_gradient, inner, outer, *low = call(
        functools.partial(middle_kernel, **sizes, shards=shards),
        [
            ((rows, frames, width, channels), BF16),
            edge,
            edge,
            ((7 * channels, half), F32),
            ((7 * channels, half), BF16),
        ],
        [pltpu.VMEM((outs + 3, shards, here * width, channels), BF16)],
        flops=20 * cells * channels * channels,
        moved=6 * 1024 * 1024,
    )(
        tall, slope, active, parts, temporal_weight, mix_weight, cotangent[0],
        *reversed(pieces),
    )

    high = call(
        functools.partial(spatial_kernel, **sizes),
        [((8 * channels, half), F32), ((8 * channels, half), BF16)],
        flops=16 * cells * channels * channels,
        moved=6 * 1024 * 1024,
    )(tall, pre_gradient)

    def shapes(rows_in, *types):
        return [((rows_in, half), dtype) for dtype in types]

    def spread_rows(chunk):
        keep, send = chunk
        got = pair(send, "cam", 1)
        size = keep.shape[0] // lines
        kept, *sends = call(deal_kernel, shapes(size, F32, *[BF16] * (lines - 1)))(
            keep.reshape(lines, size, half), got.reshape(lines, size, half)
        )
        return [kept] + pairs(sends, "height")[::-1]

    def halved(pieces):
        size = pieces[0].shape[0] // 2
        kept, send = call(halve_kernel, shapes(size, F32, BF16))(
            *[piece.reshape(2, size, half) for piece in pieces]
        )
        return (kept, pair(send, "tm", 1))

    def added(values):
        (total,) = call(add_kernel, shapes(values[0].shape[0], BF16))(*values)
        return total

    def doubled(values):
        total = added(values)
        for step in range(1, shards.bit_length() - 1):
            if step > 1:
                total = added((total, other))
            other = pair(total, "tm", 1 << step)
        return (total, other)

    def regained(values):
        total = added(values)
        return (total, pair(total, "tm", 1))

    def gathered(values):
        size = values[0].shape[0]
        (total,) = call(whole_kernel, [((2, size, half), BF16)])(*values)
        total = total.reshape(2 * size, half)
        return [total] + pairs([total] * (lines - 1), "height")

    def joined(pieces):
        size = pieces[0].shape[0]
        (total,) = call(join_kernel, [((lines, size, half), BF16)])(*pieces)
        return total.reshape(lines * size, half)

    low = spread_rows(low)
    high = spread_rows(high)
    far = pairs(strided[1:], "tm")[1:]
    low = list(halved(low))
    low[0], inner, outer = together(low[0], inner, outer)
    inner, outer = neighbours(inner, outer, "height")
    high[0], *low = together(high[0], *low)
    high[0], *far = together(high[0], *far)
    high = halved(high)
    low = doubled(low)
    high = list(high)
    high[0], *low = together(high[0], *low)
    high = doubled(high)
    low = regained(low)
    (halo_rows,) = call(halo_kernel, [((2, frames, width, channels), BF16)])(inner, outer)
    high = list(high)
    high[0], halo_rows, *low = together(high[0], halo_rows, *low)
    high = list(regained(high))
    low = gathered(low)
    (video_gradient,) = call(
        functools.partial(input_kernel, **sizes),
        [((frames, rows, width, channels), BF16)],
        [pltpu.VMEM((cells, 3 * channels), BF16)] + scalar,
        flops=18 * cells * channels * channels,
        moved=4 * 1024 * 1024,
    )(valid_from, video, pre_gradient, halo_rows, gain, spatial_weight)
    high[0], video_gradient, *low = together(high[0], video_gradient, *low)
    low = joined(low)
    low = (low, pair(low, "cam", 1))
    high[0], near = together(high[0], strided[1])
    high = gathered(high)
    strided = [strided[0], pair(near, "tm", 1)] + far

    cell_count = cells * lax.axis_size("cam") * shards * lines
    scale = 1.0 / math.sqrt(cell_count)

    def finish(operands, outs, first, count, sides, last, far, aliases):
        return call(
            functools.partial(finish_kernel, scale=scale, first=first, sides=sides, last=last),
            outs,
            [
                pltpu.VMEM((len(sides), count * channels, half), F32),
                pltpu.SemaphoreType.DMA((len(sides), count)),
            ],
            moved=2 * 1024 * 1024,
            far=far,
            aliases=aliases,
        )(*operands)

    nine = ((9, channels, channels), F32)
    three = ((3, channels, channels), F32)
    partial_gain = ((channels, half), F32)
    spatial, temporal, mix, total = finish(
        (*low, spatial_weight), [nine, three, three, partial_gain], 0, 7, (0, 1), False, 3, None
    )
    (encoded,) = call(
        functools.partial(encode_kernel, width=width, shards=shards),
        [((shards * outs, here, width, channels), BF16)],
        [
            pltpu.VMEM(((shards * outs + 2) * here * width, channels), BF16),
            pltpu.VMEM((shards, outs + 1, here, width, channels), BF16),
        ],
        flops=3 * cells * channels * channels,
        moved=2 * 1024 * 1024,
    )(mix_weight, *strided)
    high[-1], total, encoded = together(high[-1], total, encoded)
    high = joined(high)
    other = pair(high, "cam", 1)
    spatial, total = finish(
        (high, spatial_weight, total, spatial), [nine, partial_gain], 7, 8, (0,), False, 1, {3: 0}
    )
    spatial, gain_gradient = finish(
        (other, spatial_weight, total, gain, spatial),
        [nine, ((1, channels), F32)],
        7,
        8,
        (1,),
        True,
        1,
        {4: 0},
    )

    return (
        encoded[None],
        video_gradient[None],
        spatial.reshape(spatial_weight.shape),
        temporal,
        mix,
        gain_gradient.reshape(channels),
    )


def solution(mesh):
    return jax.shard_map(
        on_device,
        mesh=mesh,
        in_specs=(
            P("cam", "tm", "height", None, None),
            P("cam"),
            P(),
            P(),
            P(),
            P(),
            P("cam", None, ("height", "tm"), None, None),
        ),
        out_specs=(
            P("cam", None, ("height", "tm"), None, None),
            P("cam", "tm", "height", None, None),
            P(),
            P(),
            P(),
            P(),
        ),
        check_vma=False,
    )
```

```python
import functools
import math

import jax
import jax.numpy as jnp
from jax import lax
from jax.experimental import pallas as pl
from jax.experimental.pallas import tpu as pltpu
from jax.sharding import PartitionSpec as P

F32 = jnp.float32
BF16 = jnp.bfloat16
VMEM_LIMIT = 16 * 1024 * 1024
SPLIT = 11


def dot(left, right):
    return jnp.dot(left, right, preferred_element_type=F32)


def dot_nt(left, right):
    return lax.dot_general(left, right, (((1,), (1,)), ((), ())), preferred_element_type=F32)


def dot_tn(left, right):
    return lax.dot_general(left, right, (((0,), (0,)), ((), ())), preferred_element_type=F32)


def from_left(cells, width):
    column = lax.broadcasted_iota(jnp.int32, cells.shape, 0) % width
    return jnp.where(column == 0, 0.0, pltpu.roll(cells, 1, 0))


def from_right(cells, width):
    column = lax.broadcasted_iota(jnp.int32, cells.shape, 0) % width
    return jnp.where(column == width - 1, 0.0, pltpu.roll(cells, cells.shape[0] - 1, 0))


def present(start, frame, frames):
    return (lax.axis_index("tm") * frames + frame >= start[0]).astype(F32)


def normalised(tile, keep):
    values = tile.astype(F32) * keep
    inverse = lax.rsqrt(jnp.mean(values * values, axis=-1, keepdims=True) + 1e-06)
    return (values * inverse, inverse)


def first_frame(shard, outs, span, total):
    return jnp.minimum(shard * outs, total - span)


def run_copies(pairs_of_refs, done):
    copies = [
        pltpu.make_async_copy(source, target, done.at[at])
        for at, (source, target) in enumerate(pairs_of_refs)
    ]
    for copy in copies:
        copy.start()
    for copy in copies:
        copy.wait()


def pieces_kernel(cotangent, *refs, outs):
    pieces, done = (refs[:-1], refs[-1])
    span = outs + 3
    me = lax.axis_index("tm")
    copies = []
    for step, piece in enumerate(pieces):
        begin = first_frame(me ^ (step + 1), outs, span, cotangent.shape[0])
        copies.append((cotangent.at[pl.ds(begin, span)], piece))
    run_copies(copies, done)


def edges_kernel(video, inner, outer, done, *, rows):
    odd = lax.axis_index("height") % 2
    run_copies(
        [
            (video.at[:, (1 - odd) * (rows - 1)], inner),
            (video.at[:, odd * (rows - 1)], outer),
        ],
        done,
    )


def first_frame(shard, outs, span, total):
    return jnp.minimum(shard * outs, total - span)


def place_halos(halo, inner, outer):
    odd = lax.axis_index("height") % 2
    halo[1 - odd] = inner[...]
    halo[odd] = outer[...]


def column_sum(cells, weight, taps, width):
    products = [
        dot(cells, jnp.concatenate([weight[i, j] for i in taps], axis=0)) for j in range(3)
    ]
    return from_left(products[0], width) + products[1] + from_right(products[2], width)


def halo_kernel(inner, outer, halo):
    place_halos(halo, inner, outer)


def own_kernel(
    valid_from, video, gain, weight, normed, partial, start, done, *, frames, rows, width
):
    run_copies([(valid_from, start)], done)
    block = frames * width
    for row in range(rows):
        for frame in range(frames):
            unit, _ = normalised(video[frame, row], present(start, frame, frames))
            at = row * block + frame * width
            normed[at : at + width] = (unit * gain[...]).astype(BF16)
    for row in range(rows):
        taps = [i for i in range(3) if 0 <= row + i - 1 < rows]
        cells = [normed[(row + i - 1) * block : (row + i) * block] for i in taps]
        partial[row * block : row * block + block] = column_sum(
            jnp.concatenate(cells, axis=1), weight, taps, width
        )


def front_kernel(
    valid_from, normed, partial, inner, outer, gain, weight, temporal, *refs,
    frames, rows, width, shards
):
    tall, slope, active, parts, *refs = refs
    strided, (halo, start, done, lines) = (refs[:shards], refs[shards:])
    outs = frames // 2
    plane = rows * width
    here = rows // shards
    block = frames * width

    run_copies([(valid_from, start)], done)
    place_halos(halo, inner, outer)
    tall[block : block + rows * block] = normed[...]
    for side, at in ((0, 0), (1, (rows + 1) * block)):
        for frame in range(frames):
            unit, _ = normalised(halo[side, frame], present(start, frame, frames))
            to = at + frame * width
            tall[to : to + width] = (unit * gain[...]).astype(BF16)
    for row in range(rows):
        pre = partial[row * block : row * block + block]
        if row == 0:
            pre = pre + column_sum(tall[:block], weight, [0], width)
        if row == rows - 1:
            pre = pre + column_sum(tall[(rows + 1) * block :], weight, [2], width)
        sigmoid = 1.0 / (1.0 + jnp.exp(-pre))
        slope[row * block : row * block + block] = sigmoid * (1.0 + pre * (1.0 - sigmoid))
        cells = (pre * sigmoid).astype(BF16)
        for frame in range(frames):
            at = (frame // 2) * plane + row * width
            active[frame % 2, at : at + width] = cells[frame * width : frame * width + width]
    evens = active[0]
    odds = active[1]
    carried = dot(odds, temporal[2])
    mixed = dot(odds, temporal[0]) + dot(evens, temporal[1])
    pieces = [mixed[:plane]]
    for s in range(1, outs):
        pieces.append(
            mixed[s * plane : s * plane + plane] + carried[(s - 1) * plane : s * plane]
        )
    pieces.append(carried[(outs - 1) * plane :])
    pieces = jnp.concatenate(pieces, axis=0).astype(BF16)
    parts[...] = pieces
    for frame in range(outs + 1):
        cells = pieces[frame * plane : frame * plane + plane]
        lines[:, frame] = cells.reshape(shards, here, width, 256)
    for step, piece in enumerate(strided):
        piece[...] = lines[lax.axis_index("tm") ^ step]


def middle_kernel(
    tall, slope, active, parts, temporal, mix, cotangent, *refs, frames, rows, width, shards
):
    pieces, refs = (refs[: shards - 1], refs[shards - 1 :])
    pre_gradient, inner_out, outer_out, keep, send, cot = refs
    outs = frames // 2
    plane = rows * width
    here = rows // shards
    me = lax.axis_index("tm")
    total = shards * outs
    cut = outs + 3
    skip = me * outs - first_frame(me, outs, cut, total)
    for frame in range(cut):
        here_is = (me * outs + frame < total).astype(F32)
        own = cotangent[jnp.minimum(me * outs + frame, total - 1)]
        others = [piece[jnp.minimum(frame + skip, cut - 1)] for piece in pieces]
        for step, cells in enumerate([own] + others[::-1]):
            cells = (cells.astype(F32) * here_is).astype(BF16)
            cot[frame, me ^ step] = cells.reshape(here * width, 256)

    def ahead(k, count=outs + 1):
        return cot[k : k + count].reshape(count * plane, 256)

    gradient = ahead(0).astype(F32)
    for k in range(3):
        gradient = gradient + dot_nt(ahead(k), mix[k])
    gradient = gradient.astype(BF16)
    now = gradient[: outs * plane]
    later = gradient[plane:]
    even_gradient = dot_nt(now, temporal[1])
    odd_gradient = dot_nt(now, temporal[0]) + dot_nt(later, temporal[2])
    for row in range(rows):
        for frame in range(frames):
            source = odd_gradient if frame % 2 else even_gradient
            at = (frame // 2) * plane + row * width
            to = (row * frames + frame) * width
            tile = (source[at : at + width] * slope[to : to + width]).astype(BF16)
            pre_gradient[row, frame] = tile
    side = (lax.axis_index("height") % 2) * (rows - 1)
    inner_out[...] = pre_gradient[rows - 1 - side]
    outer_out[...] = pre_gradient[side]
    evens = active[0]
    odds = active[1]
    for k in range(3):
        deliver(keep, send, k, dot_tn(parts[...], ahead(k)))
    deliver(keep, send, 3, dot_tn(odds, now))
    deliver(keep, send, 4, dot_tn(evens, now))
    deliver(keep, send, 5, dot_tn(odds, later))
    block = frames * width
    spatial_sums(tall, pre_gradient, keep, send, 6, range(SPLIT - 6), block, rows, width)


def spatial_kernel(tall, pre_gradient, keep, send, *, frames, rows, width):
    block = frames * width
    spatial_sums(tall, pre_gradient, keep, send, 0, range(SPLIT - 6, 9), block, rows, width)


def spatial_sums(tall, pre_gradient, keep, send, first, taps, block, rows, width):
    columns = column_shifts(pre_gradient, width)
    for i in range(3):
        here = [tap for tap in taps if tap // 3 == i]
        if not here:
            continue
        cells = tall[i * block : (i + rows) * block]
        product = dot_tn(cells, jnp.concatenate([columns[tap % 3] for tap in here], axis=1))
        for place, tap in enumerate(here):
            index = first + tap - taps[0]
            deliver(keep, send, index, product[:, place * 256 : place * 256 + 256])


def column_shifts(pre_gradient, width):
    gradient = pre_gradient[...].reshape(-1, 256)
    exact = gradient.astype(F32)
    left = from_right(exact, width).astype(BF16)
    right = from_left(exact, width).astype(BF16)
    return [left, gradient, right]


def deliver(keep, send, index, product):
    first = jnp.full((256, 128), lax.axis_index("cam")) == 0
    low, high = (product[:, :128], product[:, 128:])
    at = index * 256
    keep[at : at + 256] = jnp.where(first, low, high)
    send[at : at + 256] = jnp.where(first, high, low).astype(BF16)


def core_columns():
    mine = pl.ds(pl.multiple_of(lax.axis_index("cam") * 128, 128), 128)
    other = pl.ds(pl.multiple_of((1 - lax.axis_index("cam")) * 128, 128), 128)
    return (mine, other)


def deal_kernel(keep, got, kept, *sends):
    me = lax.axis_index("height")
    kept[...] = keep[me] + got[me].astype(F32)
    for step, send in enumerate(sends):
        at = me ^ (step + 1)
        send[...] = (keep[at] + got[at].astype(F32)).astype(BF16)


def halve_kernel(*refs):
    (kept_in, *received), (kept, send) = (refs[:-2], refs[-2:])
    mine = lax.axis_index("tm") % 2

    def total(at):
        value = kept_in[at]
        for piece in received:
            value = value + piece[at].astype(F32)
        return value

    kept[...] = total(mine)
    send[...] = total(1 - mine).astype(BF16)


def add_kernel(left, right, out):
    out[...] = (left[...].astype(F32) + right[...].astype(F32)).astype(BF16)


def whole_kernel(mine, other, out, *, axis, step):
    at = (lax.axis_index(axis) >> step) % 2
    out[at] = mine[...]
    out[1 - at] = other[...]


def join_kernel(*refs):
    for step, piece in enumerate(refs[:-1]):
        refs[-1][lax.axis_index("height") ^ step] = piece[...]


def input_kernel(
    valid_from, video, pre_gradient, halo, gain, weight, out, tall, start, done,
    *, frames, rows, width
):
    run_copies([(valid_from, start)], done)
    block = frames * width
    for row in range(-1, rows + 1):
        if row < 0:
            cells = halo[0]
        elif row == rows:
            cells = halo[1]
        else:
            cells = pre_gradient[row]
        cells = cells.reshape(block, 256)
        for tap in range(3):
            target = row - 1 + tap
            if 0 <= target < rows:
                tall[target * block : target * block + block, tap * 256 : tap * 256 + 256] = cells
    for row in range(rows):
        cells = tall[row * block : row * block + block]
        taps = [
            dot_nt(cells, jnp.concatenate([weight[0, j], weight[1, j], weight[2, j]], axis=1))
            for j in range(3)
        ]
        gradient = from_right(taps[0], width) + taps[1] + from_left(taps[2], width)
        gradient = gradient * gain[...]
        for frame in range(frames):
            keep = present(start, frame, frames)
            unit, inverse = normalised(video[frame, row], keep)
            tile = gradient[frame * width : frame * width + width]
            mean = jnp.mean(tile * unit, axis=-1, keepdims=True)
            out[frame, row] = (inverse * (tile - unit * mean) * keep).astype(BF16)


def encode_kernel(mix, *refs, width, shards):
    pieces, (out, line, strided) = (refs[:shards], refs[shards:])
    for step, piece in enumerate(pieces):
        strided[lax.axis_index("tm") ^ step] = piece[...]
    parts, here = strided.shape[1:3]
    outs = parts - 1
    plane = here * width
    total = shards * outs
    for frame in range(total):
        shard, part = (frame // outs, frame % outs)
        cells = strided[shard, part].reshape(plane, 256)
        if part == 0 and shard > 0:
            carried = strided[shard - 1, outs].reshape(plane, 256)
            cells = (cells.astype(F32) + carried.astype(F32)).astype(BF16)
        line[(frame + 2) * plane : (frame + 3) * plane] = cells
    line[0 : 2 * plane] = jnp.zeros((2 * plane, 256), BF16)
    span = total * plane
    result = line[2 * plane : 2 * plane + span].astype(F32)
    for k in range(3):
        result = result + dot(line[(2 - k) * plane : (2 - k) * plane + span], mix[k])
    out[...] = result.astype(BF16).reshape(out.shape)


def finish_kernel(low, high, weight, *refs, scale, last):
    if last:
        before, gain, _, _, _, spatial, temporal, mix, after, staged, done = refs
        total = before[...]
    else:
        spatial, temporal, mix, after, staged, done = refs
        total = jnp.zeros((256, 128), F32)
    columns = core_columns()[1 if last else 0]
    results = [(mix, k) for k in range(3)] + [(temporal, k) for k in range(3)]
    results = results + [(spatial, k) for k in range(9)]
    copies = []
    for index, (result, k) in enumerate(results):
        source = low if index < SPLIT else high
        at = (index if index < SPLIT else index - SPLIT) * 256
        cells = source[at : at + 256].astype(F32) * scale
        staged[index] = cells
        copies.append(
            pltpu.make_async_copy(staged.at[index], result.at[k, :, columns], done.at[index])
        )
        copies[-1].start()
        if result is spatial:
            total = total + cells * weight[k // 3, k % 3, :, columns].astype(F32)
    if last:
        upper = total.astype(BF16)
        lower = (total - upper.astype(F32)).astype(BF16)
        ones = jnp.ones((16, 128), BF16)
        after[...] = (dot_nt(ones, upper) + dot_nt(ones, lower))[:1] / gain[...]
    else:
        after[...] = total
    for copy in copies:
        copy.wait()


def call(kernel, outs, scratch=(), flops=0, moved=0, aliases=None, far=0):
    where = pl.BlockSpec(memory_space=pltpu.VMEM)

    def run(*operands):
        results = pl.pallas_call(
            kernel,
            out_shape=[jax.ShapeDtypeStruct(shape, dtype) for shape, dtype in outs],
            in_specs=[
                pl.BlockSpec(memory_space=pltpu.HBM)
                if a.dtype == jnp.int32 or at in (aliases or ())
                else where
                for at, a in enumerate(operands)
            ],
            out_specs=[pl.BlockSpec(memory_space=pltpu.HBM)] * far + [where] * (len(outs) - far),
            input_output_aliases=aliases or {},
            scratch_shapes=list(scratch),
            compiler_params=pltpu.CompilerParams(vmem_limit_bytes=VMEM_LIMIT),
            cost_estimate=pl.CostEstimate(flops=flops, bytes_accessed=moved, transcendentals=0),
        )(*operands)
        return list(results)

    return run


def neighbours(inner, outer, axis):
    size = lax.axis_size(axis)
    links = [(i, i + 1) for i in range(1, size - 1, 2)]
    links = links + [(j, i) for i, j in links]
    return (pair(inner, axis, 1), lax.ppermute(outer, axis, links))


def pair(array, axis, step):
    return lax.ppermute(array, axis, [(i, i ^ step) for i in range(lax.axis_size(axis))])


def pairs(arrays, axis):
    return [pair(array, axis, step + 1) for step, array in enumerate(arrays)]


def together(*values):
    return lax.optimization_barrier(values)


def on_device(
    video_clip, valid_from, norm_gain, spatial_weight, temporal_weight, mix_weight, cotangent
):
    video = video_clip[0]
    frames, rows, width, channels = video.shape
    outs = frames // 2
    shards = lax.axis_size("tm")
    lines = lax.axis_size("height")
    here = rows // shards
    cells = frames * rows * width
    sizes = dict(frames=frames, rows=rows, width=width)
    gain = norm_gain.reshape(1, channels)
    edge = ((frames, width, channels), BF16)
    halo = pltpu.VMEM((2, frames, width, channels), BF16)

    scalar = [pltpu.SMEM((1,), jnp.int32), pltpu.SemaphoreType.DMA((1,))]
    pieces = call(
        functools.partial(pieces_kernel, outs=outs),
        [((outs + 3, here, width, channels), BF16)] * (shards - 1),
        [pltpu.SemaphoreType.DMA((shards - 1,))],
        moved=1024 * 1024,
    )(cotangent[0])
    *pieces, edges = together(*pieces, video)
    pieces = pairs(pieces, "tm")
    inner, outer = call(
        functools.partial(edges_kernel, rows=rows),
        [edge, edge],
        [pltpu.SemaphoreType.DMA((2,))],
        moved=512 * 1024,
    )(edges)
    inner, outer = neighbours(inner, outer, "height")

    normed, partial = call(
        functools.partial(own_kernel, **sizes),
        [((cells, channels), BF16), ((cells, channels), F32)],
        scalar,
        flops=18 * cells * channels * channels,
        moved=4 * 1024 * 1024,
    )(valid_from, video, gain, spatial_weight)

    tall, slope, active, parts, *strided = call(
        functools.partial(front_kernel, **sizes, shards=shards),
        [
            ((cells + 2 * frames * width, channels), BF16),
            ((cells, channels), F32),
            ((2, cells // 2, channels), BF16),
            (((outs + 1) * rows * width, channels), BF16),
        ]
        + [((outs + 1, here, width, channels), BF16)] * shards,
        [halo, *scalar, pltpu.VMEM((shards, outs + 1, here, width, channels), BF16)],
    )(valid_from, normed, partial, inner, outer, gain, spatial_weight, temporal_weight)

    half = channels // 2
    pre_gradient, inner, outer, *low = call(
        functools.partial(middle_kernel, **sizes, shards=shards),
        [
            ((rows, frames, width, channels), BF16),
            edge,
            edge,
            ((SPLIT * channels, half), F32),
            ((SPLIT * channels, half), BF16),
        ],
        [pltpu.VMEM((outs + 3, shards, here * width, channels), BF16)],
        flops=20 * cells * channels * channels,
        moved=6 * 1024 * 1024,
    )(
        tall, slope, active, parts, temporal_weight, mix_weight, cotangent[0],
        *reversed(pieces),
    )

    high = call(
        functools.partial(spatial_kernel, **sizes),
        [((size * channels, half), dtype) for size in (15 - SPLIT,) for dtype in (F32, BF16)],
        flops=16 * cells * channels * channels,
        moved=6 * 1024 * 1024,
    )(tall, pre_gradient)

    def shapes(rows_in, *types):
        return [((rows_in, half), dtype) for dtype in types]

    def spread_rows(chunk):
        keep, send = chunk
        got = pair(send, "cam", 1)
        size = keep.shape[0] // lines
        kept, *sends = call(deal_kernel, shapes(size, F32, *[BF16] * (lines - 1)))(
            keep.reshape(lines, size, half), got.reshape(lines, size, half)
        )
        return [kept] + pairs(sends, "height")[::-1]

    def halved(pieces):
        size = pieces[0].shape[0] // 2
        kept, send = call(halve_kernel, shapes(size, F32, BF16))(
            *[piece.reshape(2, size, half) for piece in pieces]
        )
        return (kept, pair(send, "tm", 1))

    def added(values):
        (total,) = call(add_kernel, shapes(values[0].shape[0], BF16))(*values)
        return total

    def doubled(values):
        total = added(values)
        for step in range(1, shards.bit_length() - 1):
            if step > 1:
                total = added((total, other))
            other = pair(total, "tm", 1 << step)
        return (total, other)

    def regained(values):
        total = added(values)
        return (total, pair(total, "tm", 1))

    def whole(values, axis, step):
        size = values[0].shape[0]
        (total,) = call(
            functools.partial(whole_kernel, axis=axis, step=step), [((2, size, half), BF16)]
        )(*values)
        return total.reshape(2 * size, half)

    def gathered(values):
        total = whole(values, "tm", 0)
        return [total] + pairs([total] * (lines - 1), "height")

    def joined(pieces):
        size = pieces[0].shape[0]
        (total,) = call(join_kernel, [((lines, size, half), BF16)])(*pieces)
        return total.reshape(lines * size, half)

    low = spread_rows(low)
    high = spread_rows(high)
    strided = [strided[0]] + pairs(strided[1:], "tm")
    low[0], *strided = together(low[0], *strided)
    low = list(halved(low))
    high[0], *low = together(high[0], *low)
    low = list(doubled(low))
    high = list(halved(high))
    high[0], inner, outer = together(high[0], inner, outer)
    inner, outer = neighbours(inner, outer, "height")
    low[0], *high = together(low[0], *high)
    high = list(doubled(high))
    low = list(regained(low))
    (halo_rows,) = call(halo_kernel, [((2, frames, width, channels), BF16)])(inner, outer)
    low[0], halo_rows, *high = together(low[0], halo_rows, *high)
    high = list(regained(high))
    low = gathered(low)
    high = [whole(high, "tm", 0)]
    for step in range(lines.bit_length() - 1):
        if step:
            high = [whole(high, "height", step - 1)]
        high.append(pair(high[0], "height", 1 << step))
    (video_gradient,) = call(
        functools.partial(input_kernel, **sizes),
        [((frames, rows, width, channels), BF16)],
        [pltpu.VMEM((cells, 3 * channels), BF16)] + scalar,
        flops=18 * cells * channels * channels,
        moved=4 * 1024 * 1024,
    )(valid_from, video, pre_gradient, halo_rows, gain, spatial_weight)
    (encoded,) = call(
        functools.partial(encode_kernel, width=width, shards=shards),
        [((shards * outs, here, width, channels), BF16)],
        [
            pltpu.VMEM(((shards * outs + 2) * here * width, channels), BF16),
            pltpu.VMEM((shards, outs + 1, here, width, channels), BF16),
        ],
        flops=3 * cells * channels * channels,
        moved=2 * 1024 * 1024,
    )(mix_weight, *strided)
    low[0], video_gradient, encoded, *high = together(low[0], video_gradient, encoded, *high)
    low = joined(low)
    high = whole(high, "height", lines.bit_length() - 2)
    other = [pair(low, "cam", 1), pair(high, "cam", 1)]

    cell_count = cells * lax.axis_size("cam") * shards * lines
    scale = 1.0 / math.sqrt(cell_count)
    results = [((9, channels, channels), F32)] + [((3, channels, channels), F32)] * 2
    scratch = [pltpu.VMEM((15, channels, half), F32), pltpu.SemaphoreType.DMA((15,))]
    *results_own, total = call(
        functools.partial(finish_kernel, scale=scale, last=False),
        results + [((channels, half), F32)],
        scratch,
        moved=4 * 1024 * 1024,
        far=3,
    )(low, high, spatial_weight)
    spatial, temporal, mix, gain_gradient = call(
        functools.partial(finish_kernel, scale=scale, last=True),
        results + [((1, channels), F32)],
        scratch,
        moved=4 * 1024 * 1024,
        far=3,
        aliases={5: 0, 6: 1, 7: 2},
    )(*other, spatial_weight, total, gain, *results_own)

    return (
        encoded[None],
        video_gradient[None],
        spatial.reshape(spatial_weight.shape),
        temporal,
        mix,
        gain_gradient.reshape(channels),
    )


def solution(mesh):
    return jax.shard_map(
        on_device,
        mesh=mesh,
        in_specs=(
            P("cam", "tm", "height", None, None),
            P("cam"),
            P(),
            P(),
            P(),
            P(),
            P("cam", None, ("height", "tm"), None, None),
        ),
        out_specs=(
            P("cam", None, ("height", "tm"), None, None),
            P("cam", "tm", "height", None, None),
            P(),
            P(),
            P(),
            P(),
        ),
        check_vma=False,
    )
```

```python
import functools
import math

import jax
import jax.numpy as jnp
from jax import lax
from jax.experimental import pallas as pl
from jax.experimental.pallas import tpu as pltpu
from jax.sharding import PartitionSpec as P

F32 = jnp.float32
BF16 = jnp.bfloat16
VMEM_LIMIT = 16 * 1024 * 1024
SPLIT = 8


def dot(left, right):
    return jnp.dot(left, right, preferred_element_type=F32)


def dot_nt(left, right):
    return lax.dot_general(left, right, (((1,), (1,)), ((), ())), preferred_element_type=F32)


def dot_tn(left, right):
    return lax.dot_general(left, right, (((0,), (0,)), ((), ())), preferred_element_type=F32)


def from_left(cells, width):
    column = lax.broadcasted_iota(jnp.int32, cells.shape, 0) % width
    return jnp.where(column == 0, 0.0, pltpu.roll(cells, 1, 0))


def from_right(cells, width):
    column = lax.broadcasted_iota(jnp.int32, cells.shape, 0) % width
    return jnp.where(column == width - 1, 0.0, pltpu.roll(cells, cells.shape[0] - 1, 0))


def present(start, frame, frames):
    return (lax.axis_index("tm") * frames + frame >= start[0]).astype(F32)


def normalised(tile, keep):
    values = tile.astype(F32) * keep
    inverse = lax.rsqrt(jnp.mean(values * values, axis=-1, keepdims=True) + 1e-06)
    return (values * inverse, inverse)


def first_frame(shard, outs, span, total):
    return jnp.minimum(shard * outs, total - span)


def run_copies(pairs_of_refs, done):
    copies = [
        pltpu.make_async_copy(source, target, done.at[at])
        for at, (source, target) in enumerate(pairs_of_refs)
    ]
    for copy in copies:
        copy.start()
    for copy in copies:
        copy.wait()


def pieces_kernel(cotangent, *refs, outs):
    pieces, done = (refs[:-1], refs[-1])
    span = outs + 3
    me = lax.axis_index("tm")
    copies = []
    for step, piece in enumerate(pieces):
        begin = first_frame(me ^ (step + 1), outs, span, cotangent.shape[0])
        copies.append((cotangent.at[pl.ds(begin, span)], piece))
    run_copies(copies, done)


def edges_kernel(video, inner, outer, done, *, rows):
    odd = lax.axis_index("height") % 2
    run_copies(
        [
            (video.at[:, (1 - odd) * (rows - 1)], inner),
            (video.at[:, odd * (rows - 1)], outer),
        ],
        done,
    )


def first_frame(shard, outs, span, total):
    return jnp.minimum(shard * outs, total - span)


def place_halos(halo, inner, outer):
    odd = lax.axis_index("height") % 2
    halo[1 - odd] = inner[...]
    halo[odd] = outer[...]


def column_sum(cells, weight, taps, width):
    products = [
        dot(cells, jnp.concatenate([weight[i, j] for i in taps], axis=0)) for j in range(3)
    ]
    return from_left(products[0], width) + products[1] + from_right(products[2], width)


def halo_kernel(inner, outer, halo):
    place_halos(halo, inner, outer)


def own_kernel(
    valid_from, video, gain, weight, normed, partial, start, done, *, frames, rows, width
):
    run_copies([(valid_from, start)], done)
    block = frames * width
    for row in range(rows):
        for frame in range(frames):
            unit, _ = normalised(video[frame, row], present(start, frame, frames))
            at = row * block + frame * width
            normed[at : at + width] = (unit * gain[...]).astype(BF16)
    for row in range(rows):
        taps = [i for i in range(3) if 0 <= row + i - 1 < rows]
        cells = [normed[(row + i - 1) * block : (row + i) * block] for i in taps]
        partial[row * block : row * block + block] = column_sum(
            jnp.concatenate(cells, axis=1), weight, taps, width
        )


def front_kernel(
    valid_from, normed, partial, inner, outer, gain, weight, temporal, *refs,
    frames, rows, width, shards
):
    tall, slope, active, parts, *refs = refs
    strided, (halo, start, done, lines) = (refs[:shards], refs[shards:])
    outs = frames // 2
    plane = rows * width
    here = rows // shards
    block = frames * width

    run_copies([(valid_from, start)], done)
    place_halos(halo, inner, outer)
    tall[block : block + rows * block] = normed[...]
    for side, at in ((0, 0), (1, (rows + 1) * block)):
        for frame in range(frames):
            unit, _ = normalised(halo[side, frame], present(start, frame, frames))
            to = at + frame * width
            tall[to : to + width] = (unit * gain[...]).astype(BF16)
    for row in range(rows):
        pre = partial[row * block : row * block + block]
        if row == 0:
            pre = pre + column_sum(tall[:block], weight, [0], width)
        if row == rows - 1:
            pre = pre + column_sum(tall[(rows + 1) * block :], weight, [2], width)
        sigmoid = 1.0 / (1.0 + jnp.exp(-pre))
        slope[row * block : row * block + block] = sigmoid * (1.0 + pre * (1.0 - sigmoid))
        cells = (pre * sigmoid).astype(BF16)
        for frame in range(frames):
            at = (frame // 2) * plane + row * width
            active[frame % 2, at : at + width] = cells[frame * width : frame * width + width]
    evens = active[0]
    odds = active[1]
    carried = dot(odds, temporal[2])
    mixed = dot(odds, temporal[0]) + dot(evens, temporal[1])
    pieces = [mixed[:plane]]
    for s in range(1, outs):
        pieces.append(
            mixed[s * plane : s * plane + plane] + carried[(s - 1) * plane : s * plane]
        )
    pieces.append(carried[(outs - 1) * plane :])
    pieces = jnp.concatenate(pieces, axis=0).astype(BF16)
    parts[...] = pieces
    for frame in range(outs + 1):
        cells = pieces[frame * plane : frame * plane + plane]
        lines[:, frame] = cells.reshape(shards, here, width, 256)
    for step, piece in enumerate(strided):
        piece[...] = lines[lax.axis_index("tm") ^ step]


def middle_kernel(
    tall, slope, active, parts, temporal, mix, cotangent, *refs, frames, rows, width, shards
):
    pieces, refs = (refs[: shards - 1], refs[shards - 1 :])
    pre_gradient, inner_out, outer_out, keep, send, cot = refs
    outs = frames // 2
    plane = rows * width
    here = rows // shards
    me = lax.axis_index("tm")
    total = shards * outs
    cut = outs + 3
    skip = me * outs - first_frame(me, outs, cut, total)
    for frame in range(cut):
        here_is = (me * outs + frame < total).astype(F32)
        own = cotangent[jnp.minimum(me * outs + frame, total - 1)]
        others = [piece[jnp.minimum(frame + skip, cut - 1)] for piece in pieces]
        for step, cells in enumerate([own] + others[::-1]):
            cells = (cells.astype(F32) * here_is).astype(BF16)
            cot[frame, me ^ step] = cells.reshape(here * width, 256)

    def ahead(k, count=outs + 1):
        return cot[k : k + count].reshape(count * plane, 256)

    gradient = ahead(0).astype(F32)
    for k in range(3):
        gradient = gradient + dot_nt(ahead(k), mix[k])
    gradient = gradient.astype(BF16)
    now = gradient[: outs * plane]
    later = gradient[plane:]
    even_gradient = dot_nt(now, temporal[1])
    odd_gradient = dot_nt(now, temporal[0]) + dot_nt(later, temporal[2])
    for row in range(rows):
        for frame in range(frames):
            source = odd_gradient if frame % 2 else even_gradient
            at = (frame // 2) * plane + row * width
            to = (row * frames + frame) * width
            tile = (source[at : at + width] * slope[to : to + width]).astype(BF16)
            pre_gradient[row, frame] = tile
    side = (lax.axis_index("height") % 2) * (rows - 1)
    inner_out[...] = pre_gradient[rows - 1 - side]
    outer_out[...] = pre_gradient[side]
    evens = active[0]
    odds = active[1]
    for k in range(3):
        deliver(keep, send, k, dot_tn(parts[...], ahead(k)))
    deliver(keep, send, 3, dot_tn(odds, now))
    deliver(keep, send, 4, dot_tn(evens, now))
    deliver(keep, send, 5, dot_tn(odds, later))
    block = frames * width
    spatial_sums(tall, pre_gradient, keep, send, 6, range(SPLIT - 6), block, rows, width)


def spatial_kernel(tall, pre_gradient, keep, send, *, frames, rows, width):
    block = frames * width
    spatial_sums(tall, pre_gradient, keep, send, 0, range(SPLIT - 6, 9), block, rows, width)


def spatial_sums(tall, pre_gradient, keep, send, first, taps, block, rows, width):
    columns = column_shifts(pre_gradient, width)
    for i in range(3):
        here = [tap for tap in taps if tap // 3 == i]
        if not here:
            continue
        cells = tall[i * block : (i + rows) * block]
        product = dot_tn(cells, jnp.concatenate([columns[tap % 3] for tap in here], axis=1))
        for place, tap in enumerate(here):
            index = first + tap - taps[0]
            deliver(keep, send, index, product[:, place * 256 : place * 256 + 256])


def column_shifts(pre_gradient, width):
    gradient = pre_gradient[...].reshape(-1, 256)
    exact = gradient.astype(F32)
    left = from_right(exact, width).astype(BF16)
    right = from_left(exact, width).astype(BF16)
    return [left, gradient, right]


def deliver(keep, send, index, product):
    first = jnp.full((256, 128), lax.axis_index("cam")) == 0
    low, high = (product[:, :128], product[:, 128:])
    at = index * 256
    keep[at : at + 256] = jnp.where(first, low, high)
    send[at : at + 256] = jnp.where(first, high, low).astype(BF16)


def core_columns():
    mine = pl.ds(pl.multiple_of(lax.axis_index("cam") * 128, 128), 128)
    other = pl.ds(pl.multiple_of((1 - lax.axis_index("cam")) * 128, 128), 128)
    return (mine, other)


def deal_kernel(low, low_got, high, high_got, kept, *sends):
    me = lax.axis_index("height")
    cut = low.shape[1]

    def fill(target, at):
        target[:cut] = (low[at] + low_got[at].astype(F32)).astype(target.dtype)
        target[cut:] = (high[at] + high_got[at].astype(F32)).astype(target.dtype)

    fill(kept, me)
    for step, send in enumerate(sends):
        fill(send, me ^ (step + 1))


def halve_kernel(*refs):
    (kept_in, *received), (kept, send) = (refs[:-2], refs[-2:])
    mine = lax.axis_index("tm") % 2

    def total(at):
        value = kept_in[at]
        for piece in received:
            value = value + piece[at].astype(F32)
        return value

    kept[...] = total(mine)
    send[...] = total(1 - mine).astype(BF16)


def add_kernel(left, right, out):
    out[...] = (left[...].astype(F32) + right[...].astype(F32)).astype(BF16)


def whole_kernel(mine, other, out, *, axis, step):
    at = (lax.axis_index(axis) >> step) % 2
    out[at] = mine[...]
    out[1 - at] = other[...]


def input_kernel(
    valid_from, video, pre_gradient, halo, gain, weight, out, tall, start, done,
    *, frames, rows, width
):
    run_copies([(valid_from, start)], done)
    block = frames * width
    for row in range(-1, rows + 1):
        if row < 0:
            cells = halo[0]
        elif row == rows:
            cells = halo[1]
        else:
            cells = pre_gradient[row]
        cells = cells.reshape(block, 256)
        for tap in range(3):
            target = row - 1 + tap
            if 0 <= target < rows:
                tall[target * block : target * block + block, tap * 256 : tap * 256 + 256] = cells
    for row in range(rows):
        cells = tall[row * block : row * block + block]
        taps = [
            dot_nt(cells, jnp.concatenate([weight[0, j], weight[1, j], weight[2, j]], axis=1))
            for j in range(3)
        ]
        gradient = from_right(taps[0], width) + taps[1] + from_left(taps[2], width)
        gradient = gradient * gain[...]
        for frame in range(frames):
            keep = present(start, frame, frames)
            unit, inverse = normalised(video[frame, row], keep)
            tile = gradient[frame * width : frame * width + width]
            mean = jnp.mean(tile * unit, axis=-1, keepdims=True)
            out[frame, row] = (inverse * (tile - unit * mean) * keep).astype(BF16)


def encode_kernel(mix, *refs, width, shards):
    pieces, (out, line, strided) = (refs[:shards], refs[shards:])
    for step, piece in enumerate(pieces):
        strided[lax.axis_index("tm") ^ step] = piece[...]
    parts, here = strided.shape[1:3]
    outs = parts - 1
    plane = here * width
    total = shards * outs
    for frame in range(total):
        shard, part = (frame // outs, frame % outs)
        cells = strided[shard, part].reshape(plane, 256)
        if part == 0 and shard > 0:
            carried = strided[shard - 1, outs].reshape(plane, 256)
            cells = (cells.astype(F32) + carried.astype(F32)).astype(BF16)
        line[(frame + 2) * plane : (frame + 3) * plane] = cells
    line[0 : 2 * plane] = jnp.zeros((2 * plane, 256), BF16)
    span = total * plane
    result = line[2 * plane : 2 * plane + span].astype(F32)
    for k in range(3):
        result = result + dot(line[(2 - k) * plane : (2 - k) * plane + span], mix[k])
    out[...] = result.astype(BF16).reshape(out.shape)


def finish_kernel(*refs, scale, parts, last):
    (pieces, weight, refs) = (refs[:parts], refs[parts], refs[parts + 1 :])
    if last:
        before, gain, _, _, _, spatial, temporal, mix, gain_out, staged, row, done = refs
        total = before[...]
    else:
        spatial, temporal, mix, after, staged, done = refs
        total = jnp.zeros((256, 128), F32)
    columns = core_columns()[1 if last else 0]
    low, high = (SPLIT * 256 // parts, (15 - SPLIT) * 256 // parts)
    for step, piece in enumerate(pieces):
        part = lax.axis_index("height") ^ step
        at = pl.multiple_of(part * low, low)
        staged[pl.ds(at, low)] = piece[:low].astype(F32) * scale
        at = pl.multiple_of(SPLIT * 256 + part * high, high)
        staged[pl.ds(at, high)] = piece[low:].astype(F32) * scale
    results = [(mix, k) for k in range(3)] + [(temporal, k) for k in range(3)]
    results = results + [(spatial, k) for k in range(9)]
    copies = []
    for index, (result, k) in enumerate(results):
        cells = staged.at[pl.ds(index * 256, 256)]
        copies.append(pltpu.make_async_copy(cells, result.at[k, :, columns], done.at[index]))
        copies[-1].start()
    for k in range(9):
        cells = staged[1536 + k * 256 : 1792 + k * 256]
        total = total + cells * weight[k // 3, k % 3, :, columns].astype(F32)
    if last:
        upper = total.astype(BF16)
        lower = (total - upper.astype(F32)).astype(BF16)
        ones = jnp.ones((16, 128), BF16)
        row[...] = (dot_nt(ones, upper) + dot_nt(ones, lower))[:1] / gain[...]
        copies.append(pltpu.make_async_copy(row, gain_out, done.at[15]))
        copies[-1].start()
    else:
        after[...] = total
    for copy in copies:
        copy.wait()


def call(kernel, outs, scratch=(), flops=0, moved=0, aliases=None, far=0):
    where = pl.BlockSpec(memory_space=pltpu.VMEM)

    def run(*operands):
        results = pl.pallas_call(
            kernel,
            out_shape=[jax.ShapeDtypeStruct(shape, dtype) for shape, dtype in outs],
            in_specs=[
                pl.BlockSpec(memory_space=pltpu.HBM)
                if a.dtype == jnp.int32 or at in (aliases or ())
                else where
                for at, a in enumerate(operands)
            ],
            out_specs=[pl.BlockSpec(memory_space=pltpu.HBM)] * far + [where] * (len(outs) - far),
            input_output_aliases=aliases or {},
            scratch_shapes=list(scratch),
            compiler_params=pltpu.CompilerParams(vmem_limit_bytes=VMEM_LIMIT),
            cost_estimate=pl.CostEstimate(flops=flops, bytes_accessed=moved, transcendentals=0),
        )(*operands)
        return list(results)

    return run


def neighbours(inner, outer, axis):
    size = lax.axis_size(axis)
    links = [(i, i + 1) for i in range(1, size - 1, 2)]
    links = links + [(j, i) for i, j in links]
    return (pair(inner, axis, 1), lax.ppermute(outer, axis, links))


def pair(array, axis, step):
    return lax.ppermute(array, axis, [(i, i ^ step) for i in range(lax.axis_size(axis))])


def pairs(arrays, axis):
    return [pair(array, axis, step + 1) for step, array in enumerate(arrays)]


def together(*values):
    return lax.optimization_barrier(values)


def on_device(
    video_clip, valid_from, norm_gain, spatial_weight, temporal_weight, mix_weight, cotangent
):
    video = video_clip[0]
    frames, rows, width, channels = video.shape
    outs = frames // 2
    shards = lax.axis_size("tm")
    lines = lax.axis_size("height")
    here = rows // shards
    cells = frames * rows * width
    sizes = dict(frames=frames, rows=rows, width=width)
    gain = norm_gain.reshape(1, channels)
    edge = ((frames, width, channels), BF16)
    halo = pltpu.VMEM((2, frames, width, channels), BF16)

    scalar = [pltpu.SMEM((1,), jnp.int32), pltpu.SemaphoreType.DMA((1,))]
    pieces = call(
        functools.partial(pieces_kernel, outs=outs),
        [((outs + 3, here, width, channels), BF16)] * (shards - 1),
        [pltpu.SemaphoreType.DMA((shards - 1,))],
        moved=1024 * 1024,
    )(cotangent[0])
    *pieces, edges = together(*pieces, video)
    pieces = pairs(pieces, "tm")
    inner, outer = call(
        functools.partial(edges_kernel, rows=rows),
        [edge, edge],
        [pltpu.SemaphoreType.DMA((2,))],
        moved=512 * 1024,
    )(edges)
    inner, outer = neighbours(inner, outer, "height")

    normed, partial = call(
        functools.partial(own_kernel, **sizes),
        [((cells, channels), BF16), ((cells, channels), F32)],
        scalar,
        flops=18 * cells * channels * channels,
        moved=4 * 1024 * 1024,
    )(valid_from, video, gain, spatial_weight)

    tall, slope, active, parts, *strided = call(
        functools.partial(front_kernel, **sizes, shards=shards),
        [
            ((cells + 2 * frames * width, channels), BF16),
            ((cells, channels), F32),
            ((2, cells // 2, channels), BF16),
            (((outs + 1) * rows * width, channels), BF16),
        ]
        + [((outs + 1, here, width, channels), BF16)] * shards,
        [halo, *scalar, pltpu.VMEM((shards, outs + 1, here, width, channels), BF16)],
    )(valid_from, normed, partial, inner, outer, gain, spatial_weight, temporal_weight)

    half = channels // 2
    pre_gradient, inner, outer, *low = call(
        functools.partial(middle_kernel, **sizes, shards=shards),
        [
            ((rows, frames, width, channels), BF16),
            edge,
            edge,
            ((SPLIT * channels, half), F32),
            ((SPLIT * channels, half), BF16),
        ],
        [pltpu.VMEM((outs + 3, shards, here * width, channels), BF16)],
        flops=20 * cells * channels * channels,
        moved=6 * 1024 * 1024,
    )(
        tall, slope, active, parts, temporal_weight, mix_weight, cotangent[0],
        *reversed(pieces),
    )

    high = call(
        functools.partial(spatial_kernel, **sizes),
        [((size * channels, half), dtype) for size in (15 - SPLIT,) for dtype in (F32, BF16)],
        flops=16 * cells * channels * channels,
        moved=6 * 1024 * 1024,
    )(tall, pre_gradient)

    def shapes(rows_in, *types):
        return [((rows_in, half), dtype) for dtype in types]

    def halved(pieces):
        size = pieces[0].shape[0] // 2
        kept, send = call(halve_kernel, shapes(size, F32, BF16))(
            *[piece.reshape(2, size, half) for piece in pieces]
        )
        return (kept, pair(send, "tm", 1))

    def added(values):
        (total,) = call(add_kernel, shapes(values[0].shape[0], BF16))(*values)
        return total

    def doubled(total):
        for step in range(1, shards.bit_length() - 1):
            if step > 1:
                total = added((total, other))
            other = pair(total, "tm", 1 << step)
        return (total, other)

    def regained(values):
        total = added(values)
        return (total, pair(total, "tm", 1))

    def whole(values, axis, step):
        size = values[0].shape[0]
        (total,) = call(
            functools.partial(whole_kernel, axis=axis, step=step), [((2, size, half), BF16)]
        )(*values)
        return total.reshape(2 * size, half)

    def gathered(values):
        total = whole(values, "tm", 0)
        return [total] + pairs([total] * (lines - 1), "height")

    (low, low_send), (high, high_send) = (low, high)
    low_got = pair(low_send, "cam", 1)
    high_got = pair(high_send, "cam", 1)
    kept, *sends = call(deal_kernel, shapes(15 * channels // lines, F32, *[BF16] * (lines - 1)))(
        *[a.reshape(lines, -1, half) for a in (low, low_got, high, high_got)]
    )
    received = pairs(sends, "height")
    kept, *far = together(kept, *strided[2:])
    strided = strided[:2] + far
    strided = [strided[0]] + pairs(strided[1:], "tm")
    kept, *strided = together(kept, *strided)
    first = added(halved([kept] + received[::-1]))
    first, strided[0] = together(first, strided[0])
    (encoded,) = call(
        functools.partial(encode_kernel, width=width, shards=shards),
        [((shards * outs, here, width, channels), BF16)],
        [
            pltpu.VMEM(((shards * outs + 2) * here * width, channels), BF16),
            pltpu.VMEM((shards, outs + 1, here, width, channels), BF16),
        ],
        flops=3 * cells * channels * channels,
        moved=2 * 1024 * 1024,
    )(mix_weight, *strided)
    encoded, inner, outer = together(encoded, inner, outer)
    inner, outer = neighbours(inner, outer, "height")
    (halo_rows,) = call(halo_kernel, [((2, frames, width, channels), BF16)])(inner, outer)
    values = regained(doubled(first))
    values, halo_rows = together(values, halo_rows)
    pieces = gathered(values)
    (video_gradient,) = call(
        functools.partial(input_kernel, **sizes),
        [((frames, rows, width, channels), BF16)],
        [pltpu.VMEM((cells, 3 * channels), BF16)] + scalar,
        flops=18 * cells * channels * channels,
        moved=4 * 1024 * 1024,
    )(valid_from, video, pre_gradient, halo_rows, gain, spatial_weight)
    pieces[-1], video_gradient = together(pieces[-1], video_gradient)
    others = [pair(piece, "cam", 1) for piece in pieces]

    cell_count = cells * lax.axis_size("cam") * shards * lines
    scale = 1.0 / math.sqrt(cell_count)
    results = [((9, channels, channels), F32)] + [((3, channels, channels), F32)] * 2
    staged = pltpu.VMEM((15 * channels, half), F32)
    *results_own, total = call(
        functools.partial(finish_kernel, scale=scale, parts=lines, last=False),
        results + [((channels, half), F32)],
        [staged, pltpu.SemaphoreType.DMA((15,))],
        moved=4 * 1024 * 1024,
        far=3,
    )(*pieces, spatial_weight)
    spatial, temporal, mix, gain_gradient = call(
        functools.partial(finish_kernel, scale=scale, parts=lines, last=True),
        results + [((1, channels), F32)],
        [staged, pltpu.VMEM((1, channels), F32), pltpu.SemaphoreType.DMA((16,))],
        moved=4 * 1024 * 1024,
        far=4,
        aliases={lines + 3 + at: at for at in range(3)},
    )(*others, spatial_weight, total, gain, *results_own)

    return (
        encoded[None],
        video_gradient[None],
        spatial.reshape(spatial_weight.shape),
        temporal,
        mix,
        gain_gradient.reshape(channels),
    )


def solution(mesh):
    return jax.shard_map(
        on_device,
        mesh=mesh,
        in_specs=(
            P("cam", "tm", "height", None, None),
            P("cam"),
            P(),
            P(),
            P(),
            P(),
            P("cam", None, ("height", "tm"), None, None),
        ),
        out_specs=(
            P("cam", None, ("height", "tm"), None, None),
            P("cam", "tm", "height", None, None),
            P(),
            P(),
            P(),
            P(),
        ),
        check_vma=False,
    )
```

```python
import functools
import math

import jax
import jax.numpy as jnp
from jax import lax
from jax.experimental import pallas as pl
from jax.experimental.pallas import tpu as pltpu
from jax.sharding import PartitionSpec as P

F32 = jnp.float32
BF16 = jnp.bfloat16
VMEM_LIMIT = 16 * 1024 * 1024
SPLIT = 8


def dot(left, right):
    return jnp.dot(left, right, preferred_element_type=F32)


def dot_nt(left, right):
    return lax.dot_general(left, right, (((1,), (1,)), ((), ())), preferred_element_type=F32)


def dot_tn(left, right):
    return lax.dot_general(left, right, (((0,), (0,)), ((), ())), preferred_element_type=F32)


def from_left(cells, width):
    column = lax.broadcasted_iota(jnp.int32, cells.shape, 0) % width
    return jnp.where(column == 0, 0.0, pltpu.roll(cells, 1, 0))


def from_right(cells, width):
    column = lax.broadcasted_iota(jnp.int32, cells.shape, 0) % width
    return jnp.where(column == width - 1, 0.0, pltpu.roll(cells, cells.shape[0] - 1, 0))


def present(start, frame, frames):
    return (lax.axis_index("tm") * frames + frame >= start[0]).astype(F32)


def normalised(tile, keep):
    values = tile.astype(F32) * keep
    inverse = lax.rsqrt(jnp.mean(values * values, axis=-1, keepdims=True) + 1e-06)
    return (values * inverse, inverse)


def first_frame(shard, outs, span, total):
    return jnp.minimum(shard * outs, total - span)


def run_copies(pairs_of_refs, done):
    copies = [
        pltpu.make_async_copy(source, target, done.at[at])
        for at, (source, target) in enumerate(pairs_of_refs)
    ]
    for copy in copies:
        copy.start()
    for copy in copies:
        copy.wait()


def pieces_kernel(cotangent, *refs, outs):
    pieces, done = (refs[:-1], refs[-1])
    span = outs + 3
    me = lax.axis_index("tm")
    copies = []
    for step, piece in enumerate(pieces):
        begin = first_frame(me ^ (step + 1), outs, span, cotangent.shape[0])
        copies.append((cotangent.at[pl.ds(begin, span)], piece))
    run_copies(copies, done)


def edges_kernel(source, inner, outer, done, *, rows, frames_first):
    odd = lax.axis_index("height") % 2

    def row(at):
        return source.at[:, at] if frames_first else source.at[at]

    run_copies(
        [(row((1 - odd) * (rows - 1)), inner), (row(odd * (rows - 1)), outer)], done
    )


def first_frame(shard, outs, span, total):
    return jnp.minimum(shard * outs, total - span)


def place_halos(halo, inner, outer):
    odd = lax.axis_index("height") % 2
    halo[1 - odd] = inner[...]
    halo[odd] = outer[...]


def column_sum(cells, weight, taps, width):
    products = [
        dot(cells, jnp.concatenate([weight[i, j] for i in taps], axis=0)) for j in range(3)
    ]
    return from_left(products[0], width) + products[1] + from_right(products[2], width)


def halo_kernel(inner, outer, halo):
    place_halos(halo, inner, outer)


def own_kernel(
    valid_from, video, gain, weight, normed, partial, start, done, *, frames, rows, width
):
    run_copies([(valid_from, start)], done)
    block = frames * width
    for row in range(rows):
        for frame in range(frames):
            unit, _ = normalised(video[frame, row], present(start, frame, frames))
            at = row * block + frame * width
            normed[at : at + width] = (unit * gain[...]).astype(BF16)
    for row in range(rows):
        taps = [i for i in range(3) if 0 <= row + i - 1 < rows]
        cells = [normed[(row + i - 1) * block : (row + i) * block] for i in taps]
        partial[row * block : row * block + block] = column_sum(
            jnp.concatenate(cells, axis=1), weight, taps, width
        )


def front_kernel(
    valid_from, normed, partial, inner, outer, gain, weight, temporal, *refs,
    frames, rows, width, shards
):
    tall, slope, active, parts, *refs = refs
    strided, (halo, start, done, lines) = (refs[:2], refs[2:])
    outs = frames // 2
    plane = rows * width
    here = rows // shards
    block = frames * width

    run_copies([(valid_from, start)], done)
    place_halos(halo, inner, outer)
    tall[block : block + rows * block] = normed[...]
    for side, at in ((0, 0), (1, (rows + 1) * block)):
        for frame in range(frames):
            unit, _ = normalised(halo[side, frame], present(start, frame, frames))
            to = at + frame * width
            tall[to : to + width] = (unit * gain[...]).astype(BF16)
    for row in range(rows):
        pre = partial[row * block : row * block + block]
        if row == 0:
            pre = pre + column_sum(tall[:block], weight, [0], width)
        if row == rows - 1:
            pre = pre + column_sum(tall[(rows + 1) * block :], weight, [2], width)
        sigmoid = 1.0 / (1.0 + jnp.exp(-pre))
        slope[row * block : row * block + block] = sigmoid * (1.0 + pre * (1.0 - sigmoid))
        cells = (pre * sigmoid).astype(BF16)
        for frame in range(frames):
            at = (frame // 2) * plane + row * width
            active[frame % 2, at : at + width] = cells[frame * width : frame * width + width]
    evens = active[0]
    odds = active[1]
    carried = dot(odds, temporal[2])
    mixed = dot(odds, temporal[0]) + dot(evens, temporal[1])
    pieces = [mixed[:plane]]
    for s in range(1, outs):
        pieces.append(
            mixed[s * plane : s * plane + plane] + carried[(s - 1) * plane : s * plane]
        )
    pieces.append(carried[(outs - 1) * plane :])
    pieces = jnp.concatenate(pieces, axis=0).astype(BF16)
    parts[...] = pieces
    for frame in range(outs + 1):
        cells = pieces[frame * plane : frame * plane + plane]
        lines[:, frame] = cells.reshape(shards, here, width, 256)
    stay, leave = strided
    for step in range(shards):
        target = leave if step % 2 else stay
        target[0, step // 2] = lines[lax.axis_index("tm") ^ step]


def split_kernel(stay_in, came_in, stay, leave):
    count, pieces = stay_in.shape[:2]
    for place, source in enumerate((stay_in, came_in)):
        for at in range(count):
            for piece in range(pieces):
                target = leave if piece % 2 else stay
                target[place * count + at, piece // 2] = source[at, piece]


def middle_kernel(
    tall, slope, active, parts, temporal, mix, cotangent, *refs, frames, rows, width, shards
):
    pieces, refs = (refs[: shards - 1], refs[shards - 1 :])
    pre_gradient, keep, send, cot = refs
    outs = frames // 2
    plane = rows * width
    here = rows // shards
    me = lax.axis_index("tm")
    total = shards * outs
    cut = outs + 3
    skip = me * outs - first_frame(me, outs, cut, total)
    for frame in range(cut):
        here_is = (me * outs + frame < total).astype(F32)
        own = cotangent[jnp.minimum(me * outs + frame, total - 1)]
        others = [piece[jnp.minimum(frame + skip, cut - 1)] for piece in pieces]
        for step, cells in enumerate([own] + others[::-1]):
            cells = (cells.astype(F32) * here_is).astype(BF16)
            cot[frame, me ^ step] = cells.reshape(here * width, 256)

    def ahead(k, count=outs + 1):
        return cot[k : k + count].reshape(count * plane, 256)

    gradient = ahead(0).astype(F32)
    for k in range(3):
        gradient = gradient + dot_nt(ahead(k), mix[k])
    gradient = gradient.astype(BF16)
    now = gradient[: outs * plane]
    later = gradient[plane:]
    even_gradient = dot_nt(now, temporal[1])
    odd_gradient = dot_nt(now, temporal[0]) + dot_nt(later, temporal[2])
    for row in range(rows):
        for frame in range(frames):
            source = odd_gradient if frame % 2 else even_gradient
            at = (frame // 2) * plane + row * width
            to = (row * frames + frame) * width
            tile = (source[at : at + width] * slope[to : to + width]).astype(BF16)
            pre_gradient[row, frame] = tile
    evens = active[0]
    odds = active[1]
    for k in range(3):
        deliver(keep, send, k, dot_tn(parts[...], ahead(k)))
    deliver(keep, send, 3, dot_tn(odds, now))
    deliver(keep, send, 4, dot_tn(evens, now))
    deliver(keep, send, 5, dot_tn(odds, later))
    block = frames * width
    spatial_sums(tall, pre_gradient, keep, send, 6, range(SPLIT - 6), block, rows, width)


def spatial_kernel(tall, pre_gradient, keep, send, *, frames, rows, width):
    block = frames * width
    spatial_sums(tall, pre_gradient, keep, send, 0, range(SPLIT - 6, 9), block, rows, width)


def spatial_sums(tall, pre_gradient, keep, send, first, taps, block, rows, width):
    columns = column_shifts(pre_gradient, width)
    for i in range(3):
        here = [tap for tap in taps if tap // 3 == i]
        if not here:
            continue
        cells = tall[i * block : (i + rows) * block]
        product = dot_tn(cells, jnp.concatenate([columns[tap % 3] for tap in here], axis=1))
        for place, tap in enumerate(here):
            index = first + tap - taps[0]
            deliver(keep, send, index, product[:, place * 256 : place * 256 + 256])


def column_shifts(pre_gradient, width):
    gradient = pre_gradient[...].reshape(-1, 256)
    exact = gradient.astype(F32)
    left = from_right(exact, width).astype(BF16)
    right = from_left(exact, width).astype(BF16)
    return [left, gradient, right]


def deliver(keep, send, index, product):
    first = jnp.full((256, 128), lax.axis_index("cam")) == 0
    low, high = (product[:, :128], product[:, 128:])
    at = index * 256
    keep[at : at + 256] = jnp.where(first, low, high)
    send[at : at + 256] = jnp.where(first, high, low).astype(BF16)


def core_columns():
    mine = pl.ds(pl.multiple_of(lax.axis_index("cam") * 128, 128), 128)
    other = pl.ds(pl.multiple_of((1 - lax.axis_index("cam")) * 128, 128), 128)
    return (mine, other)


def deal_kernel(low, low_got, high, high_got, *outs):
    me = lax.axis_index("height")
    home = lax.axis_index("tm") % 2
    cut = low.shape[2]
    count = len(outs) // 2
    for target, half in [(outs[:count], 1 - home), (outs[count:], home)]:
        for step, out in enumerate(target):
            at = me ^ step
            out[:cut] = (low[at, half] + low_got[at, half].astype(F32)).astype(out.dtype)
            out[cut:] = (high[at, half] + high_got[at, half].astype(F32)).astype(out.dtype)


def gather_sum_kernel(kept, *refs):
    value = kept[...]
    for piece in refs[:-1]:
        value = value + piece[...].astype(F32)
    refs[-1][...] = value.astype(BF16)


def add_kernel(left, right, out):
    out[...] = (left[...].astype(F32) + right[...].astype(F32)).astype(BF16)


def join_kernel(*refs):
    for step, piece in enumerate(refs[:-1]):
        refs[-1][lax.axis_index("height") ^ step] = piece[...]


def input_kernel(
    valid_from, video, pre_gradient, halo, gain, weight, out, tall, start, done,
    *, frames, rows, width
):
    run_copies([(valid_from, start)], done)
    block = frames * width
    for row in range(-1, rows + 1):
        if row < 0:
            cells = halo[0]
        elif row == rows:
            cells = halo[1]
        else:
            cells = pre_gradient[row]
        cells = cells.reshape(block, 256)
        for tap in range(3):
            target = row - 1 + tap
            if 0 <= target < rows:
                tall[target * block : target * block + block, tap * 256 : tap * 256 + 256] = cells
    for row in range(rows):
        cells = tall[row * block : row * block + block]
        taps = [
            dot_nt(cells, jnp.concatenate([weight[0, j], weight[1, j], weight[2, j]], axis=1))
            for j in range(3)
        ]
        gradient = from_right(taps[0], width) + taps[1] + from_left(taps[2], width)
        gradient = gradient * gain[...]
        for frame in range(frames):
            keep = present(start, frame, frames)
            unit, inverse = normalised(video[frame, row], keep)
            tile = gradient[frame * width : frame * width + width]
            mean = jnp.mean(tile * unit, axis=-1, keepdims=True)
            out[frame, row] = (inverse * (tile - unit * mean) * keep).astype(BF16)


def encode_kernel(mix, stay, came, out, line, strided, *, width, shards):
    for step in range(shards):
        source = came if step >= shards // 2 else stay
        strided[lax.axis_index("tm") ^ step] = source[step % (shards // 2), 0]
    parts, here = strided.shape[1:3]
    outs = parts - 1
    plane = here * width
    total = shards * outs
    for frame in range(total):
        shard, part = (frame // outs, frame % outs)
        cells = strided[shard, part].reshape(plane, 256)
        if part == 0 and shard > 0:
            carried = strided[shard - 1, outs].reshape(plane, 256)
            cells = (cells.astype(F32) + carried.astype(F32)).astype(BF16)
        line[(frame + 2) * plane : (frame + 3) * plane] = cells
    line[0 : 2 * plane] = jnp.zeros((2 * plane, 256), BF16)
    span = total * plane
    result = line[2 * plane : 2 * plane + span].astype(F32)
    for k in range(3):
        result = result + dot(line[(2 - k) * plane : (2 - k) * plane + span], mix[k])
    out[...] = result.astype(BF16).reshape(out.shape)


def finish_kernel(home, away, weight, *refs, scale, last):
    if last:
        before, gain, _, _, _, spatial, temporal, mix, gain_out, staged, row, done = refs
        total = before[...]
    else:
        spatial, temporal, mix, after, staged, done = refs
        total = jnp.zeros((256, 128), F32)
    columns = core_columns()[1 if last else 0]
    parts = home.shape[0]
    low, high = (SPLIT * 128 // parts, (15 - SPLIT) * 128 // parts)
    mine = lax.axis_index("tm") % 2
    for half, source in ((mine, home), (1 - mine, away)):
        for part in range(parts):
            at = pl.multiple_of((2 * part + half) * low, low)
            staged[pl.ds(at, low)] = source[part, :low].astype(F32) * scale
            at = pl.multiple_of(SPLIT * 256 + (2 * part + half) * high, high)
            staged[pl.ds(at, high)] = source[part, low:].astype(F32) * scale
    results = [(mix, k) for k in range(3)] + [(temporal, k) for k in range(3)]
    results = results + [(spatial, k) for k in range(9)]
    copies = []
    for index, (result, k) in enumerate(results):
        cells = staged.at[pl.ds(index * 256, 256)]
        copies.append(pltpu.make_async_copy(cells, result.at[k, :, columns], done.at[index]))
        copies[-1].start()
    for k in range(9):
        cells = staged[1536 + k * 256 : 1792 + k * 256]
        total = total + cells * weight[k // 3, k % 3, :, columns].astype(F32)
    if last:
        upper = total.astype(BF16)
        lower = (total - upper.astype(F32)).astype(BF16)
        ones = jnp.ones((16, 128), BF16)
        row[...] = (dot_nt(ones, upper) + dot_nt(ones, lower))[:1] / gain[...]
        copies.append(pltpu.make_async_copy(row, gain_out, done.at[15]))
        copies[-1].start()
    else:
        after[...] = total
    for copy in copies:
        copy.wait()


def call(kernel, outs, scratch=(), flops=0, moved=0, aliases=None, far=0):
    where = pl.BlockSpec(memory_space=pltpu.VMEM)

    def run(*operands):
        results = pl.pallas_call(
            kernel,
            out_shape=[jax.ShapeDtypeStruct(shape, dtype) for shape, dtype in outs],
            in_specs=[
                pl.BlockSpec(memory_space=pltpu.HBM)
                if a.dtype == jnp.int32 or at in (aliases or ())
                else where
                for at, a in enumerate(operands)
            ],
            out_specs=[pl.BlockSpec(memory_space=pltpu.HBM)] * far + [where] * (len(outs) - far),
            input_output_aliases=aliases or {},
            scratch_shapes=list(scratch),
            compiler_params=pltpu.CompilerParams(vmem_limit_bytes=VMEM_LIMIT),
            cost_estimate=pl.CostEstimate(flops=flops, bytes_accessed=moved, transcendentals=0),
        )(*operands)
        return list(results)

    return run


def neighbours(inner, outer, axis):
    size = lax.axis_size(axis)
    links = [(i, i + 1) for i in range(1, size - 1, 2)]
    links = links + [(j, i) for i, j in links]
    return (pair(inner, axis, 1), lax.ppermute(outer, axis, links))


def pair(array, axis, step):
    return lax.ppermute(array, axis, [(i, i ^ step) for i in range(lax.axis_size(axis))])


def pairs(arrays, axis):
    return [pair(array, axis, step + 1) for step, array in enumerate(arrays)]


def together(*values):
    return lax.optimization_barrier(values)


def on_device(
    video_clip, valid_from, norm_gain, spatial_weight, temporal_weight, mix_weight, cotangent
):
    video = video_clip[0]
    frames, rows, width, channels = video.shape
    outs = frames // 2
    shards = lax.axis_size("tm")
    lines = lax.axis_size("height")
    here = rows // shards
    cells = frames * rows * width
    sizes = dict(frames=frames, rows=rows, width=width)
    gain = norm_gain.reshape(1, channels)
    edge = ((frames, width, channels), BF16)
    halo = pltpu.VMEM((2, frames, width, channels), BF16)

    scalar = [pltpu.SMEM((1,), jnp.int32), pltpu.SemaphoreType.DMA((1,))]
    pieces = call(
        functools.partial(pieces_kernel, outs=outs),
        [((outs + 3, here, width, channels), BF16)] * (shards - 1),
        [pltpu.SemaphoreType.DMA((shards - 1,))],
        moved=1024 * 1024,
    )(cotangent[0])
    *pieces, edges = together(*pieces, video)
    pieces = pairs(pieces, "tm")
    inner, outer = call(
        functools.partial(edges_kernel, rows=rows, frames_first=True),
        [edge, edge],
        [pltpu.SemaphoreType.DMA((2,))],
        moved=512 * 1024,
    )(edges)
    inner, outer = neighbours(inner, outer, "height")

    normed, partial = call(
        functools.partial(own_kernel, **sizes),
        [((cells, channels), BF16), ((cells, channels), F32)],
        scalar,
        flops=18 * cells * channels * channels,
        moved=4 * 1024 * 1024,
    )(valid_from, video, gain, spatial_weight)

    tall, slope, active, parts, stay, leave = call(
        functools.partial(front_kernel, **sizes, shards=shards),
        [
            ((cells + 2 * frames * width, channels), BF16),
            ((cells, channels), F32),
            ((2, cells // 2, channels), BF16),
            (((outs + 1) * rows * width, channels), BF16),
        ]
        + [((1, shards // 2, outs + 1, here, width, channels), BF16)] * 2,
        [halo, *scalar, pltpu.VMEM((shards, outs + 1, here, width, channels), BF16)],
    )(valid_from, normed, partial, inner, outer, gain, spatial_weight, temporal_weight)

    half = channels // 2
    pre_gradient, *low = call(
        functools.partial(middle_kernel, **sizes, shards=shards),
        [
            ((rows, frames, width, channels), BF16),
            ((SPLIT * channels, half), F32),
            ((SPLIT * channels, half), BF16),
        ],
        [pltpu.VMEM((outs + 3, shards, here * width, channels), BF16)],
        flops=20 * cells * channels * channels,
        moved=6 * 1024 * 1024,
    )(
        tall, slope, active, parts, temporal_weight, mix_weight, cotangent[0],
        *reversed(pieces),
    )

    high = call(
        functools.partial(spatial_kernel, **sizes),
        [((size * channels, half), dtype) for size in (15 - SPLIT,) for dtype in (F32, BF16)],
        flops=16 * cells * channels * channels,
        moved=6 * 1024 * 1024,
    )(tall, pre_gradient)

    def shapes(rows_in, *types):
        return [((rows_in, half), dtype) for dtype in types]

    def added(left, right):
        (total,) = call(add_kernel, shapes(left.shape[0], BF16))(left, right)
        return total

    def joined(pieces):
        (total,) = call(join_kernel, [((lines,) + pieces[0].shape, BF16)])(*pieces)
        return total

    def summed(pieces):
        (total,) = call(gather_sum_kernel, shapes(pieces[0].shape[0], BF16))(*pieces)
        return total

    (low, low_send), (high, high_send) = (low, high)
    low_got = pair(low_send, "cam", 1)
    high_got = pair(high_send, "cam", 1)
    size = 15 * channels // lines // 2
    dealt = call(deal_kernel, shapes(size, *([F32] + [BF16] * (lines - 1)) * 2))(
        *[a.reshape(lines, 2, -1, half) for a in (low, low_got, high, high_got)]
    )
    (away, *away_sends), (home, *home_sends) = (dealt[:lines], dealt[lines:])
    away_came = pairs(away_sends, "height")
    home_came = pairs(home_sends, "height")
    came = pair(leave, "tm", 1)
    away, came = together(away, came)
    crossed = pair(summed([away] + away_came[::-1]), "tm", 1)
    total = summed([home] + home_came[::-1] + [crossed])
    pre_gradient, total = together(pre_gradient, total)
    inner, outer = call(
        functools.partial(edges_kernel, rows=rows, frames_first=False),
        [edge, edge],
        [pltpu.SemaphoreType.DMA((2,))],
        flops=240 * cells * channels * channels,
        moved=512 * 1024,
    )(pre_gradient)
    inner, outer = neighbours(inner, outer, "height")
    (halo_rows,) = call(halo_kernel, [((2, frames, width, channels), BF16)])(inner, outer)
    for step in range(1, shards.bit_length() - 1):
        if step > 1:
            total = added(total, other)
        other = pair(total, "tm", 1 << step)
    total = added(total, other)
    total, stay, came = together(total, stay, came)
    other = pair(total, "tm", 1)
    other, halo_rows = together(other, halo_rows)
    for step in range(1, shards.bit_length() - 1):
        count, pieces = (2 * stay.shape[0], stay.shape[1] // 2)
        stay, leave = call(split_kernel, [((count, pieces) + stay.shape[2:], BF16)] * 2)(stay, came)
        came = pair(leave, "tm", 1 << step)
    home_pieces = [total] + pairs([total] * (lines - 1), "height")
    away_pieces = [other] + pairs([other] * (lines - 1), "height")
    (video_gradient,) = call(
        functools.partial(input_kernel, **sizes),
        [((frames, rows, width, channels), BF16)],
        [pltpu.VMEM((cells, 3 * channels), BF16)] + scalar,
        flops=18 * cells * channels * channels,
        moved=4 * 1024 * 1024,
    )(valid_from, video, pre_gradient, halo_rows, gain, spatial_weight)
    home = joined(home_pieces)
    home, came = together(home, came)
    (encoded,) = call(
        functools.partial(encode_kernel, width=width, shards=shards),
        [((shards * outs, here, width, channels), BF16)],
        [
            pltpu.VMEM(((shards * outs + 2) * here * width, channels), BF16),
            pltpu.VMEM((shards, outs + 1, here, width, channels), BF16),
        ],
        flops=3 * cells * channels * channels,
        moved=2 * 1024 * 1024,
    )(mix_weight, stay, came)
    away_pieces[-1], home, video_gradient, encoded = together(
        away_pieces[-1], home, video_gradient, encoded
    )
    away = joined(away_pieces)
    own = (home, away)
    others = (pair(home, "cam", 1), pair(away, "cam", 1))

    cell_count = cells * lax.axis_size("cam") * shards * lines
    scale = 1.0 / math.sqrt(cell_count)
    results = [((9, channels, channels), F32)] + [((3, channels, channels), F32)] * 2
    staged = pltpu.VMEM((15 * channels, half), F32)
    *results_own, total = call(
        functools.partial(finish_kernel, scale=scale, last=False),
        results + [((channels, half), F32)],
        [staged, pltpu.SemaphoreType.DMA((15,))],
        moved=4 * 1024 * 1024,
        far=3,
    )(*own, spatial_weight)
    spatial, temporal, mix, gain_gradient = call(
        functools.partial(finish_kernel, scale=scale, last=True),
        results + [((1, channels), F32)],
        [staged, pltpu.VMEM((1, channels), F32), pltpu.SemaphoreType.DMA((16,))],
        moved=4 * 1024 * 1024,
        far=4,
        aliases={5 + at: at for at in range(3)},
    )(*others, spatial_weight, total, gain, *results_own)

    return (
        encoded[None],
        video_gradient[None],
        spatial.reshape(spatial_weight.shape),
        temporal,
        mix,
        gain_gradient.reshape(channels),
    )


def solution(mesh):
    return jax.shard_map(
        on_device,
        mesh=mesh,
        in_specs=(
            P("cam", "tm", "height", None, None),
            P("cam"),
            P(),
            P(),
            P(),
            P(),
            P("cam", None, ("height", "tm"), None, None),
        ),
        out_specs=(
            P("cam", None, ("height", "tm"), None, None),
            P("cam", "tm", "height", None, None),
            P(),
            P(),
            P(),
            P(),
        ),
        check_vma=False,
    )
```

```python
import functools
import math

import jax
import jax.numpy as jnp
from jax import lax
from jax.experimental import pallas as pl
from jax.experimental.pallas import tpu as pltpu
from jax.sharding import PartitionSpec as P

F32 = jnp.float32
BF16 = jnp.bfloat16
VMEM_LIMIT = 16 * 1024 * 1024
SPLIT = 8


def dot(left, right):
    return jnp.dot(left, right, preferred_element_type=F32)


def dot_nt(left, right):
    return lax.dot_general(left, right, (((1,), (1,)), ((), ())), preferred_element_type=F32)


def dot_tn(left, right):
    return lax.dot_general(left, right, (((0,), (0,)), ((), ())), preferred_element_type=F32)


def from_left(cells, width):
    column = lax.broadcasted_iota(jnp.int32, cells.shape, 0) % width
    return jnp.where(column == 0, 0.0, pltpu.roll(cells, 1, 0))


def from_right(cells, width):
    column = lax.broadcasted_iota(jnp.int32, cells.shape, 0) % width
    return jnp.where(column == width - 1, 0.0, pltpu.roll(cells, cells.shape[0] - 1, 0))


def present(start, frame, frames):
    return (lax.axis_index("tm") * frames + frame >= start[0]).astype(F32)


def normalised(tile, keep):
    values = tile.astype(F32) * keep
    inverse = lax.rsqrt(jnp.mean(values * values, axis=-1, keepdims=True) + 1e-06)
    return (values * inverse, inverse)


def first_frame(shard, outs, span, total):
    return jnp.minimum(shard * outs, total - span)


def run_copies(pairs_of_refs, done):
    copies = [
        pltpu.make_async_copy(source, target, done.at[at])
        for at, (source, target) in enumerate(pairs_of_refs)
    ]
    for copy in copies:
        copy.start()
    for copy in copies:
        copy.wait()


def pieces_kernel(cotangent, *refs, outs):
    pieces, done = (refs[:-1], refs[-1])
    span = outs + 3
    me = lax.axis_index("tm")
    copies = []
    for step, piece in enumerate(pieces):
        begin = first_frame(me ^ (step + 1), outs, span, cotangent.shape[0])
        copies.append((cotangent.at[pl.ds(begin, span)], piece))
    run_copies(copies, done)


def edges_kernel(source, inner, outer, done, *, rows, frames_first):
    odd = lax.axis_index("height") % 2

    def row(at):
        return source.at[:, at] if frames_first else source.at[at]

    run_copies(
        [(row((1 - odd) * (rows - 1)), inner), (row(odd * (rows - 1)), outer)], done
    )


def first_frame(shard, outs, span, total):
    return jnp.minimum(shard * outs, total - span)


def place_halos(halo, inner, outer):
    odd = lax.axis_index("height") % 2
    halo[1 - odd] = inner[...]
    halo[odd] = outer[...]


def column_sum(cells, weight, taps, width):
    products = [
        dot(cells, jnp.concatenate([weight[i, j] for i in taps], axis=0)) for j in range(3)
    ]
    return from_left(products[0], width) + products[1] + from_right(products[2], width)


def halo_kernel(inner, outer, halo):
    place_halos(halo, inner, outer)


def own_kernel(
    valid_from, video, gain, weight, normed, partial, start, done, *, frames, rows, width
):
    run_copies([(valid_from, start)], done)
    block = frames * width
    for row in range(rows):
        for frame in range(frames):
            unit, _ = normalised(video[frame, row], present(start, frame, frames))
            at = row * block + frame * width
            normed[at : at + width] = (unit * gain[...]).astype(BF16)
    for row in range(rows):
        taps = [i for i in range(3) if 0 <= row + i - 1 < rows]
        cells = [normed[(row + i - 1) * block : (row + i) * block] for i in taps]
        partial[row * block : row * block + block] = column_sum(
            jnp.concatenate(cells, axis=1), weight, taps, width
        )


def front_kernel(
    valid_from, normed, partial, inner, outer, gain, weight, temporal, *refs,
    frames, rows, width, shards
):
    tall, slope, active, parts, *refs = refs
    strided, (halo, start, done, lines) = (refs[:2], refs[2:])
    outs = frames // 2
    plane = rows * width
    here = rows // shards
    block = frames * width

    run_copies([(valid_from, start)], done)
    place_halos(halo, inner, outer)
    tall[block : block + rows * block] = normed[...]
    for side, at in ((0, 0), (1, (rows + 1) * block)):
        for frame in range(frames):
            unit, _ = normalised(halo[side, frame], present(start, frame, frames))
            to = at + frame * width
            tall[to : to + width] = (unit * gain[...]).astype(BF16)
    for row in range(rows):
        pre = partial[row * block : row * block + block]
        if row == 0:
            pre = pre + column_sum(tall[:block], weight, [0], width)
        if row == rows - 1:
            pre = pre + column_sum(tall[(rows + 1) * block :], weight, [2], width)
        sigmoid = 1.0 / (1.0 + jnp.exp(-pre))
        slope[row * block : row * block + block] = sigmoid * (1.0 + pre * (1.0 - sigmoid))
        cells = (pre * sigmoid).astype(BF16)
        for frame in range(frames):
            at = (frame // 2) * plane + row * width
            active[frame % 2, at : at + width] = cells[frame * width : frame * width + width]
    evens = active[0]
    odds = active[1]
    carried = dot(odds, temporal[2])
    mixed = dot(odds, temporal[0]) + dot(evens, temporal[1])
    pieces = [mixed[:plane]]
    for s in range(1, outs):
        pieces.append(
            mixed[s * plane : s * plane + plane] + carried[(s - 1) * plane : s * plane]
        )
    pieces.append(carried[(outs - 1) * plane :])
    pieces = jnp.concatenate(pieces, axis=0).astype(BF16)
    parts[...] = pieces
    for frame in range(outs + 1):
        cells = pieces[frame * plane : frame * plane + plane]
        lines[:, frame] = cells.reshape(shards, here, width, 256)
    stay, leave = strided
    for step in range(shards):
        target = leave if step % 2 else stay
        target[0, step // 2] = lines[lax.axis_index("tm") ^ step]


def split_kernel(stay_in, came_in, stay, leave):
    count, pieces = stay_in.shape[:2]
    for place, source in enumerate((stay_in, came_in)):
        for at in range(count):
            for piece in range(pieces):
                target = leave if piece % 2 else stay
                target[place * count + at, piece // 2] = source[at, piece]


def middle_kernel(
    tall, slope, active, parts, temporal, mix, cotangent, *refs, frames, rows, width, shards
):
    pieces, refs = (refs[: shards - 1], refs[shards - 1 :])
    pre_gradient, keep, send, cot = refs
    outs = frames // 2
    plane = rows * width
    here = rows // shards
    me = lax.axis_index("tm")
    total = shards * outs
    cut = outs + 3
    skip = me * outs - first_frame(me, outs, cut, total)
    for frame in range(cut):
        here_is = (me * outs + frame < total).astype(F32)
        own = cotangent[jnp.minimum(me * outs + frame, total - 1)]
        others = [piece[jnp.minimum(frame + skip, cut - 1)] for piece in pieces]
        for step, cells in enumerate([own] + others[::-1]):
            cells = (cells.astype(F32) * here_is).astype(BF16)
            cot[frame, me ^ step] = cells.reshape(here * width, 256)

    def ahead(k, count=outs + 1):
        return cot[k : k + count].reshape(count * plane, 256)

    gradient = ahead(0).astype(F32)
    for k in range(3):
        gradient = gradient + dot_nt(ahead(k), mix[k])
    gradient = gradient.astype(BF16)
    now = gradient[: outs * plane]
    later = gradient[plane:]
    even_gradient = dot_nt(now, temporal[1])
    odd_gradient = dot_nt(now, temporal[0]) + dot_nt(later, temporal[2])
    for row in range(rows):
        for frame in range(frames):
            source = odd_gradient if frame % 2 else even_gradient
            at = (frame // 2) * plane + row * width
            to = (row * frames + frame) * width
            tile = (source[at : at + width] * slope[to : to + width]).astype(BF16)
            pre_gradient[row, frame] = tile
    evens = active[0]
    odds = active[1]
    for k in range(3):
        deliver(keep, send, k, dot_tn(parts[...], ahead(k)))
    deliver(keep, send, 3, dot_tn(odds, now))
    deliver(keep, send, 4, dot_tn(evens, now))
    deliver(keep, send, 5, dot_tn(odds, later))
    block = frames * width
    spatial_sums(tall, pre_gradient, keep, send, 6, range(SPLIT - 6), block, rows, width)


def spatial_kernel(tall, pre_gradient, keep, send, *, frames, rows, width):
    block = frames * width
    spatial_sums(tall, pre_gradient, keep, send, 0, range(SPLIT - 6, 9), block, rows, width)


def spatial_sums(tall, pre_gradient, keep, send, first, taps, block, rows, width):
    columns = column_shifts(pre_gradient, width)
    for i in range(3):
        here = [tap for tap in taps if tap // 3 == i]
        if not here:
            continue
        cells = tall[i * block : (i + rows) * block]
        product = dot_tn(cells, jnp.concatenate([columns[tap % 3] for tap in here], axis=1))
        for place, tap in enumerate(here):
            index = first + tap - taps[0]
            deliver(keep, send, index, product[:, place * 256 : place * 256 + 256])


def column_shifts(pre_gradient, width):
    gradient = pre_gradient[...].reshape(-1, 256)
    exact = gradient.astype(F32)
    left = from_right(exact, width).astype(BF16)
    right = from_left(exact, width).astype(BF16)
    return [left, gradient, right]


def deliver(keep, send, index, product):
    first = jnp.full((256, 128), lax.axis_index("cam")) == 0
    low, high = (product[:, :128], product[:, 128:])
    at = index * 256
    keep[at : at + 256] = jnp.where(first, low, high)
    send[at : at + 256] = jnp.where(first, high, low).astype(BF16)


def core_columns():
    mine = pl.ds(pl.multiple_of(lax.axis_index("cam") * 128, 128), 128)
    other = pl.ds(pl.multiple_of((1 - lax.axis_index("cam")) * 128, 128), 128)
    return (mine, other)


def deal_kernel(low, low_got, high, high_got, *outs):
    me = lax.axis_index("height")
    home = lax.axis_index("tm") % 2
    cut = low.shape[2]
    count = len(outs) // 2
    for target, half in [(outs[:count], 1 - home), (outs[count:], home)]:
        for step, out in enumerate(target):
            at = me ^ step
            out[:cut] = (low[at, half] + low_got[at, half].astype(F32)).astype(out.dtype)
            out[cut:] = (high[at, half] + high_got[at, half].astype(F32)).astype(out.dtype)


def gather_sum_kernel(kept, *refs):
    value = kept[...]
    for piece in refs[:-1]:
        value = value + piece[...].astype(F32)
    refs[-1][...] = value.astype(BF16)


def add_kernel(left, right, out):
    out[...] = (left[...].astype(F32) + right[...].astype(F32)).astype(BF16)


def join_kernel(*refs):
    for step, piece in enumerate(refs[:-1]):
        refs[-1][lax.axis_index("height") ^ step] = piece[...]


def input_kernel(
    valid_from, video, pre_gradient, halo, gain, weight, out, tall, start, done,
    *, frames, rows, width
):
    run_copies([(valid_from, start)], done)
    block = frames * width
    for row in range(-1, rows + 1):
        if row < 0:
            cells = halo[0]
        elif row == rows:
            cells = halo[1]
        else:
            cells = pre_gradient[row]
        cells = cells.reshape(block, 256)
        for tap in range(3):
            target = row - 1 + tap
            if 0 <= target < rows:
                tall[target * block : target * block + block, tap * 256 : tap * 256 + 256] = cells
    for row in range(rows):
        cells = tall[row * block : row * block + block]
        taps = [
            dot_nt(cells, jnp.concatenate([weight[0, j], weight[1, j], weight[2, j]], axis=1))
            for j in range(3)
        ]
        gradient = from_right(taps[0], width) + taps[1] + from_left(taps[2], width)
        gradient = gradient * gain[...]
        for frame in range(frames):
            keep = present(start, frame, frames)
            unit, inverse = normalised(video[frame, row], keep)
            tile = gradient[frame * width : frame * width + width]
            mean = jnp.mean(tile * unit, axis=-1, keepdims=True)
            out[frame, row] = (inverse * (tile - unit * mean) * keep).astype(BF16)


def encode_kernel(mix, stay, came, out, line, strided, *, width, shards):
    for step in range(shards):
        source = came if step >= shards // 2 else stay
        strided[lax.axis_index("tm") ^ step] = source[step % (shards // 2), 0]
    parts, here = strided.shape[1:3]
    outs = parts - 1
    plane = here * width
    total = shards * outs
    for frame in range(total):
        shard, part = (frame // outs, frame % outs)
        cells = strided[shard, part].reshape(plane, 256)
        if part == 0 and shard > 0:
            carried = strided[shard - 1, outs].reshape(plane, 256)
            cells = (cells.astype(F32) + carried.astype(F32)).astype(BF16)
        line[(frame + 2) * plane : (frame + 3) * plane] = cells
    line[0 : 2 * plane] = jnp.zeros((2 * plane, 256), BF16)
    span = total * plane
    result = line[2 * plane : 2 * plane + span].astype(F32)
    for k in range(3):
        result = result + dot(line[(2 - k) * plane : (2 - k) * plane + span], mix[k])
    out[...] = result.astype(BF16).reshape(out.shape)


def finish_kernel(home, away, weight, *refs, scale, last):
    if last:
        before, gain, _, _, _, spatial, temporal, mix, gain_out, staged, row, done = refs
        total = before[...]
    else:
        spatial, temporal, mix, after, staged, done = refs
        total = jnp.zeros((256, 128), F32)
    columns = core_columns()[1 if last else 0]
    parts = home.shape[0]
    low, high = (SPLIT * 128 // parts, (15 - SPLIT) * 128 // parts)
    mine = lax.axis_index("tm") % 2
    for half, source in ((mine, home), (1 - mine, away)):
        for part in range(parts):
            at = pl.multiple_of((2 * part + half) * low, low)
            staged[pl.ds(at, low)] = source[part, :low].astype(F32) * scale
            at = pl.multiple_of(SPLIT * 256 + (2 * part + half) * high, high)
            staged[pl.ds(at, high)] = source[part, low:].astype(F32) * scale
    results = [(mix, k) for k in range(3)] + [(temporal, k) for k in range(3)]
    results = results + [(spatial, k) for k in range(9)]
    copies = []
    for index, (result, k) in enumerate(results):
        cells = staged.at[pl.ds(index * 256, 256)]
        copies.append(pltpu.make_async_copy(cells, result.at[k, :, columns], done.at[index]))
        copies[-1].start()
    for k in range(9):
        cells = staged[1536 + k * 256 : 1792 + k * 256]
        total = total + cells * weight[k // 3, k % 3, :, columns].astype(F32)
    if last:
        upper = total.astype(BF16)
        lower = (total - upper.astype(F32)).astype(BF16)
        ones = jnp.ones((16, 128), BF16)
        row[...] = (dot_nt(ones, upper) + dot_nt(ones, lower))[:1] / gain[...]
        copies.append(pltpu.make_async_copy(row, gain_out, done.at[15]))
        copies[-1].start()
    else:
        after[...] = total
    for copy in copies:
        copy.wait()


def call(kernel, outs, scratch=(), flops=0, moved=0, aliases=None, far=0):
    where = pl.BlockSpec(memory_space=pltpu.VMEM)

    def run(*operands):
        results = pl.pallas_call(
            kernel,
            out_shape=[jax.ShapeDtypeStruct(shape, dtype) for shape, dtype in outs],
            in_specs=[
                pl.BlockSpec(memory_space=pltpu.HBM)
                if a.dtype == jnp.int32 or at in (aliases or ())
                else where
                for at, a in enumerate(operands)
            ],
            out_specs=[pl.BlockSpec(memory_space=pltpu.HBM)] * far + [where] * (len(outs) - far),
            input_output_aliases=aliases or {},
            scratch_shapes=list(scratch),
            compiler_params=pltpu.CompilerParams(vmem_limit_bytes=VMEM_LIMIT),
            cost_estimate=pl.CostEstimate(flops=flops, bytes_accessed=moved, transcendentals=0),
        )(*operands)
        return list(results)

    return run


def neighbours(inner, outer, axis):
    size = lax.axis_size(axis)
    links = [(i, i + 1) for i in range(1, size - 1, 2)]
    links = links + [(j, i) for i, j in links]
    return (pair(inner, axis, 1), lax.ppermute(outer, axis, links))


def pair(array, axis, step):
    return lax.ppermute(array, axis, [(i, i ^ step) for i in range(lax.axis_size(axis))])


def pairs(arrays, axis):
    return [pair(array, axis, step + 1) for step, array in enumerate(arrays)]


def together(*values):
    return lax.optimization_barrier(values)


def on_device(
    video_clip, valid_from, norm_gain, spatial_weight, temporal_weight, mix_weight, cotangent
):
    video = video_clip[0]
    frames, rows, width, channels = video.shape
    outs = frames // 2
    shards = lax.axis_size("tm")
    lines = lax.axis_size("height")
    here = rows // shards
    cells = frames * rows * width
    sizes = dict(frames=frames, rows=rows, width=width)
    gain = norm_gain.reshape(1, channels)
    edge = ((frames, width, channels), BF16)
    halo = pltpu.VMEM((2, frames, width, channels), BF16)

    scalar = [pltpu.SMEM((1,), jnp.int32), pltpu.SemaphoreType.DMA((1,))]
    pieces = call(
        functools.partial(pieces_kernel, outs=outs),
        [((outs + 3, here, width, channels), BF16)] * (shards - 1),
        [pltpu.SemaphoreType.DMA((shards - 1,))],
        moved=1024 * 1024,
    )(cotangent[0])
    *pieces, edges = together(*pieces, video)
    pieces = pairs(pieces, "tm")
    inner, outer = call(
        functools.partial(edges_kernel, rows=rows, frames_first=True),
        [edge, edge],
        [pltpu.SemaphoreType.DMA((2,))],
        moved=512 * 1024,
    )(edges)
    inner, outer = neighbours(inner, outer, "height")

    normed, partial = call(
        functools.partial(own_kernel, **sizes),
        [((cells, channels), BF16), ((cells, channels), F32)],
        scalar,
        flops=18 * cells * channels * channels,
        moved=4 * 1024 * 1024,
    )(valid_from, video, gain, spatial_weight)

    tall, slope, active, parts, stay, leave = call(
        functools.partial(front_kernel, **sizes, shards=shards),
        [
            ((cells + 2 * frames * width, channels), BF16),
            ((cells, channels), F32),
            ((2, cells // 2, channels), BF16),
            (((outs + 1) * rows * width, channels), BF16),
        ]
        + [((1, shards // 2, outs + 1, here, width, channels), BF16)] * 2,
        [halo, *scalar, pltpu.VMEM((shards, outs + 1, here, width, channels), BF16)],
    )(valid_from, normed, partial, inner, outer, gain, spatial_weight, temporal_weight)

    half = channels // 2
    pre_gradient, *low = call(
        functools.partial(middle_kernel, **sizes, shards=shards),
        [
            ((rows, frames, width, channels), BF16),
            ((SPLIT * channels, half), F32),
            ((SPLIT * channels, half), BF16),
        ],
        [pltpu.VMEM((outs + 3, shards, here * width, channels), BF16)],
        flops=20 * cells * channels * channels,
        moved=6 * 1024 * 1024,
    )(
        tall, slope, active, parts, temporal_weight, mix_weight, cotangent[0],
        *reversed(pieces),
    )

    high = call(
        functools.partial(spatial_kernel, **sizes),
        [((size * channels, half), dtype) for size in (15 - SPLIT,) for dtype in (F32, BF16)],
        flops=16 * cells * channels * channels,
        moved=6 * 1024 * 1024,
    )(tall, pre_gradient)

    def shapes(rows_in, *types):
        return [((rows_in, half), dtype) for dtype in types]

    def added(left, right):
        (total,) = call(add_kernel, shapes(left.shape[0], BF16))(left, right)
        return total

    def joined(pieces):
        (total,) = call(join_kernel, [((lines,) + pieces[0].shape, BF16)])(*pieces)
        return total

    def summed(pieces):
        (total,) = call(gather_sum_kernel, shapes(pieces[0].shape[0], BF16))(*pieces)
        return total

    (low, low_send), (high, high_send) = (low, high)
    low_got = pair(low_send, "cam", 1)
    high_got = pair(high_send, "cam", 1)
    size = 15 * channels // lines // 2
    dealt = call(deal_kernel, shapes(size, *([F32] + [BF16] * (lines - 1)) * 2))(
        *[a.reshape(lines, 2, -1, half) for a in (low, low_got, high, high_got)]
    )
    (away, *away_sends), (home, *home_sends) = (dealt[:lines], dealt[lines:])
    away_came = pairs(away_sends, "height")
    home_came = pairs(home_sends, "height")
    came = pair(leave, "tm", 1)
    away, came = together(away, came)
    crossed = pair(summed([away] + away_came[::-1]), "tm", 1)
    pre_gradient, home_came[-1] = together(pre_gradient, home_came[-1])
    total = summed([home] + home_came[::-1] + [crossed])
    inner, outer = call(
        functools.partial(edges_kernel, rows=rows, frames_first=False),
        [edge, edge],
        [pltpu.SemaphoreType.DMA((2,))],
        moved=512 * 1024,
    )(pre_gradient)
    inner, outer = neighbours(inner, outer, "height")
    (halo_rows,) = call(halo_kernel, [((2, frames, width, channels), BF16)])(inner, outer)
    for step in range(1, shards.bit_length() - 1):
        if step > 1:
            total = added(total, other)
        other = pair(total, "tm", 1 << step)
    (video_gradient,) = call(
        functools.partial(input_kernel, **sizes),
        [((frames, rows, width, channels), BF16)],
        [pltpu.VMEM((cells, 3 * channels), BF16)] + scalar,
        flops=18 * cells * channels * channels,
        moved=4 * 1024 * 1024,
    )(valid_from, video, pre_gradient, halo_rows, gain, spatial_weight)
    other, video_gradient = together(other, video_gradient)
    total = added(total, other)
    other = pair(total, "tm", 1)
    for step in range(1, shards.bit_length() - 1):
        count, pieces = (2 * stay.shape[0], stay.shape[1] // 2)
        stay, leave = call(split_kernel, [((count, pieces) + stay.shape[2:], BF16)] * 2)(stay, came)
        came = pair(leave, "tm", 1 << step)
    home_pieces = [total] + pairs([total] * (lines - 1), "height")
    away_pieces = [other] + pairs([other] * (lines - 1), "height")
    home = joined(home_pieces)
    home, came = together(home, came)
    (encoded,) = call(
        functools.partial(encode_kernel, width=width, shards=shards),
        [((shards * outs, here, width, channels), BF16)],
        [
            pltpu.VMEM(((shards * outs + 2) * here * width, channels), BF16),
            pltpu.VMEM((shards, outs + 1, here, width, channels), BF16),
        ],
        flops=3 * cells * channels * channels,
        moved=2 * 1024 * 1024,
    )(mix_weight, stay, came)
    away_pieces[-1], home, video_gradient, encoded = together(
        away_pieces[-1], home, video_gradient, encoded
    )
    away = joined(away_pieces)
    own = (home, away)
    others = (pair(home, "cam", 1), pair(away, "cam", 1))

    cell_count = cells * lax.axis_size("cam") * shards * lines
    scale = 1.0 / math.sqrt(cell_count)
    results = [((9, channels, channels), F32)] + [((3, channels, channels), F32)] * 2
    staged = pltpu.VMEM((15 * channels, half), F32)
    *results_own, total = call(
        functools.partial(finish_kernel, scale=scale, last=False),
        results + [((channels, half), F32)],
        [staged, pltpu.SemaphoreType.DMA((15,))],
        moved=4 * 1024 * 1024,
        far=3,
    )(*own, spatial_weight)
    spatial, temporal, mix, gain_gradient = call(
        functools.partial(finish_kernel, scale=scale, last=True),
        results + [((1, channels), F32)],
        [staged, pltpu.VMEM((1, channels), F32), pltpu.SemaphoreType.DMA((16,))],
        moved=4 * 1024 * 1024,
        far=4,
        aliases={5 + at: at for at in range(3)},
    )(*others, spatial_weight, total, gain, *results_own)

    return (
        encoded[None],
        video_gradient[None],
        spatial.reshape(spatial_weight.shape),
        temporal,
        mix,
        gain_gradient.reshape(channels),
    )


def solution(mesh):
    return jax.shard_map(
        on_device,
        mesh=mesh,
        in_specs=(
            P("cam", "tm", "height", None, None),
            P("cam"),
            P(),
            P(),
            P(),
            P(),
            P("cam", None, ("height", "tm"), None, None),
        ),
        out_specs=(
            P("cam", None, ("height", "tm"), None, None),
            P("cam", "tm", "height", None, None),
            P(),
            P(),
            P(),
            P(),
        ),
        check_vma=False,
    )
```

```python
import functools
import math

import jax
import jax.numpy as jnp
from jax import lax
from jax.experimental import pallas as pl
from jax.experimental.pallas import tpu as pltpu
from jax.sharding import PartitionSpec as P

F32 = jnp.float32
BF16 = jnp.bfloat16
VMEM_LIMIT = 16 * 1024 * 1024
SPLIT = 8


def dot(left, right):
    return jnp.dot(left, right, preferred_element_type=F32)


def dot_nt(left, right):
    return lax.dot_general(left, right, (((1,), (1,)), ((), ())), preferred_element_type=F32)


def dot_tn(left, right):
    return lax.dot_general(left, right, (((0,), (0,)), ((), ())), preferred_element_type=F32)


def from_left(cells, width):
    column = lax.broadcasted_iota(jnp.int32, cells.shape, 0) % width
    return jnp.where(column == 0, 0.0, pltpu.roll(cells, 1, 0))


def from_right(cells, width):
    column = lax.broadcasted_iota(jnp.int32, cells.shape, 0) % width
    return jnp.where(column == width - 1, 0.0, pltpu.roll(cells, cells.shape[0] - 1, 0))


def present(start, frame, frames):
    return (lax.axis_index("tm") * frames + frame >= start[0]).astype(F32)


def normalised(tile, keep):
    values = tile.astype(F32) * keep
    inverse = lax.rsqrt(jnp.mean(values * values, axis=-1, keepdims=True) + 1e-06)
    return (values * inverse, inverse)


def first_frame(shard, outs, span, total):
    return jnp.minimum(shard * outs, total - span)


def run_copies(pairs_of_refs, done):
    copies = [
        pltpu.make_async_copy(source, target, done.at[at])
        for at, (source, target) in enumerate(pairs_of_refs)
    ]
    for copy in copies:
        copy.start()
    for copy in copies:
        copy.wait()


def pieces_kernel(cotangent, *refs, outs):
    pieces, done = (refs[:-1], refs[-1])
    span = outs + 3
    me = lax.axis_index("tm")
    copies = []
    for step, piece in enumerate(pieces):
        begin = first_frame(me ^ (step + 1), outs, span, cotangent.shape[0])
        copies.append((cotangent.at[pl.ds(begin, span)], piece))
    run_copies(copies, done)


def edges_kernel(source, inner, outer, done, *, rows, frames_first):
    odd = lax.axis_index("height") % 2

    def row(at):
        return source.at[:, at] if frames_first else source.at[at]

    run_copies(
        [(row((1 - odd) * (rows - 1)), inner), (row(odd * (rows - 1)), outer)], done
    )


def first_frame(shard, outs, span, total):
    return jnp.minimum(shard * outs, total - span)


def place_halos(halo, inner, outer):
    odd = lax.axis_index("height") % 2
    halo[1 - odd] = inner[...]
    halo[odd] = outer[...]


def column_sum(cells, weight, taps, width):
    products = [
        dot(cells, jnp.concatenate([weight[i, j] for i in taps], axis=0)) for j in range(3)
    ]
    return from_left(products[0], width) + products[1] + from_right(products[2], width)


def halo_kernel(inner, outer, halo):
    place_halos(halo, inner, outer)


def own_kernel(
    valid_from, video, gain, weight, normed, partial, start, done, *, frames, rows, width
):
    run_copies([(valid_from, start)], done)
    block = frames * width
    for row in range(rows):
        for frame in range(frames):
            unit, _ = normalised(video[frame, row], present(start, frame, frames))
            at = row * block + frame * width
            normed[at : at + width] = (unit * gain[...]).astype(BF16)
    for row in range(rows):
        taps = [i for i in range(3) if 0 <= row + i - 1 < rows]
        cells = [normed[(row + i - 1) * block : (row + i) * block] for i in taps]
        partial[row * block : row * block + block] = column_sum(
            jnp.concatenate(cells, axis=1), weight, taps, width
        )


def front_kernel(
    valid_from, normed, partial, inner, outer, gain, weight, temporal, *refs,
    frames, rows, width, shards
):
    tall, slope, active, parts, *refs = refs
    strided, (halo, start, done, lines) = (refs[:2], refs[2:])
    outs = frames // 2
    plane = rows * width
    here = rows // shards
    block = frames * width

    run_copies([(valid_from, start)], done)
    place_halos(halo, inner, outer)
    tall[block : block + rows * block] = normed[...]
    for side, at in ((0, 0), (1, (rows + 1) * block)):
        for frame in range(frames):
            unit, _ = normalised(halo[side, frame], present(start, frame, frames))
            to = at + frame * width
            tall[to : to + width] = (unit * gain[...]).astype(BF16)
    for row in range(rows):
        pre = partial[row * block : row * block + block]
        if row == 0:
            pre = pre + column_sum(tall[:block], weight, [0], width)
        if row == rows - 1:
            pre = pre + column_sum(tall[(rows + 1) * block :], weight, [2], width)
        sigmoid = 1.0 / (1.0 + jnp.exp(-pre))
        slope[row * block : row * block + block] = sigmoid * (1.0 + pre * (1.0 - sigmoid))
        cells = (pre * sigmoid).astype(BF16)
        for frame in range(frames):
            at = (frame // 2) * plane + row * width
            active[frame % 2, at : at + width] = cells[frame * width : frame * width + width]
    evens = active[0]
    odds = active[1]
    carried = dot(odds, temporal[2])
    mixed = dot(odds, temporal[0]) + dot(evens, temporal[1])
    pieces = [mixed[:plane]]
    for s in range(1, outs):
        pieces.append(
            mixed[s * plane : s * plane + plane] + carried[(s - 1) * plane : s * plane]
        )
    pieces.append(carried[(outs - 1) * plane :])
    pieces = jnp.concatenate(pieces, axis=0).astype(BF16)
    parts[...] = pieces
    for frame in range(outs + 1):
        cells = pieces[frame * plane : frame * plane + plane]
        lines[:, frame] = cells.reshape(shards, here, width, 256)
    stay, leave = strided
    for step in range(shards):
        target = leave if step % 2 else stay
        target[0, step // 2] = lines[lax.axis_index("tm") ^ step]


def split_kernel(stay_in, came_in, stay, leave):
    count, pieces = stay_in.shape[:2]
    for place, source in enumerate((stay_in, came_in)):
        for at in range(count):
            for piece in range(pieces):
                target = leave if piece % 2 else stay
                target[place * count + at, piece // 2] = source[at, piece]


def middle_kernel(
    tall, slope, active, parts, temporal, mix, cotangent, *refs, frames, rows, width, shards
):
    pieces, refs = (refs[: shards - 1], refs[shards - 1 :])
    pre_gradient, keep, send, cot = refs
    outs = frames // 2
    plane = rows * width
    here = rows // shards
    me = lax.axis_index("tm")
    total = shards * outs
    cut = outs + 3
    skip = me * outs - first_frame(me, outs, cut, total)
    for frame in range(cut):
        here_is = (me * outs + frame < total).astype(F32)
        own = cotangent[jnp.minimum(me * outs + frame, total - 1)]
        others = [piece[jnp.minimum(frame + skip, cut - 1)] for piece in pieces]
        for step, cells in enumerate([own] + others[::-1]):
            cells = (cells.astype(F32) * here_is).astype(BF16)
            cot[frame, me ^ step] = cells.reshape(here * width, 256)

    def ahead(k, count=outs + 1):
        return cot[k : k + count].reshape(count * plane, 256)

    gradient = ahead(0).astype(F32)
    for k in range(3):
        gradient = gradient + dot_nt(ahead(k), mix[k])
    gradient = gradient.astype(BF16)
    now = gradient[: outs * plane]
    later = gradient[plane:]
    even_gradient = dot_nt(now, temporal[1])
    odd_gradient = dot_nt(now, temporal[0]) + dot_nt(later, temporal[2])
    for row in range(rows):
        for frame in range(frames):
            source = odd_gradient if frame % 2 else even_gradient
            at = (frame // 2) * plane + row * width
            to = (row * frames + frame) * width
            tile = (source[at : at + width] * slope[to : to + width]).astype(BF16)
            pre_gradient[row, frame] = tile
    evens = active[0]
    odds = active[1]
    for k in range(3):
        deliver(keep, send, k, dot_tn(parts[...], ahead(k)))
    deliver(keep, send, 3, dot_tn(odds, now))
    deliver(keep, send, 4, dot_tn(evens, now))
    deliver(keep, send, 5, dot_tn(odds, later))
    block = frames * width
    spatial_sums(tall, pre_gradient, keep, send, 6, range(SPLIT - 6), block, rows, width)


def spatial_kernel(tall, pre_gradient, keep, send, *, frames, rows, width):
    block = frames * width
    spatial_sums(tall, pre_gradient, keep, send, 0, range(SPLIT - 6, 9), block, rows, width)


def spatial_sums(tall, pre_gradient, keep, send, first, taps, block, rows, width):
    columns = column_shifts(pre_gradient, width)
    for i in range(3):
        here = [tap for tap in taps if tap // 3 == i]
        if not here:
            continue
        cells = tall[i * block : (i + rows) * block]
        product = dot_tn(cells, jnp.concatenate([columns[tap % 3] for tap in here], axis=1))
        for place, tap in enumerate(here):
            index = first + tap - taps[0]
            deliver(keep, send, index, product[:, place * 256 : place * 256 + 256])


def column_shifts(pre_gradient, width):
    gradient = pre_gradient[...].reshape(-1, 256)
    exact = gradient.astype(F32)
    left = from_right(exact, width).astype(BF16)
    right = from_left(exact, width).astype(BF16)
    return [left, gradient, right]


def deliver(keep, send, index, product):
    first = jnp.full((256, 128), lax.axis_index("cam")) == 0
    low, high = (product[:, :128], product[:, 128:])
    at = index * 256
    keep[at : at + 256] = jnp.where(first, low, high)
    send[at : at + 256] = jnp.where(first, high, low).astype(BF16)


def core_columns():
    mine = pl.ds(pl.multiple_of(lax.axis_index("cam") * 128, 128), 128)
    other = pl.ds(pl.multiple_of((1 - lax.axis_index("cam")) * 128, 128), 128)
    return (mine, other)


def deal_kernel(low, low_got, high, high_got, *outs):
    me = lax.axis_index("height")
    home = lax.axis_index("tm") % 2
    cut = low.shape[2]
    count = len(outs) // 2
    for target, half in [(outs[:count], 1 - home), (outs[count:], home)]:
        for step, out in enumerate(target):
            at = me ^ step
            out[:cut] = (low[at, half] + low_got[at, half].astype(F32)).astype(out.dtype)
            out[cut:] = (high[at, half] + high_got[at, half].astype(F32)).astype(out.dtype)


def gather_sum_kernel(kept, *refs):
    value = kept[...]
    for piece in refs[:-1]:
        value = value + piece[...].astype(F32)
    refs[-1][...] = value.astype(BF16)


def add_kernel(left, right, out):
    out[...] = (left[...].astype(F32) + right[...].astype(F32)).astype(BF16)


def join_kernel(*refs):
    for step, piece in enumerate(refs[:-1]):
        refs[-1][lax.axis_index("height") ^ step] = piece[...]


def input_kernel(
    valid_from, video, pre_gradient, halo, gain, weight, out, tall, start, done,
    *, frames, rows, width
):
    run_copies([(valid_from, start)], done)
    block = frames * width
    for row in range(-1, rows + 1):
        if row < 0:
            cells = halo[0]
        elif row == rows:
            cells = halo[1]
        else:
            cells = pre_gradient[row]
        cells = cells.reshape(block, 256)
        for tap in range(3):
            target = row - 1 + tap
            if 0 <= target < rows:
                tall[target * block : target * block + block, tap * 256 : tap * 256 + 256] = cells
    for row in range(rows):
        cells = tall[row * block : row * block + block]
        taps = [
            dot_nt(cells, jnp.concatenate([weight[0, j], weight[1, j], weight[2, j]], axis=1))
            for j in range(3)
        ]
        gradient = from_right(taps[0], width) + taps[1] + from_left(taps[2], width)
        gradient = gradient * gain[...]
        for frame in range(frames):
            keep = present(start, frame, frames)
            unit, inverse = normalised(video[frame, row], keep)
            tile = gradient[frame * width : frame * width + width]
            mean = jnp.mean(tile * unit, axis=-1, keepdims=True)
            out[frame, row] = (inverse * (tile - unit * mean) * keep).astype(BF16)


def encode_kernel(mix, stay, came, out, line, strided, *, width, shards):
    for step in range(shards):
        source = came if step >= shards // 2 else stay
        strided[lax.axis_index("tm") ^ step] = source[step % (shards // 2), 0]
    parts, here = strided.shape[1:3]
    outs = parts - 1
    plane = here * width
    total = shards * outs
    for frame in range(total):
        shard, part = (frame // outs, frame % outs)
        cells = strided[shard, part].reshape(plane, 256)
        if part == 0 and shard > 0:
            carried = strided[shard - 1, outs].reshape(plane, 256)
            cells = (cells.astype(F32) + carried.astype(F32)).astype(BF16)
        line[(frame + 2) * plane : (frame + 3) * plane] = cells
    line[0 : 2 * plane] = jnp.zeros((2 * plane, 256), BF16)
    span = total * plane
    result = line[2 * plane : 2 * plane + span].astype(F32)
    for k in range(3):
        result = result + dot(line[(2 - k) * plane : (2 - k) * plane + span], mix[k])
    out[...] = result.astype(BF16).reshape(out.shape)


def finish_kernel(home, away, weight, *refs, scale, last):
    if last:
        before, gain, _, _, _, spatial, temporal, mix, gain_out, staged, row, done = refs
        total = before[...]
    else:
        spatial, temporal, mix, after, staged, done = refs
        total = jnp.zeros((256, 128), F32)
    columns = core_columns()[1 if last else 0]
    parts = home.shape[0]
    low, high = (SPLIT * 128 // parts, (15 - SPLIT) * 128 // parts)
    mine = lax.axis_index("tm") % 2
    for half, source in ((mine, home), (1 - mine, away)):
        for part in range(parts):
            at = pl.multiple_of((2 * part + half) * low, low)
            staged[pl.ds(at, low)] = source[part, :low].astype(F32) * scale
            at = pl.multiple_of(SPLIT * 256 + (2 * part + half) * high, high)
            staged[pl.ds(at, high)] = source[part, low:].astype(F32) * scale
    results = [(mix, k) for k in range(3)] + [(temporal, k) for k in range(3)]
    results = results + [(spatial, k) for k in range(9)]
    copies = []
    for index, (result, k) in enumerate(results):
        cells = staged.at[pl.ds(index * 256, 256)]
        copies.append(pltpu.make_async_copy(cells, result.at[k, :, columns], done.at[index]))
        copies[-1].start()
    for k in range(9):
        cells = staged[1536 + k * 256 : 1792 + k * 256]
        total = total + cells * weight[k // 3, k % 3, :, columns].astype(F32)
    if last:
        upper = total.astype(BF16)
        lower = (total - upper.astype(F32)).astype(BF16)
        ones = jnp.ones((16, 128), BF16)
        row[...] = (dot_nt(ones, upper) + dot_nt(ones, lower))[:1] / gain[...]
        copies.append(pltpu.make_async_copy(row, gain_out, done.at[15]))
        copies[-1].start()
    else:
        after[...] = total
    for copy in copies:
        copy.wait()


def call(kernel, outs, scratch=(), flops=0, moved=0, aliases=None, far=0):
    where = pl.BlockSpec(memory_space=pltpu.VMEM)

    def run(*operands):
        results = pl.pallas_call(
            kernel,
            out_shape=[jax.ShapeDtypeStruct(shape, dtype) for shape, dtype in outs],
            in_specs=[
                pl.BlockSpec(memory_space=pltpu.HBM)
                if a.dtype == jnp.int32 or at in (aliases or ())
                else where
                for at, a in enumerate(operands)
            ],
            out_specs=[pl.BlockSpec(memory_space=pltpu.HBM)] * far + [where] * (len(outs) - far),
            input_output_aliases=aliases or {},
            scratch_shapes=list(scratch),
            compiler_params=pltpu.CompilerParams(vmem_limit_bytes=VMEM_LIMIT),
            cost_estimate=pl.CostEstimate(flops=flops, bytes_accessed=moved, transcendentals=0),
        )(*operands)
        return list(results)

    return run


def neighbours(inner, outer, axis):
    size = lax.axis_size(axis)
    links = [(i, i + 1) for i in range(1, size - 1, 2)]
    links = links + [(j, i) for i, j in links]
    return (pair(inner, axis, 1), lax.ppermute(outer, axis, links))


def pair(array, axis, step):
    return lax.ppermute(array, axis, [(i, i ^ step) for i in range(lax.axis_size(axis))])


def pairs(arrays, axis):
    return [pair(array, axis, step + 1) for step, array in enumerate(arrays)]


def together(*values):
    return lax.optimization_barrier(values)


def on_device(
    video_clip, valid_from, norm_gain, spatial_weight, temporal_weight, mix_weight, cotangent
):
    video = video_clip[0]
    frames, rows, width, channels = video.shape
    outs = frames // 2
    shards = lax.axis_size("tm")
    lines = lax.axis_size("height")
    here = rows // shards
    cells = frames * rows * width
    sizes = dict(frames=frames, rows=rows, width=width)
    gain = norm_gain.reshape(1, channels)
    edge = ((frames, width, channels), BF16)
    halo = pltpu.VMEM((2, frames, width, channels), BF16)

    scalar = [pltpu.SMEM((1,), jnp.int32), pltpu.SemaphoreType.DMA((1,))]
    pieces = call(
        functools.partial(pieces_kernel, outs=outs),
        [((outs + 3, here, width, channels), BF16)] * (shards - 1),
        [pltpu.SemaphoreType.DMA((shards - 1,))],
        moved=1024 * 1024,
    )(cotangent[0])
    *pieces, edges = together(*pieces, video)
    pieces = pairs(pieces, "tm")
    inner, outer = call(
        functools.partial(edges_kernel, rows=rows, frames_first=True),
        [edge, edge],
        [pltpu.SemaphoreType.DMA((2,))],
        moved=512 * 1024,
    )(edges)
    inner, outer = neighbours(inner, outer, "height")

    normed, partial = call(
        functools.partial(own_kernel, **sizes),
        [((cells, channels), BF16), ((cells, channels), F32)],
        scalar,
        flops=18 * cells * channels * channels,
        moved=4 * 1024 * 1024,
    )(valid_from, video, gain, spatial_weight)

    tall, slope, active, parts, stay, leave = call(
        functools.partial(front_kernel, **sizes, shards=shards),
        [
            ((cells + 2 * frames * width, channels), BF16),
            ((cells, channels), F32),
            ((2, cells // 2, channels), BF16),
            (((outs + 1) * rows * width, channels), BF16),
        ]
        + [((1, shards // 2, outs + 1, here, width, channels), BF16)] * 2,
        [halo, *scalar, pltpu.VMEM((shards, outs + 1, here, width, channels), BF16)],
    )(valid_from, normed, partial, inner, outer, gain, spatial_weight, temporal_weight)

    half = channels // 2
    pre_gradient, *low = call(
        functools.partial(middle_kernel, **sizes, shards=shards),
        [
            ((rows, frames, width, channels), BF16),
            ((SPLIT * channels, half), F32),
            ((SPLIT * channels, half), BF16),
        ],
        [pltpu.VMEM((outs + 3, shards, here * width, channels), BF16)],
        flops=20 * cells * channels * channels,
        moved=6 * 1024 * 1024,
    )(
        tall, slope, active, parts, temporal_weight, mix_weight, cotangent[0],
        *reversed(pieces),
    )

    high = call(
        functools.partial(spatial_kernel, **sizes),
        [((size * channels, half), dtype) for size in (15 - SPLIT,) for dtype in (F32, BF16)],
        flops=16 * cells * channels * channels,
        moved=6 * 1024 * 1024,
    )(tall, pre_gradient)

    def shapes(rows_in, *types):
        return [((rows_in, half), dtype) for dtype in types]

    def added(left, right):
        (total,) = call(add_kernel, shapes(left.shape[0], BF16))(left, right)
        return total

    def joined(pieces):
        (total,) = call(join_kernel, [((lines,) + pieces[0].shape, BF16)])(*pieces)
        return total

    def summed(pieces):
        (total,) = call(gather_sum_kernel, shapes(pieces[0].shape[0], BF16))(*pieces)
        return total

    (low, low_send), (high, high_send) = (low, high)
    low_got = pair(low_send, "cam", 1)
    high_got = pair(high_send, "cam", 1)
    size = 15 * channels // lines // 2
    dealt = call(deal_kernel, shapes(size, *([F32] + [BF16] * (lines - 1)) * 2))(
        *[a.reshape(lines, 2, -1, half) for a in (low, low_got, high, high_got)]
    )
    (away, *away_sends), (home, *home_sends) = (dealt[:lines], dealt[lines:])
    away_came = pairs(away_sends, "height")
    home_came = pairs(home_sends, "height")
    came = pair(leave, "tm", 1)
    away, came = together(away, came)
    crossed = pair(summed([away] + away_came[::-1]), "tm", 1)
    pre_gradient, home_came[-1] = together(pre_gradient, home_came[-1])
    total = summed([home] + home_came[::-1] + [crossed])
    inner, outer = call(
        functools.partial(edges_kernel, rows=rows, frames_first=False),
        [edge, edge],
        [pltpu.SemaphoreType.DMA((2,))],
        moved=512 * 1024,
    )(pre_gradient)
    inner, outer = neighbours(inner, outer, "height")
    (halo_rows,) = call(halo_kernel, [((2, frames, width, channels), BF16)])(inner, outer)
    for step in range(1, shards.bit_length() - 1):
        if step > 1:
            total = added(total, other)
        other = pair(total, "tm", 1 << step)
    (video_gradient,) = call(
        functools.partial(input_kernel, **sizes),
        [((frames, rows, width, channels), BF16)],
        [pltpu.VMEM((cells, 3 * channels), BF16)] + scalar,
        flops=18 * cells * channels * channels,
        moved=4 * 1024 * 1024,
    )(valid_from, video, pre_gradient, halo_rows, gain, spatial_weight)
    other, video_gradient = together(other, video_gradient)
    total = added(total, other)
    for step in range(1, shards.bit_length() - 1):
        count, pieces = (2 * stay.shape[0], stay.shape[1] // 2)
        stay, leave = call(split_kernel, [((count, pieces) + stay.shape[2:], BF16)] * 2)(stay, came)
        came = pair(leave, "tm", 1 << step)
    other = pair(total, "tm", 1)
    home_pieces = [total] + pairs([total] * (lines - 1), "height")
    away_pieces = [other] + pairs([other] * (lines - 1), "height")
    home = joined(home_pieces)
    (encoded,) = call(
        functools.partial(encode_kernel, width=width, shards=shards),
        [((shards * outs, here, width, channels), BF16)],
        [
            pltpu.VMEM(((shards * outs + 2) * here * width, channels), BF16),
            pltpu.VMEM((shards, outs + 1, here, width, channels), BF16),
        ],
        flops=3 * cells * channels * channels,
        moved=2 * 1024 * 1024,
    )(mix_weight, stay, came)
    away_pieces[-1], home, video_gradient, encoded = together(
        away_pieces[-1], home, video_gradient, encoded
    )
    away = joined(away_pieces)
    own = (home, away)
    others = (pair(home, "cam", 1), pair(away, "cam", 1))

    cell_count = cells * lax.axis_size("cam") * shards * lines
    scale = 1.0 / math.sqrt(cell_count)
    results = [((9, channels, channels), F32)] + [((3, channels, channels), F32)] * 2
    staged = pltpu.VMEM((15 * channels, half), F32)
    *results_own, total = call(
        functools.partial(finish_kernel, scale=scale, last=False),
        results + [((channels, half), F32)],
        [staged, pltpu.SemaphoreType.DMA((15,))],
        moved=4 * 1024 * 1024,
        far=3,
    )(*own, spatial_weight)
    spatial, temporal, mix, gain_gradient = call(
        functools.partial(finish_kernel, scale=scale, last=True),
        results + [((1, channels), F32)],
        [staged, pltpu.VMEM((1, channels), F32), pltpu.SemaphoreType.DMA((16,))],
        moved=4 * 1024 * 1024,
        far=4,
        aliases={5 + at: at for at in range(3)},
    )(*others, spatial_weight, total, gain, *results_own)

    return (
        encoded[None],
        video_gradient[None],
        spatial.reshape(spatial_weight.shape),
        temporal,
        mix,
        gain_gradient.reshape(channels),
    )


def solution(mesh):
    return jax.shard_map(
        on_device,
        mesh=mesh,
        in_specs=(
            P("cam", "tm", "height", None, None),
            P("cam"),
            P(),
            P(),
            P(),
            P(),
            P("cam", None, ("height", "tm"), None, None),
        ),
        out_specs=(
            P("cam", None, ("height", "tm"), None, None),
            P("cam", "tm", "height", None, None),
            P(),
            P(),
            P(),
            P(),
        ),
        check_vma=False,
    )
```

```python
import functools
import math

import jax
import jax.numpy as jnp
from jax import lax
from jax.experimental import pallas as pl
from jax.experimental.pallas import tpu as pltpu
from jax.sharding import PartitionSpec as P

F32 = jnp.float32
BF16 = jnp.bfloat16
VMEM_LIMIT = 16 * 1024 * 1024
SPLIT = 8


def dot(left, right):
    return jnp.dot(left, right, preferred_element_type=F32)


def dot_nt(left, right):
    return lax.dot_general(left, right, (((1,), (1,)), ((), ())), preferred_element_type=F32)


def dot_tn(left, right):
    return lax.dot_general(left, right, (((0,), (0,)), ((), ())), preferred_element_type=F32)


def from_left(cells, width):
    column = lax.broadcasted_iota(jnp.int32, cells.shape, 0) % width
    return jnp.where(column == 0, 0.0, pltpu.roll(cells, 1, 0))


def from_right(cells, width):
    column = lax.broadcasted_iota(jnp.int32, cells.shape, 0) % width
    return jnp.where(column == width - 1, 0.0, pltpu.roll(cells, cells.shape[0] - 1, 0))


def present(start, frame, frames):
    return (lax.axis_index("tm") * frames + frame >= start[0]).astype(F32)


def normalised(tile, keep):
    values = tile.astype(F32) * keep
    inverse = lax.rsqrt(jnp.mean(values * values, axis=-1, keepdims=True) + 1e-06)
    return (values * inverse, inverse)


def first_frame(shard, outs, span, total):
    return jnp.minimum(shard * outs, total - span)


def run_copies(pairs_of_refs, done):
    copies = [
        pltpu.make_async_copy(source, target, done.at[at])
        for at, (source, target) in enumerate(pairs_of_refs)
    ]
    for copy in copies:
        copy.start()
    for copy in copies:
        copy.wait()


def pieces_kernel(cotangent, *refs, outs):
    pieces, done = (refs[:-1], refs[-1])
    span = outs + 3
    me = lax.axis_index("tm")
    copies = []
    for step, piece in enumerate(pieces):
        begin = first_frame(me ^ (step + 1), outs, span, cotangent.shape[0])
        copies.append((cotangent.at[pl.ds(begin, span)], piece))
    run_copies(copies, done)


def edges_kernel(source, inner, outer, done, *, rows, frames_first):
    odd = lax.axis_index("height") % 2

    def row(at):
        return source.at[:, at] if frames_first else source.at[at]

    run_copies(
        [(row((1 - odd) * (rows - 1)), inner), (row(odd * (rows - 1)), outer)], done
    )


def first_frame(shard, outs, span, total):
    return jnp.minimum(shard * outs, total - span)


def place_halos(halo, inner, outer):
    odd = lax.axis_index("height") % 2
    halo[1 - odd] = inner[...]
    halo[odd] = outer[...]


def column_sum(cells, weight, taps, width):
    products = [
        dot(cells, jnp.concatenate([weight[i, j] for i in taps], axis=0)) for j in range(3)
    ]
    return from_left(products[0], width) + products[1] + from_right(products[2], width)


def halo_kernel(inner, outer, halo):
    place_halos(halo, inner, outer)


def own_kernel(
    valid_from, video, gain, weight, normed, partial, start, done, *, frames, rows, width
):
    run_copies([(valid_from, start)], done)
    block = frames * width
    for row in range(rows):
        for frame in range(frames):
            unit, _ = normalised(video[frame, row], present(start, frame, frames))
            at = row * block + frame * width
            normed[at : at + width] = (unit * gain[...]).astype(BF16)
    for row in range(rows):
        taps = [i for i in range(3) if 0 <= row + i - 1 < rows]
        cells = [normed[(row + i - 1) * block : (row + i) * block] for i in taps]
        partial[row * block : row * block + block] = column_sum(
            jnp.concatenate(cells, axis=1), weight, taps, width
        )


def front_kernel(
    valid_from, normed, partial, inner, outer, gain, weight, temporal, *refs,
    frames, rows, width, shards
):
    tall, slope, active, parts, *refs = refs
    strided, (halo, start, done, lines) = (refs[:2], refs[2:])
    outs = frames // 2
    plane = rows * width
    here = rows // shards
    block = frames * width

    run_copies([(valid_from, start)], done)
    place_halos(halo, inner, outer)
    tall[block : block + rows * block] = normed[...]
    for side, at in ((0, 0), (1, (rows + 1) * block)):
        for frame in range(frames):
            unit, _ = normalised(halo[side, frame], present(start, frame, frames))
            to = at + frame * width
            tall[to : to + width] = (unit * gain[...]).astype(BF16)
    for row in range(rows):
        pre = partial[row * block : row * block + block]
        if row == 0:
            pre = pre + column_sum(tall[:block], weight, [0], width)
        if row == rows - 1:
            pre = pre + column_sum(tall[(rows + 1) * block :], weight, [2], width)
        sigmoid = 1.0 / (1.0 + jnp.exp(-pre))
        slope[row * block : row * block + block] = sigmoid * (1.0 + pre * (1.0 - sigmoid))
        cells = (pre * sigmoid).astype(BF16)
        for frame in range(frames):
            at = (frame // 2) * plane + row * width
            active[frame % 2, at : at + width] = cells[frame * width : frame * width + width]
    evens = active[0]
    odds = active[1]
    carried = dot(odds, temporal[2])
    mixed = dot(odds, temporal[0]) + dot(evens, temporal[1])
    pieces = [mixed[:plane]]
    for s in range(1, outs):
        pieces.append(
            mixed[s * plane : s * plane + plane] + carried[(s - 1) * plane : s * plane]
        )
    pieces.append(carried[(outs - 1) * plane :])
    pieces = jnp.concatenate(pieces, axis=0).astype(BF16)
    parts[...] = pieces
    for frame in range(outs + 1):
        cells = pieces[frame * plane : frame * plane + plane]
        lines[:, frame] = cells.reshape(shards, here, width, 256)
    stay, leave = strided
    for step in range(shards):
        target = leave if step % 2 else stay
        target[0, step // 2] = lines[lax.axis_index("tm") ^ step]


def split_kernel(stay_in, came_in, stay, leave):
    count, pieces = stay_in.shape[:2]
    for place, source in enumerate((stay_in, came_in)):
        for at in range(count):
            for piece in range(pieces):
                target = leave if piece % 2 else stay
                target[place * count + at, piece // 2] = source[at, piece]


def middle_kernel(
    tall, slope, active, parts, temporal, mix, cotangent, *refs, frames, rows, width, shards
):
    pieces, refs = (refs[: shards - 1], refs[shards - 1 :])
    pre_gradient, keep, send, cot = refs
    outs = frames // 2
    plane = rows * width
    here = rows // shards
    me = lax.axis_index("tm")
    total = shards * outs
    cut = outs + 3
    skip = me * outs - first_frame(me, outs, cut, total)
    for frame in range(cut):
        here_is = (me * outs + frame < total).astype(F32)
        own = cotangent[jnp.minimum(me * outs + frame, total - 1)]
        others = [piece[jnp.minimum(frame + skip, cut - 1)] for piece in pieces]
        for step, cells in enumerate([own] + others[::-1]):
            cells = (cells.astype(F32) * here_is).astype(BF16)
            cot[frame, me ^ step] = cells.reshape(here * width, 256)

    def ahead(k, count=outs + 1):
        return cot[k : k + count].reshape(count * plane, 256)

    gradient = ahead(0).astype(F32)
    for k in range(3):
        gradient = gradient + dot_nt(ahead(k), mix[k])
    gradient = gradient.astype(BF16)
    now = gradient[: outs * plane]
    later = gradient[plane:]
    even_gradient = dot_nt(now, temporal[1])
    odd_gradient = dot_nt(now, temporal[0]) + dot_nt(later, temporal[2])
    for row in range(rows):
        for frame in range(frames):
            source = odd_gradient if frame % 2 else even_gradient
            at = (frame // 2) * plane + row * width
            to = (row * frames + frame) * width
            tile = (source[at : at + width] * slope[to : to + width]).astype(BF16)
            pre_gradient[row, frame] = tile
    evens = active[0]
    odds = active[1]
    for k in range(3):
        deliver(keep, send, k, dot_tn(parts[...], ahead(k)))
    deliver(keep, send, 3, dot_tn(odds, now))
    deliver(keep, send, 4, dot_tn(evens, now))
    deliver(keep, send, 5, dot_tn(odds, later))
    block = frames * width
    spatial_sums(tall, pre_gradient, keep, send, 6, range(SPLIT - 6), block, rows, width)


def spatial_kernel(tall, pre_gradient, keep, send, *, frames, rows, width):
    block = frames * width
    spatial_sums(tall, pre_gradient, keep, send, 0, range(SPLIT - 6, 9), block, rows, width)


def spatial_sums(tall, pre_gradient, keep, send, first, taps, block, rows, width):
    columns = column_shifts(pre_gradient, width)
    for i in range(3):
        here = [tap for tap in taps if tap // 3 == i]
        if not here:
            continue
        cells = tall[i * block : (i + rows) * block]
        product = dot_tn(cells, jnp.concatenate([columns[tap % 3] for tap in here], axis=1))
        for place, tap in enumerate(here):
            index = first + tap - taps[0]
            deliver(keep, send, index, product[:, place * 256 : place * 256 + 256])


def column_shifts(pre_gradient, width):
    gradient = pre_gradient[...].reshape(-1, 256)
    exact = gradient.astype(F32)
    left = from_right(exact, width).astype(BF16)
    right = from_left(exact, width).astype(BF16)
    return [left, gradient, right]


def deliver(keep, send, index, product):
    first = jnp.full((256, 128), lax.axis_index("cam")) == 0
    low, high = (product[:, :128], product[:, 128:])
    at = index * 256
    keep[at : at + 256] = jnp.where(first, low, high)
    send[at : at + 256] = jnp.where(first, high, low).astype(BF16)


def core_columns():
    mine = pl.ds(pl.multiple_of(lax.axis_index("cam") * 128, 128), 128)
    other = pl.ds(pl.multiple_of((1 - lax.axis_index("cam")) * 128, 128), 128)
    return (mine, other)


def deal_kernel(low, low_got, high, high_got, *outs):
    me = lax.axis_index("height")
    home = lax.axis_index("tm") % 2
    cut = low.shape[2]
    count = len(outs) // 2
    for target, half in [(outs[:count], 1 - home), (outs[count:], home)]:
        for step, out in enumerate(target):
            at = me ^ step
            out[:cut] = (low[at, half] + low_got[at, half].astype(F32)).astype(out.dtype)
            out[cut:] = (high[at, half] + high_got[at, half].astype(F32)).astype(out.dtype)


def gather_sum_kernel(kept, *refs):
    value = kept[...]
    for piece in refs[:-1]:
        value = value + piece[...].astype(F32)
    refs[-1][...] = value.astype(BF16)


def add_kernel(left, right, out):
    out[...] = (left[...].astype(F32) + right[...].astype(F32)).astype(BF16)


def join_kernel(*refs):
    for step, piece in enumerate(refs[:-1]):
        refs[-1][lax.axis_index("height") ^ step] = piece[...]


def input_kernel(
    valid_from, video, pre_gradient, halo, gain, weight, out, tall, start, done,
    *, frames, rows, width
):
    run_copies([(valid_from, start)], done)
    block = frames * width
    for row in range(-1, rows + 1):
        if row < 0:
            cells = halo[0]
        elif row == rows:
            cells = halo[1]
        else:
            cells = pre_gradient[row]
        cells = cells.reshape(block, 256)
        for tap in range(3):
            target = row - 1 + tap
            if 0 <= target < rows:
                tall[target * block : target * block + block, tap * 256 : tap * 256 + 256] = cells
    for row in range(rows):
        cells = tall[row * block : row * block + block]
        taps = [
            dot_nt(cells, jnp.concatenate([weight[0, j], weight[1, j], weight[2, j]], axis=1))
            for j in range(3)
        ]
        gradient = from_right(taps[0], width) + taps[1] + from_left(taps[2], width)
        gradient = gradient * gain[...]
        for frame in range(frames):
            keep = present(start, frame, frames)
            unit, inverse = normalised(video[frame, row], keep)
            tile = gradient[frame * width : frame * width + width]
            mean = jnp.mean(tile * unit, axis=-1, keepdims=True)
            out[frame, row] = (inverse * (tile - unit * mean) * keep).astype(BF16)


def encode_kernel(mix, stay, came, out, line, strided, *, width, shards):
    for step in range(shards):
        source = came if step >= shards // 2 else stay
        strided[lax.axis_index("tm") ^ step] = source[step % (shards // 2), 0]
    parts, here = strided.shape[1:3]
    outs = parts - 1
    plane = here * width
    total = shards * outs
    for frame in range(total):
        shard, part = (frame // outs, frame % outs)
        cells = strided[shard, part].reshape(plane, 256)
        if part == 0 and shard > 0:
            carried = strided[shard - 1, outs].reshape(plane, 256)
            cells = (cells.astype(F32) + carried.astype(F32)).astype(BF16)
        line[(frame + 2) * plane : (frame + 3) * plane] = cells
    line[0 : 2 * plane] = jnp.zeros((2 * plane, 256), BF16)
    span = total * plane
    result = line[2 * plane : 2 * plane + span].astype(F32)
    for k in range(3):
        result = result + dot(line[(2 - k) * plane : (2 - k) * plane + span], mix[k])
    out[...] = result.astype(BF16).reshape(out.shape)


def finish_kernel(home, away, weight, *refs, scale, last):
    if last:
        before, gain, _, _, _, spatial, temporal, mix, gain_out, staged, row, done = refs
        total = before[...]
    else:
        spatial, temporal, mix, after, staged, done = refs
        total = jnp.zeros((256, 128), F32)
    columns = core_columns()[1 if last else 0]
    parts = home.shape[0]
    low, high = (SPLIT * 128 // parts, (15 - SPLIT) * 128 // parts)
    mine = lax.axis_index("tm") % 2
    for half, source in ((mine, home), (1 - mine, away)):
        for part in range(parts):
            at = pl.multiple_of((2 * part + half) * low, low)
            staged[pl.ds(at, low)] = source[part, :low].astype(F32) * scale
            at = pl.multiple_of(SPLIT * 256 + (2 * part + half) * high, high)
            staged[pl.ds(at, high)] = source[part, low:].astype(F32) * scale
    results = [(mix, k) for k in range(3)] + [(temporal, k) for k in range(3)]
    results = results + [(spatial, k) for k in range(9)]
    copies = []
    for index, (result, k) in enumerate(results):
        cells = staged.at[pl.ds(index * 256, 256)]
        copies.append(pltpu.make_async_copy(cells, result.at[k, :, columns], done.at[index]))
        copies[-1].start()
    for k in range(9):
        cells = staged[1536 + k * 256 : 1792 + k * 256]
        total = total + cells * weight[k // 3, k % 3, :, columns].astype(F32)
    if last:
        upper = total.astype(BF16)
        lower = (total - upper.astype(F32)).astype(BF16)
        ones = jnp.ones((16, 128), BF16)
        row[...] = (dot_nt(ones, upper) + dot_nt(ones, lower))[:1] / gain[...]
        copies.append(pltpu.make_async_copy(row, gain_out, done.at[15]))
        copies[-1].start()
    else:
        after[...] = total
    for copy in copies:
        copy.wait()


def call(kernel, outs, scratch=(), flops=0, moved=0, aliases=None, far=0):
    where = pl.BlockSpec(memory_space=pltpu.VMEM)

    def run(*operands):
        results = pl.pallas_call(
            kernel,
            out_shape=[jax.ShapeDtypeStruct(shape, dtype) for shape, dtype in outs],
            in_specs=[
                pl.BlockSpec(memory_space=pltpu.HBM)
                if a.dtype == jnp.int32 or at in (aliases or ())
                else where
                for at, a in enumerate(operands)
            ],
            out_specs=[pl.BlockSpec(memory_space=pltpu.HBM)] * far + [where] * (len(outs) - far),
            input_output_aliases=aliases or {},
            scratch_shapes=list(scratch),
            compiler_params=pltpu.CompilerParams(vmem_limit_bytes=VMEM_LIMIT),
            cost_estimate=pl.CostEstimate(flops=flops, bytes_accessed=moved, transcendentals=0),
        )(*operands)
        return list(results)

    return run


def neighbours(inner, outer, axis):
    size = lax.axis_size(axis)
    links = [(i, i + 1) for i in range(1, size - 1, 2)]
    links = links + [(j, i) for i, j in links]
    return (pair(inner, axis, 1), lax.ppermute(outer, axis, links))


def pair(array, axis, step):
    return lax.ppermute(array, axis, [(i, i ^ step) for i in range(lax.axis_size(axis))])


def pairs(arrays, axis):
    return [pair(array, axis, step + 1) for step, array in enumerate(arrays)]


def together(*values):
    return lax.optimization_barrier(values)


def on_device(
    video_clip, valid_from, norm_gain, spatial_weight, temporal_weight, mix_weight, cotangent
):
    video = video_clip[0]
    frames, rows, width, channels = video.shape
    outs = frames // 2
    shards = lax.axis_size("tm")
    lines = lax.axis_size("height")
    here = rows // shards
    cells = frames * rows * width
    sizes = dict(frames=frames, rows=rows, width=width)
    gain = norm_gain.reshape(1, channels)
    edge = ((frames, width, channels), BF16)
    halo = pltpu.VMEM((2, frames, width, channels), BF16)

    scalar = [pltpu.SMEM((1,), jnp.int32), pltpu.SemaphoreType.DMA((1,))]
    pieces = call(
        functools.partial(pieces_kernel, outs=outs),
        [((outs + 3, here, width, channels), BF16)] * (shards - 1),
        [pltpu.SemaphoreType.DMA((shards - 1,))],
        moved=1024 * 1024,
    )(cotangent[0])
    *pieces, edges = together(*pieces, video)
    pieces = pairs(pieces, "tm")
    inner, outer = call(
        functools.partial(edges_kernel, rows=rows, frames_first=True),
        [edge, edge],
        [pltpu.SemaphoreType.DMA((2,))],
        moved=512 * 1024,
    )(edges)
    inner, outer = neighbours(inner, outer, "height")

    normed, partial = call(
        functools.partial(own_kernel, **sizes),
        [((cells, channels), BF16), ((cells, channels), F32)],
        scalar,
        flops=18 * cells * channels * channels,
        moved=4 * 1024 * 1024,
    )(valid_from, video, gain, spatial_weight)

    tall, slope, active, parts, stay, leave = call(
        functools.partial(front_kernel, **sizes, shards=shards),
        [
            ((cells + 2 * frames * width, channels), BF16),
            ((cells, channels), F32),
            ((2, cells // 2, channels), BF16),
            (((outs + 1) * rows * width, channels), BF16),
        ]
        + [((1, shards // 2, outs + 1, here, width, channels), BF16)] * 2,
        [halo, *scalar, pltpu.VMEM((shards, outs + 1, here, width, channels), BF16)],
    )(valid_from, normed, partial, inner, outer, gain, spatial_weight, temporal_weight)

    half = channels // 2
    pre_gradient, *low = call(
        functools.partial(middle_kernel, **sizes, shards=shards),
        [
            ((rows, frames, width, channels), BF16),
            ((SPLIT * channels, half), F32),
            ((SPLIT * channels, half), BF16),
        ],
        [pltpu.VMEM((outs + 3, shards, here * width, channels), BF16)],
        flops=20 * cells * channels * channels,
        moved=6 * 1024 * 1024,
    )(
        tall, slope, active, parts, temporal_weight, mix_weight, cotangent[0],
        *reversed(pieces),
    )

    high = call(
        functools.partial(spatial_kernel, **sizes),
        [((size * channels, half), dtype) for size in (15 - SPLIT,) for dtype in (F32, BF16)],
        flops=16 * cells * channels * channels,
        moved=6 * 1024 * 1024,
    )(tall, pre_gradient)

    def shapes(rows_in, *types):
        return [((rows_in, half), dtype) for dtype in types]

    def added(left, right):
        (total,) = call(add_kernel, shapes(left.shape[0], BF16))(left, right)
        return total

    def joined(pieces):
        (total,) = call(join_kernel, [((lines,) + pieces[0].shape, BF16)])(*pieces)
        return total

    def summed(pieces):
        (total,) = call(gather_sum_kernel, shapes(pieces[0].shape[0], BF16))(*pieces)
        return total

    (low, low_send), (high, high_send) = (low, high)
    low_got = pair(low_send, "cam", 1)
    high_got = pair(high_send, "cam", 1)
    size = 15 * channels // lines // 2
    dealt = call(deal_kernel, shapes(size, *([F32] + [BF16] * (lines - 1)) * 2))(
        *[a.reshape(lines, 2, -1, half) for a in (low, low_got, high, high_got)]
    )
    (away, *away_sends), (home, *home_sends) = (dealt[:lines], dealt[lines:])
    away_came = pairs(away_sends, "height")
    home_came = pairs(home_sends, "height")
    came = pair(leave, "tm", 1)
    away, came = together(away, came)
    crossed = pair(summed([away] + away_came[::-1]), "tm", 1)
    pre_gradient, home_came[-1] = together(pre_gradient, home_came[-1])
    total = summed([home] + home_came[::-1] + [crossed])
    inner, outer = call(
        functools.partial(edges_kernel, rows=rows, frames_first=False),
        [edge, edge],
        [pltpu.SemaphoreType.DMA((2,))],
        moved=512 * 1024,
    )(pre_gradient)
    inner, outer = neighbours(inner, outer, "height")
    (halo_rows,) = call(halo_kernel, [((2, frames, width, channels), BF16)])(inner, outer)
    for step in range(1, shards.bit_length() - 1):
        if step > 1:
            total = added(total, other)
        other = pair(total, "tm", 1 << step)
    (video_gradient,) = call(
        functools.partial(input_kernel, **sizes),
        [((frames, rows, width, channels), BF16)],
        [pltpu.VMEM((cells, 3 * channels), BF16)] + scalar,
        flops=18 * cells * channels * channels,
        moved=4 * 1024 * 1024,
    )(valid_from, video, pre_gradient, halo_rows, gain, spatial_weight)
    video_gradient, stay, came = together(video_gradient, stay, came)
    other, video_gradient = together(other, video_gradient)
    total = added(total, other)
    for step in range(1, shards.bit_length() - 1):
        count, pieces = (2 * stay.shape[0], stay.shape[1] // 2)
        stay, leave = call(split_kernel, [((count, pieces) + stay.shape[2:], BF16)] * 2)(stay, came)
        came = pair(leave, "tm", 1 << step)
    other = pair(total, "tm", 1)
    home_pieces = [total] + pairs([total] * (lines - 1), "height")
    away_pieces = [other] + pairs([other] * (lines - 1), "height")
    home = joined(home_pieces)
    (encoded,) = call(
        functools.partial(encode_kernel, width=width, shards=shards),
        [((shards * outs, here, width, channels), BF16)],
        [
            pltpu.VMEM(((shards * outs + 2) * here * width, channels), BF16),
            pltpu.VMEM((shards, outs + 1, here, width, channels), BF16),
        ],
        flops=3 * cells * channels * channels,
        moved=2 * 1024 * 1024,
    )(mix_weight, stay, came)
    away_pieces[-1], home, video_gradient, encoded = together(
        away_pieces[-1], home, video_gradient, encoded
    )
    away = joined(away_pieces)
    own = (home, away)
    others = (pair(home, "cam", 1), pair(away, "cam", 1))

    cell_count = cells * lax.axis_size("cam") * shards * lines
    scale = 1.0 / math.sqrt(cell_count)
    results = [((9, channels, channels), F32)] + [((3, channels, channels), F32)] * 2
    staged = pltpu.VMEM((15 * channels, half), F32)
    *results_own, total = call(
        functools.partial(finish_kernel, scale=scale, last=False),
        results + [((channels, half), F32)],
        [staged, pltpu.SemaphoreType.DMA((15,))],
        moved=4 * 1024 * 1024,
        far=3,
    )(*own, spatial_weight)
    spatial, temporal, mix, gain_gradient = call(
        functools.partial(finish_kernel, scale=scale, last=True),
        results + [((1, channels), F32)],
        [staged, pltpu.VMEM((1, channels), F32), pltpu.SemaphoreType.DMA((16,))],
        moved=4 * 1024 * 1024,
        far=4,
        aliases={5 + at: at for at in range(3)},
    )(*others, spatial_weight, total, gain, *results_own)

    return (
        encoded[None],
        video_gradient[None],
        spatial.reshape(spatial_weight.shape),
        temporal,
        mix,
        gain_gradient.reshape(channels),
    )


def solution(mesh):
    return jax.shard_map(
        on_device,
        mesh=mesh,
        in_specs=(
            P("cam", "tm", "height", None, None),
            P("cam"),
            P(),
            P(),
            P(),
            P(),
            P("cam", None, ("height", "tm"), None, None),
        ),
        out_specs=(
            P("cam", None, ("height", "tm"), None, None),
            P("cam", "tm", "height", None, None),
            P(),
            P(),
            P(),
            P(),
        ),
        check_vma=False,
    )
```

```python
import functools
import math

import jax
import jax.numpy as jnp
from jax import lax
from jax.experimental import pallas as pl
from jax.experimental.pallas import tpu as pltpu
from jax.sharding import PartitionSpec as P

F32 = jnp.float32
BF16 = jnp.bfloat16
VMEM_LIMIT = 16 * 1024 * 1024
SPLIT = 10


def dot(left, right):
    return jnp.dot(left, right, preferred_element_type=F32)


def dot_nt(left, right):
    return lax.dot_general(left, right, (((1,), (1,)), ((), ())), preferred_element_type=F32)


def dot_tn(left, right):
    return lax.dot_general(left, right, (((0,), (0,)), ((), ())), preferred_element_type=F32)


def from_left(cells, width):
    column = lax.broadcasted_iota(jnp.int32, cells.shape, 0) % width
    return jnp.where(column == 0, 0.0, pltpu.roll(cells, 1, 0))


def from_right(cells, width):
    column = lax.broadcasted_iota(jnp.int32, cells.shape, 0) % width
    return jnp.where(column == width - 1, 0.0, pltpu.roll(cells, cells.shape[0] - 1, 0))


def present(start, frame, frames):
    return (lax.axis_index("tm") * frames + frame >= start[0]).astype(F32)


def normalised(tile, keep):
    values = tile.astype(F32) * keep
    inverse = lax.rsqrt(jnp.mean(values * values, axis=-1, keepdims=True) + 1e-06)
    return (values * inverse, inverse)


def first_frame(shard, outs, span, total):
    return jnp.minimum(shard * outs, total - span)


def run_copies(pairs_of_refs, done):
    copies = [
        pltpu.make_async_copy(source, target, done.at[at])
        for at, (source, target) in enumerate(pairs_of_refs)
    ]
    for copy in copies:
        copy.start()
    for copy in copies:
        copy.wait()


def pieces_kernel(cotangent, *refs, outs):
    pieces, done = (refs[:-1], refs[-1])
    span = outs + 3
    me = lax.axis_index("tm")
    copies = []
    for step, piece in enumerate(pieces):
        begin = first_frame(me ^ (step + 1), outs, span, cotangent.shape[0])
        copies.append((cotangent.at[pl.ds(begin, span)], piece))
    run_copies(copies, done)


def edges_kernel(source, inner, outer, done, *, rows, frames_first):
    odd = lax.axis_index("height") % 2

    def row(at):
        return source.at[:, at] if frames_first else source.at[at]

    run_copies(
        [(row((1 - odd) * (rows - 1)), inner), (row(odd * (rows - 1)), outer)], done
    )


def first_frame(shard, outs, span, total):
    return jnp.minimum(shard * outs, total - span)


def place_halos(halo, inner, outer):
    odd = lax.axis_index("height") % 2
    halo[1 - odd] = inner[...]
    halo[odd] = outer[...]


def column_sum(cells, weight, taps, width):
    products = [
        dot(cells, jnp.concatenate([weight[i, j] for i in taps], axis=0)) for j in range(3)
    ]
    return from_left(products[0], width) + products[1] + from_right(products[2], width)


def halo_kernel(inner, outer, halo):
    place_halos(halo, inner, outer)


def own_kernel(
    valid_from, video, gain, weight, normed, partial, start, done, *, frames, rows, width
):
    run_copies([(valid_from, start)], done)
    block = frames * width
    for row in range(rows):
        for frame in range(frames):
            unit, _ = normalised(video[frame, row], present(start, frame, frames))
            at = row * block + frame * width
            normed[at : at + width] = (unit * gain[...]).astype(BF16)
    for row in range(rows):
        taps = [i for i in range(3) if 0 <= row + i - 1 < rows]
        cells = [normed[(row + i - 1) * block : (row + i) * block] for i in taps]
        partial[row * block : row * block + block] = column_sum(
            jnp.concatenate(cells, axis=1), weight, taps, width
        )


def front_kernel(
    valid_from, normed, partial, inner, outer, gain, weight, temporal, *refs,
    frames, rows, width, shards
):
    tall, slope, active, parts, *refs = refs
    strided, (halo, start, done, lines) = (refs[:2], refs[2:])
    outs = frames // 2
    plane = rows * width
    here = rows // shards
    block = frames * width

    run_copies([(valid_from, start)], done)
    place_halos(halo, inner, outer)
    tall[block : block + rows * block] = normed[...]
    for side, at in ((0, 0), (1, (rows + 1) * block)):
        for frame in range(frames):
            unit, _ = normalised(halo[side, frame], present(start, frame, frames))
            to = at + frame * width
            tall[to : to + width] = (unit * gain[...]).astype(BF16)
    for row in range(rows):
        pre = partial[row * block : row * block + block]
        if row == 0:
            pre = pre + column_sum(tall[:block], weight, [0], width)
        if row == rows - 1:
            pre = pre + column_sum(tall[(rows + 1) * block :], weight, [2], width)
        sigmoid = 1.0 / (1.0 + jnp.exp(-pre))
        slope[row * block : row * block + block] = sigmoid * (1.0 + pre * (1.0 - sigmoid))
        cells = (pre * sigmoid).astype(BF16)
        for frame in range(frames):
            at = (frame // 2) * plane + row * width
            active[frame % 2, at : at + width] = cells[frame * width : frame * width + width]
    evens = active[0]
    odds = active[1]
    carried = dot(odds, temporal[2])
    mixed = dot(odds, temporal[0]) + dot(evens, temporal[1])
    pieces = [mixed[:plane]]
    for s in range(1, outs):
        pieces.append(
            mixed[s * plane : s * plane + plane] + carried[(s - 1) * plane : s * plane]
        )
    pieces.append(carried[(outs - 1) * plane :])
    pieces = jnp.concatenate(pieces, axis=0).astype(BF16)
    parts[...] = pieces
    for frame in range(outs + 1):
        cells = pieces[frame * plane : frame * plane + plane]
        lines[:, frame] = cells.reshape(shards, here, width, 256)
    stay, leave = strided
    for step in range(shards):
        target = leave if step % 2 else stay
        target[0, step // 2] = lines[lax.axis_index("tm") ^ step]


def split_kernel(stay_in, came_in, stay, leave):
    count, pieces = stay_in.shape[:2]
    for place, source in enumerate((stay_in, came_in)):
        for at in range(count):
            for piece in range(pieces):
                target = leave if piece % 2 else stay
                target[place * count + at, piece // 2] = source[at, piece]


def middle_kernel(
    tall, slope, active, parts, temporal, mix, cotangent, *refs, frames, rows, width, shards
):
    pieces, refs = (refs[: shards - 1], refs[shards - 1 :])
    pre_gradient, keep, send, cot = refs
    outs = frames // 2
    plane = rows * width
    here = rows // shards
    me = lax.axis_index("tm")
    total = shards * outs
    cut = outs + 3
    skip = me * outs - first_frame(me, outs, cut, total)
    for frame in range(cut):
        here_is = (me * outs + frame < total).astype(F32)
        own = cotangent[jnp.minimum(me * outs + frame, total - 1)]
        others = [piece[jnp.minimum(frame + skip, cut - 1)] for piece in pieces]
        for step, cells in enumerate([own] + others[::-1]):
            cells = (cells.astype(F32) * here_is).astype(BF16)
            cot[frame, me ^ step] = cells.reshape(here * width, 256)

    def ahead(k, count=outs + 1):
        return cot[k : k + count].reshape(count * plane, 256)

    gradient = ahead(0).astype(F32)
    for k in range(3):
        gradient = gradient + dot_nt(ahead(k), mix[k])
    gradient = gradient.astype(BF16)
    now = gradient[: outs * plane]
    later = gradient[plane:]
    even_gradient = dot_nt(now, temporal[1])
    odd_gradient = dot_nt(now, temporal[0]) + dot_nt(later, temporal[2])
    for row in range(rows):
        for frame in range(frames):
            source = odd_gradient if frame % 2 else even_gradient
            at = (frame // 2) * plane + row * width
            to = (row * frames + frame) * width
            tile = (source[at : at + width] * slope[to : to + width]).astype(BF16)
            pre_gradient[row, frame] = tile
    evens = active[0]
    odds = active[1]
    for k in range(3):
        deliver(keep, send, k, dot_tn(parts[...], ahead(k)))
    deliver(keep, send, 3, dot_tn(odds, now))
    deliver(keep, send, 4, dot_tn(evens, now))
    deliver(keep, send, 5, dot_tn(odds, later))
    block = frames * width
    spatial_sums(tall, pre_gradient, keep, send, 6, range(SPLIT - 6), block, rows, width)


def spatial_kernel(tall, pre_gradient, keep, send, *, frames, rows, width):
    block = frames * width
    spatial_sums(tall, pre_gradient, keep, send, 0, range(SPLIT - 6, 9), block, rows, width)


def spatial_sums(tall, pre_gradient, keep, send, first, taps, block, rows, width):
    columns = column_shifts(pre_gradient, width)
    for i in range(3):
        here = [tap for tap in taps if tap // 3 == i]
        if not here:
            continue
        cells = tall[i * block : (i + rows) * block]
        product = dot_tn(cells, jnp.concatenate([columns[tap % 3] for tap in here], axis=1))
        for place, tap in enumerate(here):
            index = first + tap - taps[0]
            deliver(keep, send, index, product[:, place * 256 : place * 256 + 256])


def column_shifts(pre_gradient, width):
    gradient = pre_gradient[...].reshape(-1, 256)
    exact = gradient.astype(F32)
    left = from_right(exact, width).astype(BF16)
    right = from_left(exact, width).astype(BF16)
    return [left, gradient, right]


def deliver(keep, send, index, product):
    first = jnp.full((256, 128), lax.axis_index("cam")) == 0
    low, high = (product[:, :128], product[:, 128:])
    at = index * 256
    keep[at : at + 256] = jnp.where(first, low, high)
    send[at : at + 256] = jnp.where(first, high, low).astype(BF16)


def core_columns():
    mine = pl.ds(pl.multiple_of(lax.axis_index("cam") * 128, 128), 128)
    other = pl.ds(pl.multiple_of((1 - lax.axis_index("cam")) * 128, 128), 128)
    return (mine, other)


def deal_kernel(low, low_got, high, high_got, *outs):
    me = lax.axis_index("height")
    home = lax.axis_index("tm") % 2
    cut = low.shape[2]
    count = len(outs) // 2
    for target, half in [(outs[:count], 1 - home), (outs[count:], home)]:
        for step, out in enumerate(target):
            at = me ^ step
            out[:cut] = (low[at, half] + low_got[at, half].astype(F32)).astype(out.dtype)
            out[cut:] = (high[at, half] + high_got[at, half].astype(F32)).astype(out.dtype)


def gather_sum_kernel(kept, *refs):
    value = kept[...]
    for piece in refs[:-1]:
        value = value + piece[...].astype(F32)
    refs[-1][...] = value.astype(BF16)


def add_kernel(left, right, out):
    out[...] = (left[...].astype(F32) + right[...].astype(F32)).astype(BF16)


def join_kernel(*refs):
    for step, piece in enumerate(refs[:-1]):
        refs[-1][lax.axis_index("height") ^ step] = piece[...]


def input_kernel(
    valid_from, video, pre_gradient, halo, gain, weight, out, tall, start, done,
    *, frames, rows, width
):
    run_copies([(valid_from, start)], done)
    block = frames * width
    for row in range(-1, rows + 1):
        if row < 0:
            cells = halo[0]
        elif row == rows:
            cells = halo[1]
        else:
            cells = pre_gradient[row]
        cells = cells.reshape(block, 256)
        for tap in range(3):
            target = row - 1 + tap
            if 0 <= target < rows:
                tall[target * block : target * block + block, tap * 256 : tap * 256 + 256] = cells
    for row in range(rows):
        cells = tall[row * block : row * block + block]
        taps = [
            dot_nt(cells, jnp.concatenate([weight[0, j], weight[1, j], weight[2, j]], axis=1))
            for j in range(3)
        ]
        gradient = from_right(taps[0], width) + taps[1] + from_left(taps[2], width)
        gradient = gradient * gain[...]
        for frame in range(frames):
            keep = present(start, frame, frames)
            unit, inverse = normalised(video[frame, row], keep)
            tile = gradient[frame * width : frame * width + width]
            mean = jnp.mean(tile * unit, axis=-1, keepdims=True)
            out[frame, row] = (inverse * (tile - unit * mean) * keep).astype(BF16)


def encode_kernel(mix, stay, came, out, line, strided, *, width, shards):
    for step in range(shards):
        source = came if step >= shards // 2 else stay
        strided[lax.axis_index("tm") ^ step] = source[step % (shards // 2), 0]
    parts, here = strided.shape[1:3]
    outs = parts - 1
    plane = here * width
    total = shards * outs
    for frame in range(total):
        shard, part = (frame // outs, frame % outs)
        cells = strided[shard, part].reshape(plane, 256)
        if part == 0 and shard > 0:
            carried = strided[shard - 1, outs].reshape(plane, 256)
            cells = (cells.astype(F32) + carried.astype(F32)).astype(BF16)
        line[(frame + 2) * plane : (frame + 3) * plane] = cells
    line[0 : 2 * plane] = jnp.zeros((2 * plane, 256), BF16)
    span = total * plane
    result = line[2 * plane : 2 * plane + span].astype(F32)
    for k in range(3):
        result = result + dot(line[(2 - k) * plane : (2 - k) * plane + span], mix[k])
    out[...] = result.astype(BF16).reshape(out.shape)


def finish_kernel(home, away, weight, *refs, scale, last):
    if last:
        before, gain, _, _, _, spatial, temporal, mix, gain_out, staged, row, done = refs
        total = before[...]
    else:
        spatial, temporal, mix, after, staged, done = refs
        total = jnp.zeros((256, 128), F32)
    columns = core_columns()[1 if last else 0]
    parts = home.shape[0]
    low, high = (SPLIT * 128 // parts, (15 - SPLIT) * 128 // parts)
    mine = lax.axis_index("tm") % 2
    for half, source in ((mine, home), (1 - mine, away)):
        for part in range(parts):
            at = pl.multiple_of((2 * part + half) * low, low)
            staged[pl.ds(at, low)] = source[part, :low].astype(F32) * scale
            at = pl.multiple_of(SPLIT * 256 + (2 * part + half) * high, high)
            staged[pl.ds(at, high)] = source[part, low:].astype(F32) * scale
    results = [(mix, k) for k in range(3)] + [(temporal, k) for k in range(3)]
    results = results + [(spatial, k) for k in range(9)]
    copies = []
    for index, (result, k) in enumerate(results):
        cells = staged.at[pl.ds(index * 256, 256)]
        copies.append(pltpu.make_async_copy(cells, result.at[k, :, columns], done.at[index]))
        copies[-1].start()
    for k in range(9):
        cells = staged[1536 + k * 256 : 1792 + k * 256]
        total = total + cells * weight[k // 3, k % 3, :, columns].astype(F32)
    if last:
        upper = total.astype(BF16)
        lower = (total - upper.astype(F32)).astype(BF16)
        ones = jnp.ones((16, 128), BF16)
        row[...] = (dot_nt(ones, upper) + dot_nt(ones, lower))[:1] / gain[...]
        copies.append(pltpu.make_async_copy(row, gain_out, done.at[15]))
        copies[-1].start()
    else:
        after[...] = total
    for copy in copies:
        copy.wait()


def call(kernel, outs, scratch=(), flops=0, moved=0, aliases=None, far=0):
    where = pl.BlockSpec(memory_space=pltpu.VMEM)

    def run(*operands):
        results = pl.pallas_call(
            kernel,
            out_shape=[jax.ShapeDtypeStruct(shape, dtype) for shape, dtype in outs],
            in_specs=[
                pl.BlockSpec(memory_space=pltpu.HBM)
                if a.dtype == jnp.int32 or at in (aliases or ())
                else where
                for at, a in enumerate(operands)
            ],
            out_specs=[pl.BlockSpec(memory_space=pltpu.HBM)] * far + [where] * (len(outs) - far),
            input_output_aliases=aliases or {},
            scratch_shapes=list(scratch),
            compiler_params=pltpu.CompilerParams(vmem_limit_bytes=VMEM_LIMIT),
            cost_estimate=pl.CostEstimate(flops=flops, bytes_accessed=moved, transcendentals=0),
        )(*operands)
        return list(results)

    return run


def neighbours(inner, outer, axis):
    size = lax.axis_size(axis)
    links = [(i, i + 1) for i in range(1, size - 1, 2)]
    links = links + [(j, i) for i, j in links]
    return (pair(inner, axis, 1), lax.ppermute(outer, axis, links))


def pair(array, axis, step):
    return lax.ppermute(array, axis, [(i, i ^ step) for i in range(lax.axis_size(axis))])


def pairs(arrays, axis):
    return [pair(array, axis, step + 1) for step, array in enumerate(arrays)]


def together(*values):
    return lax.optimization_barrier(values)


def on_device(
    video_clip, valid_from, norm_gain, spatial_weight, temporal_weight, mix_weight, cotangent
):
    video = video_clip[0]
    frames, rows, width, channels = video.shape
    outs = frames // 2
    shards = lax.axis_size("tm")
    lines = lax.axis_size("height")
    here = rows // shards
    cells = frames * rows * width
    sizes = dict(frames=frames, rows=rows, width=width)
    gain = norm_gain.reshape(1, channels)
    edge = ((frames, width, channels), BF16)
    halo = pltpu.VMEM((2, frames, width, channels), BF16)

    scalar = [pltpu.SMEM((1,), jnp.int32), pltpu.SemaphoreType.DMA((1,))]
    pieces = call(
        functools.partial(pieces_kernel, outs=outs),
        [((outs + 3, here, width, channels), BF16)] * (shards - 1),
        [pltpu.SemaphoreType.DMA((shards - 1,))],
        moved=1024 * 1024,
    )(cotangent[0])
    *pieces, edges = together(*pieces, video)
    pieces = pairs(pieces, "tm")
    inner, outer = call(
        functools.partial(edges_kernel, rows=rows, frames_first=True),
        [edge, edge],
        [pltpu.SemaphoreType.DMA((2,))],
        moved=512 * 1024,
    )(edges)
    inner, outer = neighbours(inner, outer, "height")

    normed, partial = call(
        functools.partial(own_kernel, **sizes),
        [((cells, channels), BF16), ((cells, channels), F32)],
        scalar,
        flops=18 * cells * channels * channels,
        moved=4 * 1024 * 1024,
    )(valid_from, video, gain, spatial_weight)

    tall, slope, active, parts, stay, leave = call(
        functools.partial(front_kernel, **sizes, shards=shards),
        [
            ((cells + 2 * frames * width, channels), BF16),
            ((cells, channels), F32),
            ((2, cells // 2, channels), BF16),
            (((outs + 1) * rows * width, channels), BF16),
        ]
        + [((1, shards // 2, outs + 1, here, width, channels), BF16)] * 2,
        [halo, *scalar, pltpu.VMEM((shards, outs + 1, here, width, channels), BF16)],
    )(valid_from, normed, partial, inner, outer, gain, spatial_weight, temporal_weight)

    half = channels // 2
    pre_gradient, *low = call(
        functools.partial(middle_kernel, **sizes, shards=shards),
        [
            ((rows, frames, width, channels), BF16),
            ((SPLIT * channels, half), F32),
            ((SPLIT * channels, half), BF16),
        ],
        [pltpu.VMEM((outs + 3, shards, here * width, channels), BF16)],
        flops=20 * cells * channels * channels,
        moved=6 * 1024 * 1024,
    )(
        tall, slope, active, parts, temporal_weight, mix_weight, cotangent[0],
        *reversed(pieces),
    )

    high = call(
        functools.partial(spatial_kernel, **sizes),
        [((size * channels, half), dtype) for size in (15 - SPLIT,) for dtype in (F32, BF16)],
        flops=16 * cells * channels * channels,
        moved=6 * 1024 * 1024,
    )(tall, pre_gradient)

    def shapes(rows_in, *types):
        return [((rows_in, half), dtype) for dtype in types]

    def added(left, right):
        (total,) = call(add_kernel, shapes(left.shape[0], BF16))(left, right)
        return total

    def joined(pieces):
        (total,) = call(join_kernel, [((lines,) + pieces[0].shape, BF16)])(*pieces)
        return total

    def summed(pieces):
        (total,) = call(gather_sum_kernel, shapes(pieces[0].shape[0], BF16))(*pieces)
        return total

    (low, low_send), (high, high_send) = (low, high)
    low_got = pair(low_send, "cam", 1)
    high_got = pair(high_send, "cam", 1)
    size = 15 * channels // lines // 2
    dealt = call(deal_kernel, shapes(size, *([F32] + [BF16] * (lines - 1)) * 2))(
        *[a.reshape(lines, 2, -1, half) for a in (low, low_got, high, high_got)]
    )
    (away, *away_sends), (home, *home_sends) = (dealt[:lines], dealt[lines:])
    away_came = pairs(away_sends, "height")
    home_came = pairs(home_sends, "height")
    came = pair(leave, "tm", 1)
    away, came = together(away, came)
    crossed = pair(summed([away] + away_came[::-1]), "tm", 1)
    pre_gradient, home_came[-1] = together(pre_gradient, home_came[-1])
    total = summed([home] + home_came[::-1] + [crossed])
    inner, outer = call(
        functools.partial(edges_kernel, rows=rows, frames_first=False),
        [edge, edge],
        [pltpu.SemaphoreType.DMA((2,))],
        moved=512 * 1024,
    )(pre_gradient)
    inner, outer = neighbours(inner, outer, "height")
    (halo_rows,) = call(halo_kernel, [((2, frames, width, channels), BF16)])(inner, outer)
    for step in range(1, shards.bit_length() - 1):
        if step > 1:
            total = added(total, other)
        other = pair(total, "tm", 1 << step)
    (video_gradient,) = call(
        functools.partial(input_kernel, **sizes),
        [((frames, rows, width, channels), BF16)],
        [pltpu.VMEM((cells, 3 * channels), BF16)] + scalar,
        flops=18 * cells * channels * channels,
        moved=4 * 1024 * 1024,
    )(valid_from, video, pre_gradient, halo_rows, gain, spatial_weight)
    other, video_gradient = together(other, video_gradient)
    total = added(total, other)
    other = pair(total, "tm", 1)
    for step in range(1, shards.bit_length() - 1):
        count, pieces = (2 * stay.shape[0], stay.shape[1] // 2)
        stay, leave = call(split_kernel, [((count, pieces) + stay.shape[2:], BF16)] * 2)(stay, came)
        came = pair(leave, "tm", 1 << step)
    home_pieces = [total] + pairs([total] * (lines - 1), "height")
    away_pieces = [other] + pairs([other] * (lines - 1), "height")
    home = joined(home_pieces)
    home, came = together(home, came)
    (encoded,) = call(
        functools.partial(encode_kernel, width=width, shards=shards),
        [((shards * outs, here, width, channels), BF16)],
        [
            pltpu.VMEM(((shards * outs + 2) * here * width, channels), BF16),
            pltpu.VMEM((shards, outs + 1, here, width, channels), BF16),
        ],
        flops=3 * cells * channels * channels,
        moved=2 * 1024 * 1024,
    )(mix_weight, stay, came)
    away_pieces[-1], home, video_gradient, encoded = together(
        away_pieces[-1], home, video_gradient, encoded
    )
    away = joined(away_pieces)
    own = (home, away)
    others = (pair(home, "cam", 1), pair(away, "cam", 1))

    cell_count = cells * lax.axis_size("cam") * shards * lines
    scale = 1.0 / math.sqrt(cell_count)
    results = [((9, channels, channels), F32)] + [((3, channels, channels), F32)] * 2
    staged = pltpu.VMEM((15 * channels, half), F32)
    *results_own, total = call(
        functools.partial(finish_kernel, scale=scale, last=False),
        results + [((channels, half), F32)],
        [staged, pltpu.SemaphoreType.DMA((15,))],
        moved=4 * 1024 * 1024,
        far=3,
    )(*own, spatial_weight)
    spatial, temporal, mix, gain_gradient = call(
        functools.partial(finish_kernel, scale=scale, last=True),
        results + [((1, channels), F32)],
        [staged, pltpu.VMEM((1, channels), F32), pltpu.SemaphoreType.DMA((16,))],
        moved=4 * 1024 * 1024,
        far=4,
        aliases={5 + at: at for at in range(3)},
    )(*others, spatial_weight, total, gain, *results_own)

    return (
        encoded[None],
        video_gradient[None],
        spatial.reshape(spatial_weight.shape),
        temporal,
        mix,
        gain_gradient.reshape(channels),
    )


def solution(mesh):
    return jax.shard_map(
        on_device,
        mesh=mesh,
        in_specs=(
            P("cam", "tm", "height", None, None),
            P("cam"),
            P(),
            P(),
            P(),
            P(),
            P("cam", None, ("height", "tm"), None, None),
        ),
        out_specs=(
            P("cam", None, ("height", "tm"), None, None),
            P("cam", "tm", "height", None, None),
            P(),
            P(),
            P(),
            P(),
        ),
        check_vma=False,
    )
```
